32 devices in a mesh: shard: 4 (over x, core), ctx: 2 (over y), tensor: 4 (over z).
Axes of the slice: x: 2, y: 2, z: 4, core: 2. Of those that a mesh axis runs over, the one named last changes fastest.
Arguments:
- image_rows: bfloat16 [4, 2048, 1536], P('shard', 'ctx'), may hold values from -6 to 6
- text_input_rows: bfloat16 [4, 154, 1536], P('shard', 'ctx'), may hold values from -6 to 6
- condition: float32 [2, 1536], replicated, may hold values from -6 to 6
- slot_table: int32 [4], P('shard'), may hold values from -1 to 1, as said below
- weights: float32 [2, 1536, 18, 1536], P(None, ('shard', 'ctx'), None, 'tensor'), may hold values from -4 to 4
- weight_mom_one: float32 [2, 1536, 18, 1536], P(None, ('shard', 'ctx'), None, 'tensor'), may hold values from -0.00030517578 to 0.00030517578
- weight_mom_two: float32 [2, 1536, 18, 1536], P(None, ('shard', 'ctx'), None, 'tensor'), may hold values from 5.3e-10 to 2.1e-09
- biases: float32 [2, 14, 1536], replicated, may hold values from -1.5 to 1.5
- bias_mom_one: float32 [2, 14, 1536], replicated, may hold values from -0.00030517578 to 0.00030517578
- bias_mom_two: float32 [2, 14, 1536], replicated, may hold values from 5.3e-10 to 2.1e-09
- image_output_cotangent: bfloat16 [4, 2048, 1536], P('shard', 'ctx'), may hold values from -6 to 6
- text_output_cotangent: bfloat16 [4, 154, 1536], P('shard', 'ctx'), may hold values from -6 to 6
Outputs:
- image_out: bfloat16 [4, 2048, 1536], P('shard', 'ctx')
- text_out: bfloat16 [4, 154, 1536], P('shard', 'ctx')
- image_grad: bfloat16 [4, 2048, 1536], P('shard', 'ctx')
- text_grad: bfloat16 [4, 154, 1536], P('shard', 'ctx')
- condition_grad: float32 [2, 1536], replicated
- weight_grad: float32 [2, 1536, 18, 1536], P(None, ('shard', 'ctx'), None, 'tensor')
- weight_new: float32 [2, 1536, 18, 1536], P(None, ('shard', 'ctx'), None, 'tensor')
- weight_mom_one_new: float32 [2, 1536, 18, 1536], P(None, ('shard', 'ctx'), None, 'tensor')
- weight_mom_two_new: float32 [2, 1536, 18, 1536], P(None, ('shard', 'ctx'), None, 'tensor')
- bias_grad: float32 [2, 14, 1536], replicated
- bias_new: float32 [2, 14, 1536], replicated
- bias_mom_one_new: float32 [2, 14, 1536], replicated
- bias_mom_two_new: float32 [2, 14, 1536], replicated
The draws below stay inside these ranges and needn't reach their ends.
Inputs may be any that keep to these rules, and one draw needn't show every extreme that they name: `slot_table`: each of the 2 sequences stands in exactly one slot, the other slots hold -1. Slot n belongs to shard group n; slots 0 and 2 are always filled.
All inputs are finite; a program needn't handle non-finite values.
Results may differ from the reference program's by a relative error of at most 0.024.
Values may be sent and summed in bfloat16 or wider, within the bound.
No kernel may reach another device: no remote copies, remote signals or barrier semaphores. Data moves between devices by JAX's collectives and lax.ppermute only.
A program may use at most 640 MiB of HBM per device.

```python
import math
import jax
import jax.numpy as jnp
from jax import lax

MODEL_WIDTH = 1536
H = 24
DH = 64
F = 6144
IMAGE_TOKENS = 2048
TEXT_TOKENS = 154
GROUP_SLOTS = 1
TOTAL_SLOTS = 4
NSEQ = 2
SEQLEN = 2202
N_SHARD = 4


def draw_slot_table(key, part):
    ordering_key = jax.random.fold_in(key, 12)
    ident_key = jax.random.fold_in(key, 13)
    slot_position_index = jnp.arange(TOTAL_SLOTS, dtype=jnp.int32)
    group_index = slot_position_index // GROUP_SLOTS
    in_full = (group_index == 0) | (group_index == N_SHARD // 2)
    ranking_value = jax.random.permutation(ordering_key, TOTAL_SLOTS).astype(jnp.int32)
    ranking_value = jnp.where(in_full, -1 - slot_position_index, ranking_value)
    order = jnp.argsort(ranking_value, stable=True)
    seq_ids = jax.random.permutation(ident_key, NSEQ).astype(jnp.int32)
    assignment_table = jnp.full((TOTAL_SLOTS,), -1, dtype=jnp.int32)
    return assignment_table.at[order[:NSEQ]].set(seq_ids)


def draw_image_rows(key, part):
    root_random_key = jax.random.fold_in(key, 21)
    drawn_values = jax.random.normal(root_random_key, (TOTAL_SLOTS, IMAGE_TOKENS, MODEL_WIDTH), jnp.float32)
    return jnp.clip(drawn_values, -6.0, 6.0).astype(jnp.bfloat16)


def draw_weights(key, part):
    noise_key = jax.random.fold_in(key, 31)
    base = jax.random.normal(noise_key, (2, MODEL_WIDTH, 18, MODEL_WIDTH), jnp.float32)
    segment = jnp.arange(18)
    seg_scale = jnp.where(segment == 9, 16.0, 1.0) * jnp.where(segment >= 14, (MODEL_WIDTH / F) ** 0.5, 1.0) / MODEL_WIDTH ** 0.5
    drawn_values = base * seg_scale[None, None, :, None]
    return jnp.clip(drawn_values, -4.0, 4.0)


def shard_levels(stream_key, dims, split, least, largest):
    loudness = 1.0
    for position, blocks in split:
        steps = jax.random.uniform(jax.random.fold_in(jax.random.fold_in(stream_key, 6), position), (blocks,), jnp.float32, least / len(split), largest / len(split))
        loudness = loudness * jnp.repeat(jnp.exp(steps), dims[position] // blocks).reshape((-1,) + (1,) * (len(dims) - 1 - position))
    return loudness


def noise(key, dims, scale, limit, split=(), kind=jnp.bfloat16):
    factor_of = shard_levels(key, dims, split, -0.22, 0.18) if split else 1.0
    array = jax.random.normal(key, dims, jnp.float32) * scale * factor_of
    return jnp.minimum(jnp.maximum(array, -limit), limit).astype(kind)


def setup_inputs(seed: int = 0) -> dict:
    key_of = jax.random.split(jax.random.key(seed), 13)
    image_rows = draw_image_rows(jax.random.fold_in(key_of[12], 71), 0)
    text_input_rows = noise(key_of[1], (TOTAL_SLOTS, TEXT_TOKENS, MODEL_WIDTH), 1.0, 6.0, ((0, 4), (1, 2)))
    condition = noise(key_of[2], (NSEQ, MODEL_WIDTH), 1.0, 6.0, (), jnp.float32)
    slot_table = draw_slot_table(jax.random.fold_in(key_of[12], 71), 0)
    weights = draw_weights(jax.random.fold_in(key_of[12], 71), 0)
    weight_mom_one = noise(key_of[5], (2, MODEL_WIDTH, 18, MODEL_WIDTH), (2e-5), 0.00030517578, ((1, 8), (3, 4)), jnp.float32)
    weight_mom_two = jnp.clip(jnp.exp(math.log(2.099999951710174e-09) - 1.3768156 * jax.random.uniform(key_of[6], (2, MODEL_WIDTH, 18, MODEL_WIDTH), jnp.float32) ** shard_levels(key_of[6], (2, MODEL_WIDTH, 18, MODEL_WIDTH), ((1, 8), (3, 4)), -0.2, 0.2)), 5.299999883412454e-10, 2.099999951710174e-09)
    biases = noise(key_of[7], (2, 14, MODEL_WIDTH), 0.1, 1.5, (), jnp.float32)
    bias_mom_one = noise(key_of[8], (2, 14, MODEL_WIDTH), (2e-5), 0.00030517578, (), jnp.float32)
    bias_mom_two = jnp.clip(jnp.exp(jax.random.uniform(key_of[9], (2, 14, MODEL_WIDTH), jnp.float32, math.log(5.299999883412454e-10), math.log(2.099999951710174e-09))), 5.299999883412454e-10, 2.099999951710174e-09)
    image_output_cotangent = noise(key_of[10], (TOTAL_SLOTS, IMAGE_TOKENS, MODEL_WIDTH), 1.0, 6.0, ((0, 4), (1, 2)))
    text_output_cotangent = noise(key_of[11], (TOTAL_SLOTS, TEXT_TOKENS, MODEL_WIDTH), 1.0, 6.0, ((0, 4), (1, 2)))
    return dict(image_rows=image_rows, text_input_rows=text_input_rows, condition=condition, slot_table=slot_table, weights=weights, weight_mom_one=weight_mom_one, weight_mom_two=weight_mom_two, biases=biases, bias_mom_one=bias_mom_one, bias_mom_two=bias_mom_two, image_output_cotangent=image_output_cotangent, text_output_cotangent=text_output_cotangent)


beta_one = 0.9
beta_two = 0.95
learn_rate = 0.1
decay_rate = 0.1
adam_eps = 1e-08
adam_step = 10.0
norm_eps = 1e-06
gelu_coef = 0.044715
root_two_pi = 0.7978845608028654
clip_unit = 0.0001
clip_eps = 1e-12

def widen(drawn_values):
    return lax.optimization_barrier(drawn_values).astype(jnp.float32)

def matmul_bf(left, right):
    return jnp.dot(left, right, preferred_element_type=jnp.float32)

def layer_norm(drawn_values):
    center = drawn_values - lax.optimization_barrier(jnp.mean(drawn_values, axis=-1, keepdims=True))
    inverse = lax.rsqrt(lax.optimization_barrier(jnp.mean(center * center, axis=-1, keepdims=True)) + norm_eps)
    return (center * inverse, inverse)

def norm_back(normed, inverse, upstream):
    mean_grad = lax.optimization_barrier(jnp.mean(upstream, axis=-1, keepdims=True))
    mean_dot = lax.optimization_barrier(jnp.mean(upstream * normed, axis=-1, keepdims=True))
    return inverse * (upstream - mean_grad - normed * mean_dot)

def gelu_parts(preact):
    inner = root_two_pi * (preact + gelu_coef * preact * preact * preact)
    tanh_value = jnp.tanh(inner)
    value_out = 0.5 * preact * (1.0 + tanh_value)
    slope_out = 0.5 * (1.0 + tanh_value) + 0.5 * preact * (1.0 - tanh_value * tanh_value) * root_two_pi * (1.0 + 3.0 * gelu_coef * preact * preact)
    return (value_out, slope_out)

def silu_slope(drawn_values):
    sigmoid_val = jax.nn.sigmoid(drawn_values)
    return sigmoid_val * (1.0 + drawn_values * (1.0 - sigmoid_val))

def adam_update(parameter, moment_one, moment_two, gradient, decay_factor):
    new_one = beta_one * moment_one + (1.0 - beta_one) * gradient
    new_two = beta_two * moment_two + (1.0 - beta_two) * gradient * gradient
    first_hat = new_one / (1.0 - beta_one ** adam_step)
    second_hat = new_two / (1.0 - beta_two ** adam_step)
    new_param = parameter - learn_rate * (first_hat / (jnp.sqrt(second_hat) + adam_eps) + decay_factor * parameter)
    return (new_param, new_one, new_two)

def sequence_pass(rows_image, rows_text, cot_image, cot_text, cond_vec, weight_bf, biases):
    highest = lax.Precision.HIGHEST
    score_scale = DH ** (-0.5)
    silu_bf = jax.nn.silu(cond_vec).astype(jnp.bfloat16)
    silu_wide = widen(silu_bf)
    inputs_all = (rows_image, rows_text)
    cots_all = (cot_image, cot_text)
    mod_list, normed_one, inverse_one, hidden_one = ([], [], [], [])
    query_list, key_list, value_list = ([], [], [])
    for stream in range(2):
        weight_slab = weight_bf[stream]
        stream_mod = jnp.einsum('i,ije->je', silu_wide, weight_slab[:, 0:6, :].astype(jnp.float32), precision=highest) + biases[stream, 0:6]
        normed, inverse = layer_norm(inputs_all[stream].astype(jnp.float32))
        hidden = (normed * (1.0 + stream_mod[1]) + stream_mod[0]).astype(jnp.bfloat16)
        query_list.append((matmul_bf(hidden, weight_slab[:, 6, :]) + biases[stream, 6]).astype(jnp.bfloat16))
        key_list.append(matmul_bf(hidden, weight_slab[:, 7, :]).astype(jnp.bfloat16))
        value_list.append((matmul_bf(hidden, weight_slab[:, 8, :]) + biases[stream, 7]).astype(jnp.bfloat16))
        mod_list.append(stream_mod)
        normed_one.append(normed)
        inverse_one.append(inverse)
        hidden_one.append(hidden)
    query_wide = widen(jnp.concatenate(query_list, axis=0)).reshape(SEQLEN, H, DH)
    key_wide = widen(jnp.concatenate(key_list, axis=0)).reshape(SEQLEN, H, DH)
    value_wide = widen(jnp.concatenate(value_list, axis=0)).reshape(SEQLEN, H, DH)
    scores = jnp.einsum('qhd,khd->hqk', query_wide, key_wide, precision=highest) * score_scale
    row_max = lax.optimization_barrier(jnp.max(scores, axis=2))
    shifted = jnp.exp(scores - row_max[:, :, None])
    row_total = lax.optimization_barrier(jnp.sum(shifted, axis=2))
    summed = jnp.einsum('hqk,khd->qhd', widen(shifted.astype(jnp.bfloat16)), value_wide, precision=highest)
    attended = (summed / jnp.transpose(row_total)[:, :, None]).reshape(SEQLEN, H * DH).astype(jnp.bfloat16)
    log_sum = row_max + jnp.log(row_total)
    attn_split = (attended[:IMAGE_TOKENS], attended[IMAGE_TOKENS:])
    outputs_list = []
    grad_attn_list = []
    stored = []
    for stream in range(2):
        weight_slab = weight_bf[stream]
        stream_mod = mod_list[stream]
        attn_proj = jnp.dot(attn_split[stream], weight_slab[:, 9, :].T, preferred_element_type=jnp.float32) + biases[stream, 8]
        residual = inputs_all[stream].astype(jnp.float32) + stream_mod[2] * attn_proj
        normed, inverse = layer_norm(residual)
        hidden = (normed * (1.0 + stream_mod[4]) + stream_mod[3]).astype(jnp.bfloat16)
        up_weight = weight_slab[:, 10:14, :].reshape(MODEL_WIDTH, F)
        down_weight = weight_slab[:, 14:18, :].reshape(MODEL_WIDTH, F)
        preact = matmul_bf(hidden, up_weight) + biases[stream, 9:13].reshape(F)
        gelu_value, gelu_slope = gelu_parts(preact)
        gelu_bf = gelu_value.astype(jnp.bfloat16)
        mlp_proj = jnp.dot(gelu_bf, down_weight.T, preferred_element_type=jnp.float32) + biases[stream, 13]
        outputs_list.append((residual + stream_mod[5] * mlp_proj).astype(jnp.bfloat16))
        cotangent = cots_all[stream].astype(jnp.float32)
        grad_gate_m = lax.optimization_barrier(jnp.sum(cotangent * mlp_proj, axis=0))
        grad_y = cotangent * stream_mod[5]
        grad_y_bf = grad_y.astype(jnp.bfloat16)
        grad_down = matmul_bf(grad_y_bf.T, gelu_bf)
        grad_pre = matmul_bf(grad_y_bf, down_weight) * gelu_slope
        grad_pre_bf = grad_pre.astype(jnp.bfloat16)
        grad_up = matmul_bf(hidden.T, grad_pre_bf)
        back_two = jnp.dot(grad_pre_bf, up_weight.T, preferred_element_type=jnp.float32)
        grad_shift_m = lax.optimization_barrier(jnp.sum(back_two, axis=0))
        grad_scale_m = lax.optimization_barrier(jnp.sum(back_two * normed, axis=0))
        grad_resid = cotangent + norm_back(normed, inverse, back_two * (1.0 + stream_mod[4]))
        grad_gate_a = lax.optimization_barrier(jnp.sum(grad_resid * attn_proj, axis=0))
        grad_branch = grad_resid * stream_mod[2]
        grad_branch_bf = grad_branch.astype(jnp.bfloat16)
        grad_out_w = matmul_bf(grad_branch_bf.T, attn_split[stream])
        grad_attn_list.append(matmul_bf(grad_branch_bf, weight_slab[:, 9, :]).astype(jnp.bfloat16))
        bias_out = lax.optimization_barrier(jnp.sum(grad_branch, axis=0))
        bias_up = lax.optimization_barrier(jnp.sum(grad_pre, axis=0)).reshape(4, MODEL_WIDTH)
        bias_down = lax.optimization_barrier(jnp.sum(grad_y, axis=0))
        stored.append((grad_resid, grad_gate_a, grad_shift_m, grad_scale_m, grad_gate_m, grad_out_w, grad_up, grad_down, bias_out, bias_up, bias_down))
    grad_wide = widen(jnp.concatenate(grad_attn_list, axis=0)).reshape(SEQLEN, H, DH)
    attn_wide = widen(attended).reshape(SEQLEN, H, DH)
    row_delta = jnp.transpose(lax.optimization_barrier(jnp.sum(grad_wide * attn_wide, axis=2)))
    soft = jnp.exp(scores - log_sum[:, :, None])
    grad_value = jnp.einsum('hqk,qhd->khd', widen(soft.astype(jnp.bfloat16)), grad_wide, precision=highest).reshape(SEQLEN, MODEL_WIDTH)
    grad_soft = jnp.einsum('qhd,khd->hqk', grad_wide, value_wide, precision=highest)
    grad_score = widen((soft * (grad_soft - row_delta[:, :, None]) * score_scale).astype(jnp.bfloat16))
    grad_query = jnp.einsum('hqk,khd->qhd', grad_score, key_wide, precision=highest).reshape(SEQLEN, MODEL_WIDTH)
    grad_key = jnp.einsum('hqk,qhd->khd', grad_score, query_wide, precision=highest).reshape(SEQLEN, MODEL_WIDTH)
    grad_rows = []
    weight_parts = []
    bias_parts = []
    cond_back = jnp.zeros((MODEL_WIDTH,), jnp.float32)
    for stream in range(2):
        weight_slab = weight_bf[stream]
        stream_mod = mod_list[stream]
        grad_resid, grad_gate_a, grad_shift_m, grad_scale_m, grad_gate_m, grad_out_w, grad_up, grad_down, bias_out, bias_up, bias_down = stored[stream]
        row_range = slice(0, IMAGE_TOKENS) if stream == 0 else slice(IMAGE_TOKENS, SEQLEN)
        grad_q_part = grad_query[row_range]
        grad_k_part = grad_key[row_range]
        grad_v_part = grad_value[row_range]
        bias_query = lax.optimization_barrier(jnp.sum(grad_q_part, axis=0))
        bias_value = lax.optimization_barrier(jnp.sum(grad_v_part, axis=0))
        grad_q_bf = grad_q_part.astype(jnp.bfloat16)
        grad_k_bf = grad_k_part.astype(jnp.bfloat16)
        grad_v_bf = grad_v_part.astype(jnp.bfloat16)
        hidden = hidden_one[stream]
        grad_qkv = jnp.stack([matmul_bf(hidden.T, grad_q_bf), matmul_bf(hidden.T, grad_k_bf), matmul_bf(hidden.T, grad_v_bf)], axis=1)
        back_one = matmul_bf(grad_q_bf, weight_slab[:, 6, :].T) + matmul_bf(grad_k_bf, weight_slab[:, 7, :].T) + matmul_bf(grad_v_bf, weight_slab[:, 8, :].T)
        grad_shift_a = lax.optimization_barrier(jnp.sum(back_one, axis=0))
        grad_scale_a = lax.optimization_barrier(jnp.sum(back_one * normed_one[stream], axis=0))
        grad_input = grad_resid + norm_back(normed_one[stream], inverse_one[stream], back_one * (1.0 + stream_mod[1]))
        grad_rows.append(grad_input.astype(jnp.bfloat16))
        grad_mod = jnp.stack([grad_shift_a, grad_scale_a, grad_gate_a, grad_shift_m, grad_scale_m, grad_gate_m])
        mod_weight_grad = silu_wide[:, None, None] * grad_mod[None]
        cond_back = cond_back + jnp.einsum('je,ije->i', grad_mod, weight_slab[:, 0:6, :].astype(jnp.float32), precision=highest)
        weight_parts.append(jnp.concatenate([mod_weight_grad, grad_qkv, grad_out_w[:, None, :], grad_up.reshape(MODEL_WIDTH, 4, MODEL_WIDTH), grad_down.reshape(MODEL_WIDTH, 4, MODEL_WIDTH)], axis=1))
        bias_parts.append(jnp.concatenate([grad_mod, bias_query[None], bias_value[None], bias_out[None], bias_up, bias_down[None]], axis=0))
    cond_grad = cond_back * silu_slope(cond_vec)
    return (outputs_list[0], outputs_list[1], grad_rows[0], grad_rows[1], cond_grad, jnp.stack(weight_parts), jnp.stack(bias_parts))

def reference(image_rows, text_input_rows, condition, slot_table, weights, weight_mom_one, weight_mom_two, biases, bias_mom_one, bias_mom_two, image_output_cotangent, text_output_cotangent):
    weight_bf = weights.astype(jnp.bfloat16)
    slot_numbers = jnp.arange(TOTAL_SLOTS, dtype=jnp.int32)
    matches = slot_table[None, :] == jnp.arange(NSEQ, dtype=jnp.int32)[:, None]
    slot_of = lax.optimization_barrier(jnp.sum(jnp.where(matches, slot_numbers[None, :], 0), axis=1)).astype(jnp.int32)

    def one_sequence(carry, seq_index):
        weight_acc, bias_acc = carry
        slot_position_index = slot_of[seq_index].astype(jnp.int32)
        rows_image = lax.dynamic_index_in_dim(image_rows, slot_position_index, 0, keepdims=False)
        rows_text = lax.dynamic_index_in_dim(text_input_rows, slot_position_index, 0, keepdims=False)
        cot_image = lax.dynamic_index_in_dim(image_output_cotangent, slot_position_index, 0, keepdims=False)
        cot_text = lax.dynamic_index_in_dim(text_output_cotangent, slot_position_index, 0, keepdims=False)
        cond_vec = lax.dynamic_index_in_dim(condition, seq_index, 0, keepdims=False)
        out_image, out_text, grad_image, grad_text, cond_grad, weight_part, bias_part = sequence_pass(rows_image, rows_text, cot_image, cot_text, cond_vec, weight_bf, biases)
        return ((weight_acc + weight_part, bias_acc + bias_part), (out_image, out_text, grad_image, grad_text, cond_grad))
    start_carry = (jnp.zeros(weights.shape, jnp.float32), jnp.zeros(biases.shape, jnp.float32))
    (weight_grad, bias_grad), results = lax.scan(one_sequence, start_carry, jnp.arange(NSEQ, dtype=jnp.int32))
    image_out = jnp.zeros(image_rows.shape, jnp.bfloat16).at[slot_of].set(results[0])
    text_out = jnp.zeros(text_input_rows.shape, jnp.bfloat16).at[slot_of].set(results[1])
    image_grad = jnp.zeros(image_rows.shape, jnp.bfloat16).at[slot_of].set(results[2])
    text_grad = jnp.zeros(text_input_rows.shape, jnp.bfloat16).at[slot_of].set(results[3])
    condition_grad = results[4]
    segment_squares = lax.optimization_barrier(jnp.sum(weight_grad * weight_grad, axis=(1, 3)))
    weight_factor = jnp.minimum(1.0, clip_unit * MODEL_WIDTH / jnp.sqrt(segment_squares + clip_eps))
    weight_clipped = weight_grad * weight_factor[:, None, :, None]
    bias_squares = lax.optimization_barrier(jnp.sum(bias_grad * bias_grad, axis=2))
    bias_factor = jnp.minimum(1.0, clip_unit * MODEL_WIDTH ** 0.5 / jnp.sqrt(bias_squares + clip_eps))
    bias_clipped = bias_grad * bias_factor[:, :, None]
    weight_new, weight_one_new, weight_two_new = adam_update(weights, weight_mom_one, weight_mom_two, weight_clipped, decay_rate)
    bias_new, bias_one_new, bias_two_new = adam_update(biases, bias_mom_one, bias_mom_two, bias_clipped, 0.0)
    return (image_out, text_out, image_grad, text_grad, condition_grad, weight_grad, weight_new, weight_one_new, weight_two_new, bias_grad, bias_new, bias_one_new, bias_two_new)
```

```python
import functools
import jax
import jax.numpy as jnp
from jax import lax
from jax.experimental import pallas as pl
from jax.experimental.pallas import tpu as pltpu
from jax.experimental.layout import Layout, with_layout_constraint
from jax.sharding import PartitionSpec as P

DH=64
NT=(((1,),(1,)),((),()))
TN=(((0,),(0,)),((),()))
NN=(((1,),(0,)),((),()))
bf=jnp.bfloat16; f32=jnp.float32


beta_one = 0.9
beta_two = 0.95
learn_rate = 0.1
decay_rate = 0.1
adam_eps = 1e-08
adam_step = 10.0
norm_eps = 1e-06
gelu_coef = 0.044715
root_two_pi = 0.7978845608028654
clip_unit = 0.0001
clip_eps = 1e-12


def layer_norm(drawn_values):
    center = drawn_values - jnp.mean(drawn_values, axis=-1, keepdims=True)
    inverse = lax.rsqrt(jnp.mean(center * center, axis=-1, keepdims=True) + norm_eps)
    return (center * inverse, inverse)


def norm_back(normed, inverse, upstream):
    mean_grad = jnp.mean(upstream, axis=-1, keepdims=True)
    mean_dot = jnp.mean(upstream * normed, axis=-1, keepdims=True)
    return inverse * (upstream - mean_grad - normed * mean_dot)


def gelu_parts(preact):
    inner = root_two_pi * (preact + gelu_coef * preact * preact * preact)
    tanh_value = jnp.tanh(inner)
    value_out = 0.5 * preact * (1.0 + tanh_value)
    slope_out = 0.5 * (1.0 + tanh_value) + 0.5 * preact * (
        1.0 - tanh_value * tanh_value
    ) * root_two_pi * (1.0 + 3.0 * gelu_coef * preact * preact)
    return (value_out, slope_out)


def silu_slope(drawn_values):
    sigmoid_val = jax.nn.sigmoid(drawn_values)
    return sigmoid_val * (1.0 + drawn_values * (1.0 - sigmoid_val))


def adam_update(parameter, moment_one, moment_two, gradient, decay_factor):
    new_one = beta_one * moment_one + (1.0 - beta_one) * gradient
    new_two = beta_two * moment_two + (1.0 - beta_two) * gradient * gradient
    first_hat = new_one / (1.0 - beta_one**adam_step)
    second_hat = new_two / (1.0 - beta_two**adam_step)
    new_param = parameter - learn_rate * (
        first_hat / (jnp.sqrt(second_hat) + adam_eps) + decay_factor * parameter
    )
    return (new_param, new_one, new_two)


def dotf(a,b,dims,precision=None):
    return lax.dot_general(a,b,dims,preferred_element_type=f32,precision=precision)

def attn_fwd_kernel(heads, img, live, q_ref, kv_ref, a_ref, lse_ref):
    T=kv_ref.shape[2]
    bq=q_ref.shape[1]
    lane=lax.broadcasted_iota(jnp.int32,(1,256),1)
    lane1=lax.broadcasted_iota(jnp.int32,(1,128),1)
    keep=lax.broadcasted_iota(jnp.int32,(1,T-img),1) < live-img
    q=q_ref[0]
    acc=jnp.zeros((bq,256),f32)
    lse_tile=jnp.zeros((bq,128),f32)
    for h in range(heads):
        qm=jnp.where((lane>>6)==h,q,jnp.zeros_like(q))
        parts=[]
        for b in range(2):
            parts.append((dotf(qm,kv_ref[0,b,:img,:256],NT), b, 0, img))
            s=dotf(qm,kv_ref[0,b,img:,:256],NT)
            parts.append((jnp.where(keep,s,-1e30), b, img, T))
        m=functools.reduce(jnp.maximum,[jnp.max(p[0],axis=1,keepdims=True) for p in parts])
        l=jnp.zeros((bq,1),f32)
        pv=jnp.zeros((bq,256),f32)
        for s,b,lo,hi in parts:
            e=jnp.exp(s-m)
            l=l+jnp.sum(e,axis=1,keepdims=True)
            pv=pv+dotf(e.astype(bf),kv_ref[0,b,lo:hi,128:384],NN)
        acc=jnp.where((lane>>6)==h+1,pv/l,acc)
        lse_tile=jnp.where(lane1==h,m+jnp.log(l),lse_tile)
    a_ref[0]=acc[:,64:256].astype(bf)
    lse_ref[0]=lse_tile.T[:8]

def attn_fwd(q,kv,img,live,bq=384,heads=3):
    S,T,_=q.shape
    return pl.pallas_call(
        functools.partial(attn_fwd_kernel,heads,img,live),
        grid=(S,T//bq),
        in_specs=[pl.BlockSpec((1,bq,256),lambda s,i:(s,i,0)),
                  pl.BlockSpec((1,2,T,384),lambda s,i:(s,0,0,0))],
        out_specs=[pl.BlockSpec((1,bq,192),lambda s,i:(s,i,0)),
                   pl.BlockSpec((1,8,bq),lambda s,i:(s,0,i))],
        out_shape=[jax.ShapeDtypeStruct((S,T,192),bf),jax.ShapeDtypeStruct((S,8,T),f32)],
        compiler_params=pltpu.CompilerParams(vmem_limit_bytes=56*2**20),
        cost_estimate=pl.CostEstimate(flops=16*S*T*T*256,bytes_accessed=4*S*T*384,transcendentals=S*T*T*6),
        name="attn_fwd",
    )(q,kv)

def attn_bwd_kernel(heads, q_ref, kv_ref, a_ref, da_ref, lse_ref, dq_ref, dkv_ref, daw, delta, dqa):
    kb=pl.program_id(1)
    T=q_ref.shape[1]
    bk=kv_ref.shape[1]
    lane=lax.broadcasted_iota(jnp.int32,(1,256),1)
    @pl.when(kb==0)
    def _():
        da=da_ref[0]
        daw[...]=jnp.concatenate([jnp.zeros((T,64),bf),da],axis=1)
        prod=da.astype(f32)*a_ref[0].astype(f32)
        hm=((lax.broadcasted_iota(jnp.int32,(8,192),1)>>6)==lax.broadcasted_iota(jnp.int32,(8,192),0)).astype(f32)
        delta[...]=dotf(hm,prod,NT,lax.Precision.HIGHEST)
        dqa[...]=jnp.zeros_like(dqa)
    kw=kv_ref[0,:,:256]
    vw=kv_ref[0,:,128:384]
    dk=jnp.zeros((bk,256),f32)
    dv=jnp.zeros((bk,256),f32)
    dq=jnp.zeros((T,256),f32)
    for h in range(heads):
        sel=(lane>>6)==h
        qm=jnp.where(sel,q_ref[0],jnp.zeros((),bf))
        dam=jnp.where((lane>>6)==h+1,daw[...],jnp.zeros((),bf))
        st=dotf(kw,qm,NT)
        p=jnp.exp(st-lse_ref[0,h:h+1,:])
        dv=dv+dotf(p.astype(bf),dam,NN)
        dpt=dotf(vw,dam,NT)
        ds=(p*(dpt-delta[h:h+1,:])).astype(bf)
        dk=dk+dotf(ds,qm,NN)
        km=jnp.where(sel,kw,jnp.zeros((),bf))
        dq=dq+dotf(ds,km,TN)
    dqa[...]+=dq
    dkv_ref[0]=jnp.concatenate([dk[:,:192],dv[:,64:256]],axis=1).astype(bf)
    @pl.when(kb==pl.num_programs(1)-1)
    def _():
        dq_ref[0]=(dqa[...][:,:192]*0.125).astype(bf)

def attn_bwd(q,kv,a,da,lse,bk=384,heads=3):
    S,T,_=q.shape
    kv=kv.reshape(S,2*T,384)
    dq,dkv=pl.pallas_call(
        functools.partial(attn_bwd_kernel,heads),
        grid=(S,2*T//bk),
        in_specs=[pl.BlockSpec((1,T,256),lambda s,i:(s,0,0)),
                  pl.BlockSpec((1,bk,384),lambda s,i:(s,i,0)),
                  pl.BlockSpec((1,T,192),lambda s,i:(s,0,0)),
                  pl.BlockSpec((1,T,192),lambda s,i:(s,0,0)),
                  pl.BlockSpec((1,8,T),lambda s,i:(s,0,0))],
        out_specs=[pl.BlockSpec((1,T,192),lambda s,i:(s,0,0)),
                   pl.BlockSpec((1,bk,384),lambda s,i:(s,i,0))],
        out_shape=[jax.ShapeDtypeStruct((S,T,192),bf),jax.ShapeDtypeStruct((S,2*T,384),bf)],
        scratch_shapes=[pltpu.VMEM((T,256),bf),pltpu.VMEM((8,T),f32),pltpu.VMEM((T,256),f32)],
        compiler_params=pltpu.CompilerParams(vmem_limit_bytes=56*2**20),
        cost_estimate=pl.CostEstimate(flops=32*S*T*T*256,bytes_accessed=8*S*T*384,transcendentals=S*T*T*6),
        name="attn_bwd",
    )(q,kv,a,da,lse)
    return dq,dkv.reshape(S,2,T,384)


def asm_kernel(count, spans, idx_ref, *refs):
    for p in range(count):
        o = idx_ref[p]
        for t, (lo, size) in enumerate(spans):
            refs[count + t][:, pl.ds(o, 1)] = refs[p][:, lo : lo + size][:, None]


def assemble(pieces, index, spans):
    n, _, width = pieces[0].shape
    count = len(pieces)
    return pl.pallas_call(
        functools.partial(asm_kernel, count, spans),
        in_specs=[pl.BlockSpec(memory_space=pltpu.SMEM)]
        + [pl.BlockSpec(memory_space=pltpu.VMEM)] * count,
        out_specs=[pl.BlockSpec(memory_space=pltpu.VMEM)] * len(spans),
        out_shape=[
            jax.ShapeDtypeStruct((n, count, size, width), pieces[0].dtype) for _, size in spans
        ],
        compiler_params=pltpu.CompilerParams(vmem_limit_bytes=40 * 2**20),
        name="assemble",
    )(index, *pieces)


def adam_kernel(f_ref, g_ref, w_ref, m_ref, v_ref, *refs):
    og, ow, om, ov = refs[-4:]
    s, i = pl.program_id(0), pl.program_id(1)
    for j in range(g_ref.shape[1]):
        g = g_ref[0, j].astype(f32)
        og[0, j] = g
        ow[0, j], om[0, j], ov[0, j] = adam_update(
            w_ref[0, j], m_ref[0, j], v_ref[0, j], g * f_ref[s, i * g_ref.shape[1] + j], decay_rate
        )


def adam_segments(factor, grad, start, w, m, v, before=None):
    _, count, rows, cols = grad.shape
    block = (1, 2, rows, cols)
    here = pl.BlockSpec(block, lambda s, i: (s, i + start // 2, 0, 0))
    before = [] if before is None else list(before)
    return pl.pallas_call(
        adam_kernel,
        grid=(2, count // 2),
        in_specs=[
            pl.BlockSpec(memory_space=pltpu.SMEM),
            pl.BlockSpec(block, lambda s, i: (s, i, 0, 0)),
            here,
            here,
            here,
        ]
        + [pl.BlockSpec(memory_space=pl.ANY)] * len(before),
        out_specs=[here] * 4,
        out_shape=[jax.ShapeDtypeStruct(w.shape, f32)] * 4,
        input_output_aliases={5 + k: k for k in range(len(before))},
        compiler_params=pltpu.CompilerParams(vmem_limit_bytes=40 * 2**20),
        name="adam",
    )(factor, grad, w, m, v, *before)


def make_shards(sizes):
    ns, nc, nt = sizes["shard"], sizes["ctx"], sizes["tensor"]
    owners = 2 * nt
    block_count = ns * nc
    cbits = nc.bit_length() - 1
    links = [("shard", 1 << b, (1 << b) << cbits) for b in range(1, ns.bit_length() - 1)]
    links += [("ctx", 1 << b, 1 << b) for b in range(cbits)]
    core_rel = 1 << cbits

    def pp(x, axis, xor):
        return lax.ppermute(x, axis, [(i, i ^ xor) for i in range(sizes[axis])])

    def all_sum(x):
        x = x + pp(x, "shard", 1)
        for axis, xor, _ in links:
            x = x + pp(x, axis, xor)
        for b in range(nt.bit_length() - 1):
            x = x + pp(x, "tensor", 1 << b)
        return x

    def after(x, *deps):
        return lax.optimization_barrier((x,) + deps)[0]

    def dyn(x, i, axis=0):
        return lax.dynamic_index_in_dim(x, i, axis, keepdims=False)

    def shards(
        image_rows,
        text_rows,
        condition,
        slot_table,
        weights,
        mom_one,
        mom_two,
        biases,
        bias_one,
        bias_two,
        image_cot,
        text_cot,
    ):
        hp = lax.Precision.HIGHEST
        nseq, D = condition.shape
        img = image_rows.shape[1]
        txt = text_rows.shape[1]
        ct = -(-txt // (owners * 16)) * 16
        ci = img // owners
        tpad = ct * owners
        T = img + tpad
        live_rows = img + txt
        cw = weights.shape[3]
        hw = cw // 2
        rows = weights.shape[1]
        shard_i, ctx_i, z = (lax.axis_index(a) for a in ("shard", "ctx", "tensor"))
        core = shard_i % 2
        first = core == 0
        me = shard_i * nc + ctx_i
        own = core * nt + z

        fixed = nseq == 2
        def pair(x):
            other = pp(x, "shard", 1)
            even = jnp.where(first, x, other)
            if fixed:
                return even
            return jnp.concatenate([even, jnp.where(first, other, x)], axis=0)

        def unpair(x):
            if fixed:
                return jnp.where(first, x, jnp.zeros_like(x))
            return jnp.where(first, x[:1], x[1:])

        table = pair(slot_table)
        S = table.shape[0]
        live = (table >= 0).astype(f32)
        picker = (table[:, None] == jnp.arange(nseq, dtype=jnp.int32)[None, :]).astype(f32)
        pad_txt = lambda x: jnp.pad(x, ((0, 0), (0, tpad - txt), (0, 0)))
        X = (pair(image_rows), pad_txt(pair(text_rows)))
        cots = (pair(image_cot), pad_txt(pair(text_cot)))

        wt = jnp.moveaxis(weights, 2, 1)
        wt = with_layout_constraint(wt, Layout(major_to_minor=(0, 1, 2, 3)))
        wb = wt.astype(bf)

        def halves(w):
            lo, hi = w[..., :hw], w[..., hw:]
            return lo, hi

        def cat(a, b):
            return jnp.concatenate([a, b], axis=-1)

        def group_one(w, which):
            k, v = halves(w[:, 7])[which], halves(w[:, 8])[which]
            q, o = halves(w[:, 6])[which], halves(w[:, 9])[which]
            return jnp.stack([cat(k[0], v[0]), cat(q[0], q[1]), cat(k[1], v[1]), cat(o[0], o[1])])

        one_lo, one_hi = group_one(wb, 0), group_one(wb, 1)
        up_pair = wb[:, 10:14].reshape(2, 2, 2, rows, cw)
        dn_pair = wb[:, 14:18].reshape(2, 2, 2, rows, cw)

        def gather_start(mine, theirs):
            return mine, pp(theirs, "shard", 1)

        def gather_step(state, step, ties=((), ())):
            if step == 0:
                mine, got = state
                n = mine.shape[0]
                state = [
                    {0: mine[part], core_rel: got[part]}
                    for part in (slice(0, n // 2), slice(n // 2, n))
                ]
            res = []
            for pieces, order, tie in zip(state, (links, links[::-1]), ties):
                axis, xor, rel = order[step]
                new = dict(pieces)
                for p, v in pieces.items():
                    new[p ^ rel] = pp(after(v, *tie) if tie else v, axis, xor)
                res.append(new)
            return res

        def gather_end(state):
            outs = []
            for pieces in state:
                keys = sorted(pieces)
                index = jnp.array(keys, jnp.int32) ^ me
                (full,) = assemble([pieces[p] for p in keys], index, [(0, rows)])
                outs.append(full.reshape(-1, D, cw))
            return outs

        def scatter_start(halves_in):
            res = []
            for g in halves_in:
                g = g.reshape(-1, block_count, rows, cw)
                res.append({p: dyn(g, me ^ p, 1) for p in range(block_count)})
            return res

        def scatter_send(state, step):
            res = []
            for pieces, order in zip(state, (links, links[::-1])):
                axis, xor, rel = order[step]
                res.append({p: pp(pieces[p ^ rel], axis, xor) for p in pieces if not p & rel})
            return res

        def scatter_add(state, got, tie=()):
            res = []
            for pieces, new in zip(state, got):
                res.append(
                    {
                        p: (pieces[p].astype(f32) + (after(v, *tie) if tie else v).astype(f32)).astype(bf)
                        for p, v in new.items()
                    }
                )
            return res

        def scatter_end(state):
            mine = jnp.concatenate([pieces[0] for pieces in state], axis=0)
            theirs = jnp.concatenate([pieces[core_rel] for pieces in state], axis=0)
            theirs = pp(theirs, "shard", 1)
            return jnp.where(first, mine, theirs), jnp.where(first, theirs, mine)

        def own_chunk(x, size):
            return lax.dynamic_slice_in_dim(x, own * size, size, 1)

        def fold(part_img, part_txt):
            buf = jnp.concatenate(
                [part_img.reshape(S, 2, nt, ci, D), part_txt.reshape(S, 2, nt, ct, D)], axis=3
            )
            buf = jnp.moveaxis(buf, 0, 2)
            got = pp(dyn(buf, 1 - core), "shard", 1)
            return (dyn(buf, core).astype(f32) + got.astype(f32)).astype(bf)

        def sum_scatter(half, tie=()):
            half = after(half, *tie) if tie else half
            got = [pp(dyn(half, z ^ k), "tensor", k) for k in range(nt - 1, 0, -1)]
            total = dyn(half, z).astype(f32)
            for g in got:
                total = total + g.astype(f32)
            return total[:, :ci], total[:, ci:]

        def spread_send(own_img, own_txt, tie=()):
            chunk = jnp.concatenate([own_img, own_txt], axis=1)
            chunk = after(chunk, *tie) if tie else chunk
            pieces = {0: chunk}
            for k in range(nt - 1, 0, -1):
                pieces[k] = pp(chunk, "tensor", k)
            return pieces

        def spread_end(pieces):
            pieces = dict(pieces)
            pieces.update({k + nt: pp(v, "shard", 1) for k, v in list(pieces.items())})
            keys = sorted(pieces)
            index = jnp.array(keys, jnp.int32) ^ own
            a, b = assemble([pieces[k] for k in keys], index, [(0, ci), (ci, ct)])
            return a.reshape(S, img, D), b.reshape(S, tpad, D)

        silu_all = jax.nn.silu(condition).astype(bf)
        sc_rows = lax.dynamic_slice_in_dim(silu_all, me * rows, rows, 1)
        mod = jnp.einsum("ni,sjie->nsje", sc_rows, wb[:, :6], preferred_element_type=f32)
        mod = mod + pp(mod, "shard", 1)
        for axis, xor, _ in links:
            mod = mod + pp(mod, axis, xor)
        mod = jnp.einsum("pn,nsje->psje", picker, mod, precision=hp)

        def over_tensor(x):
            stacked = jnp.stack([x] + [pp(x, "tensor", k) for k in range(1, nt)])
            return jnp.concatenate([dyn(stacked, z ^ k) for k in range(nt)], axis=-1)

        mod = over_tensor(mod) + biases[None, :, :6]
        row_of = lambda s, j: mod[:, s, j][:, None, :]


        steps = len(links)
        one = gather_start(jnp.where(first, one_lo, one_hi), jnp.where(first, one_hi, one_lo))
        for step in range(steps):
            one = gather_step(one, step)
        g_a, g_b = gather_end(one)
        w_kv = (g_a[0], g_b[0])
        w_q = (g_a[1][:, :hw], g_a[1][:, hw:])
        w_o = (g_b[1][:, :hw], g_b[1][:, hw:])
        mlp_half = lambda i: jnp.concatenate(
            [dyn(up_pair, i, 1), dyn(dn_pair, i, 1)], axis=1
        ).reshape(8, rows, cw)
        mlp = gather_start(mlp_half(core), mlp_half(1 - core))

        col = z * cw
        bias_half = lax.dynamic_slice_in_dim(biases, col + core * hw, hw, 2)
        bias_full = lax.dynamic_slice_in_dim(biases, col, cw, 2)

        hidden_one, q_parts, kv_parts = [], [], []
        token_live = jnp.arange(tpad) < txt
        for s in range(2):
            normed, _ = layer_norm(X[s].astype(f32))
            h = (normed * (1.0 + row_of(s, 1)) + row_of(s, 0)).astype(bf)
            hidden_one.append(h)
            q = jnp.einsum("sti,ie->ste", h, w_q[s], preferred_element_type=f32) + bias_half[s, 6]
            q = q.astype(bf) * jnp.asarray(DH**-0.5, bf)
            kv = jnp.einsum("sti,ie->ste", h, w_kv[s], preferred_element_type=f32)
            kv = kv + jnp.concatenate([jnp.zeros((hw,), f32), bias_half[s, 7]])
            if s == 1:
                kv = jnp.where(token_live[None, :, None], kv, 0.0)
            q_parts.append(jnp.pad(q, ((0, 0), (0, 0), (0, 64))))
            kv_parts.append(kv.astype(bf))
        q_all = jnp.concatenate(q_parts, axis=1)
        kv_own = jnp.concatenate(kv_parts, axis=1)
        kv_got = pp(kv_own, "ctx", 1)
        kv_all = jnp.stack([kv_own, kv_got], axis=1)
        mlp = gather_step(mlp, 0, ((kv_own,), (kv_got,)))
        attn, lse = attn_fwd(q_all, kv_all, img, live_rows)
        attn_split = (attn[:, :img], attn[:, img:])
        o_half = fold(
            *(
                jnp.einsum("ste,ie->sti", attn_split[s], w_o[s], preferred_element_type=f32).astype(bf)
                for s in range(2)
            )
        )
        o_sum = sum_scatter(o_half)
        for step in range(1, steps):
            mlp = gather_step(mlp, step, ((o_half,), (o_half,)))
        X_own = [own_chunk(X[s], (ci, ct)[s]).astype(f32) for s in range(2)]
        cot_live = [c * live.astype(bf)[:, None, None] for c in cots]
        dO = [own_chunk(cot_live[s], (ci, ct)[s]).astype(f32) for s in range(2)]
        o_proj, x1, n2, inv2, h2_own = [], [], [], [], []
        for s in range(2):
            o_proj.append(o_sum[s] + biases[s, 8])
            x1.append(X_own[s] + row_of(s, 2) * o_proj[s])
            n, i = layer_norm(x1[s])
            n2.append(n)
            inv2.append(i)
            h2_own.append((n * (1.0 + row_of(s, 4)) + row_of(s, 3)).astype(bf))
        h2 = spread_end(spread_send(*h2_own))
        mlp = [{p: after(v, h2[0]) for p, v in pieces.items()} for pieces in mlp]
        m_img, m_txt = gather_end(mlp)
        w_up, w_dn = (m_img[:2], m_txt[:2]), (m_img[2:], m_txt[2:])

        y_parts, dh_parts, up_bias, kept = [], [], [], []
        for s in range(2):
            dy_b = (cot_live[s].astype(f32) * row_of(s, 5)).astype(bf)
            dh_part = 0.0
            for j in range(2):
                u = jnp.einsum("sti,ie->ste", h2[s], w_up[s][j], preferred_element_type=f32)
                u = u + lax.dynamic_slice_in_dim(bias_full[s], 9 + 2 * core + j, 1, 0)[0]
                val, slope = gelu_parts(u)
                du = jnp.einsum("sti,ie->ste", dy_b, w_dn[s][j], preferred_element_type=f32) * slope
                du_b = du.astype(bf)
                up_bias.append(jnp.sum(du, axis=(0, 1)))
                dh_part = dh_part + jnp.einsum("ste,ie->sti", du_b, w_up[s][j], preferred_element_type=f32)
                kept.append((dy_b, val.astype(bf), du_b))
            dh_parts.append(dh_part.astype(bf))
        dh_half = fold(*dh_parts)
        dh2 = sum_scatter(dh_half)
        mlp_grads = []
        for s in range(2):
            ups, dns, y_part = [], [], 0.0
            for j in range(2):
                dy_b, G, du_b = kept[2 * s + j]
                G = after(G, dh_half)
                du_b = after(du_b, dh_half)
                y_part = y_part + jnp.einsum("ste,ie->sti", G, w_dn[s][j], preferred_element_type=f32)
                ups.append(jnp.einsum("sti,ste->ie", h2[s], du_b, preferred_element_type=f32).astype(bf))
                dns.append(jnp.einsum("sti,ste->ie", dy_b, G, preferred_element_type=f32).astype(bf))
            y_parts.append(y_part.astype(bf))
            mlp_grads.append(jnp.stack(ups + dns))
        mlp_state = scatter_start(mlp_grads)
        mlp_got = scatter_send(mlp_state, 0)
        y_half = fold(*y_parts)
        dx1, do_own, early, bias_own = [], [], [], []
        for s in range(2):
            g = dh2[s] * (1.0 + row_of(s, 4))
            d = dO[s] + norm_back(n2[s], inv2[s], g)
            dx1.append(d)
            do = d * row_of(s, 2)
            do_own.append(do.astype(bf))
            early.append(
                [
                    jnp.sum(d * o_proj[s], axis=1),
                    jnp.sum(dh2[s], axis=1),
                    jnp.sum(dh2[s] * n2[s], axis=1),
                ]
            )
            dy = dO[s] * row_of(s, 5)
            bias_own.append((jnp.sum(do, axis=(0, 1)), jnp.sum(dy, axis=(0, 1))))
        do_b = spread_end(spread_send(*do_own))
        mlp_state = scatter_add(mlp_state, mlp_got, (do_b[0],))
        y_sum = sum_scatter(y_half, (do_b[0],))
        out_own = []
        for s in range(2):
            y = y_sum[s] + biases[s, 13]
            out_own.append(((x1[s] + row_of(s, 5) * y) * live[:, None, None]).astype(bf))
            early[s] = jnp.stack(early[s] + [jnp.sum(dO[s] * y, axis=1)], axis=1)
        out_pieces = spread_send(*out_own)
        for step in range(1, steps):
            mlp_got = scatter_send(mlp_state, step)
            if step < steps - 1:
                mlp_state = scatter_add(mlp_state, mlp_got)

        da = jnp.concatenate(
            [
                jnp.einsum("sti,ie->ste", do_b[s], w_o[s], preferred_element_type=f32).astype(bf)
                for s in range(2)
            ],
            axis=1,
        )
        o_grads = [
            jnp.einsum("sti,ste->ie", do_b[s], attn_split[s], preferred_element_type=f32).astype(bf)
            for s in range(2)
        ]
        dq, dkv = attn_bwd(q_all, kv_all, attn, da, lse)
        dkv_got = pp(dkv[:, 1], "ctx", 1)
        dkv = dkv[:, 0].astype(f32) + dkv_got.astype(f32)
        out_pieces = {k: after(v, dq) for k, v in out_pieces.items()}
        out_img, out_txt = spread_end(out_pieces)
        mlp_state = scatter_add(mlp_state, mlp_got, (dq,))
        mlp_lo, mlp_hi = scatter_end(mlp_state)
        dkv = jnp.where((jnp.arange(T) < live_rows)[None, :, None], dkv, 0.0)
        dv_bias_src = dkv[:, :, hw:]
        dkv_b = dkv.astype(bf)
        q_grads, kv_grads, dh1_parts, qv_bias = [], [], [], []
        dqkv = []
        for s in range(2):
            part = slice(0, img) if s == 0 else slice(img, T)
            qs, kvs = dq[:, part], dkv_b[:, part]
            dqkv.append((qs, kvs))
            dh1_parts.append(
                (
                    jnp.einsum("ste,ie->sti", qs, w_q[s], preferred_element_type=f32)
                    + jnp.einsum("ste,ie->sti", kvs, w_kv[s], preferred_element_type=f32)
                ).astype(bf)
            )
            qv_bias.append((jnp.sum(qs.astype(f32), axis=(0, 1)), jnp.sum(dv_bias_src[:, part], axis=(0, 1))))
        d_half = fold(*dh1_parts)
        dh1 = sum_scatter(d_half)
        for s in range(2):
            qs, kvs = (after(x, d_half) for x in dqkv[s])
            q_grads.append(jnp.einsum("sti,ste->ie", hidden_one[s], qs, preferred_element_type=f32).astype(bf))
            kv_grads.append(jnp.einsum("sti,ste->ie", hidden_one[s], kvs, preferred_element_type=f32).astype(bf))
        one_state = scatter_start(
            [jnp.stack([kv_grads[0], cat(*q_grads)]), jnp.stack([kv_grads[1], cat(*o_grads)])]
        )
        one_got = scatter_send(one_state, 0)
        grad_own, late = [], []
        for s in range(2):
            n, i = layer_norm(X_own[s])
            g = dh1[s] * (1.0 + row_of(s, 1))
            grad_own.append((dx1[s] + norm_back(n, i, g)).astype(bf))
            late.append(jnp.stack([jnp.sum(dh1[s], axis=1), jnp.sum(dh1[s] * n, axis=1)], axis=1))
        grad_pieces = spread_send(*grad_own)
        one_state = scatter_add(one_state, one_got, (grad_own[0],))
        for step in range(1, steps):
            one_got = scatter_send(one_state, step)
            one_state = scatter_add(one_state, one_got)
        grad_img, grad_txt = spread_end(grad_pieces)
        one_lo, one_hi = scatter_end(one_state)
        join = lambda i, a: cat(one_lo[i, :, a * hw : (a + 1) * hw], one_hi[i, :, a * hw : (a + 1) * hw])
        dmod = jnp.stack([jnp.concatenate([late[s], early[s]], axis=1) for s in range(2)], axis=1)
        dmod = jnp.einsum("pn,psje->nsje", picker, dmod, precision=hp)

        def place(x, start):
            return lax.dynamic_update_slice_in_dim(jnp.zeros(x.shape[:-1] + (D,), f32), x, start, x.ndim - 1)

        bias_rows = []
        for s in range(2):
            qb, vb = qv_bias[s]
            up_place = jnp.stack(up_bias[2 * s : 2 * s + 2])
            up_rows = lax.dynamic_update_slice_in_dim(jnp.zeros((4, cw), f32), up_place, 2 * core, 0)
            bias_rows.append(
                jnp.concatenate(
                    [
                        place(jnp.stack([qb, vb]), col + core * hw),
                        bias_own[s][0][None],
                        place(up_rows, col),
                        bias_own[s][1][None],
                    ]
                )
            )
        packed = jnp.concatenate([dmod.reshape(-1, D), jnp.stack(bias_rows).reshape(-1, D)])
        packed = all_sum(packed)
        dmod = packed[: nseq * 12].reshape(nseq, 2, 6, D)
        bias_grad = jnp.concatenate(
            [jnp.sum(dmod, axis=0), packed[nseq * 12 :].reshape(2, 8, D)], axis=1
        )
        mod_cols = lax.dynamic_slice_in_dim(dmod, col, cw, 3)
        sc_wide = sc_rows.astype(f32)
        mod_grad = jnp.einsum("ni,nsje->sjie", sc_wide, mod_cols, precision=hp)
        cond_rows = jnp.einsum("nsje,sjie->ni", mod_cols, wb[:, :6].astype(f32), precision=hp)
        cond_part = place(cond_rows, me * rows)
        mlp_grad = jnp.stack([mlp_lo.reshape(2, 2, 2, rows, cw), mlp_hi.reshape(2, 2, 2, rows, cw)], axis=2)
        mlp_grad = mlp_grad.reshape(2, 8, rows, cw)
        one_grad = jnp.stack(
            [
                jnp.stack([join(1, s), join(2 * s, 0), join(2 * s, 1), join(3, s)])
                for s in range(2)
            ]
        )
        seg_sum = lambda g: jnp.sum(jnp.square(g.astype(f32)), axis=(2, 3))
        squares = jnp.concatenate([seg_sum(g) for g in (mod_grad, one_grad, mlp_grad)], axis=1)
        tail = jnp.concatenate([cond_part.reshape(-1), squares.reshape(-1)])
        tail = all_sum(tail)
        cond_grad = tail[: nseq * D].reshape(nseq, D) * silu_slope(condition)
        squares = tail[nseq * D :].reshape(2, 18)
        factor = jnp.minimum(1.0, clip_unit * D / jnp.sqrt(squares + clip_eps))
        moments = (wt, jnp.moveaxis(mom_one, 2, 1), jnp.moveaxis(mom_two, 2, 1))
        done = adam_segments(factor[:, 10:], mlp_grad, 10, *moments)
        done = adam_segments(factor[:, 6:10], one_grad, 6, *moments, before=done)
        done = adam_segments(factor[:, :6], mod_grad, 0, *moments, before=done)
        weight_grad, new_w, new_one, new_two = done
        bias_sq = jnp.sum(bias_grad * bias_grad, axis=2)
        bias_factor = jnp.minimum(1.0, clip_unit * D**0.5 / jnp.sqrt(bias_sq + clip_eps))
        new_b, new_b1, new_b2 = adam_update(
            biases, bias_one, bias_two, bias_grad * bias_factor[:, :, None], 0.0
        )
        back = lambda x: jnp.moveaxis(x, 1, 2)
        return (
            unpair(out_img),
            unpair(out_txt)[:, :txt],
            unpair(grad_img),
            unpair(grad_txt)[:, :txt],
            cond_grad,
            back(weight_grad),
            back(new_w),
            back(new_one),
            back(new_two),
            bias_grad,
            new_b,
            new_b1,
            new_b2,
        )

    return shards


def solution(mesh):
    sizes = dict(mesh.shape)
    rows = P("shard", "ctx", None)
    mat = P(None, ("shard", "ctx"), None, "tensor")
    return jax.shard_map(
        make_shards(sizes),
        mesh=mesh,
        in_specs=(rows, rows, P(), P("shard"), mat, mat, mat, P(), P(), P(), rows, rows),
        out_specs=(rows, rows, rows, rows, P(), mat, mat, mat, mat, P(), P(), P(), P()),
        check_vma=False,
    )
```

```python
import functools
import jax
import jax.numpy as jnp
from jax import lax
from jax.experimental import pallas as pl
from jax.experimental.pallas import tpu as pltpu
from jax.sharding import PartitionSpec as P

DH = 64
NT = (((1,), (1,)), ((), ()))
TN = (((0,), (0,)), ((), ()))
NN = (((1,), (0,)), ((), ()))
bf = jnp.bfloat16
f32 = jnp.float32

beta_one = 0.9
beta_two = 0.95
learn_rate = 0.1
decay_rate = 0.1
adam_eps = 1e-08
adam_step = 10.0
norm_eps = 1e-06
gelu_coef = 0.044715
root_two_pi = 0.7978845608028654
clip_unit = 0.0001
clip_eps = 1e-12


def norm_back(normed, inverse, upstream):
    mean_grad = jnp.mean(upstream, axis=-1, keepdims=True)
    mean_dot = jnp.mean(upstream * normed, axis=-1, keepdims=True)
    return inverse * (upstream - mean_grad - normed * mean_dot)


def gelu_parts(preact):
    inner = root_two_pi * (preact + gelu_coef * preact * preact * preact)
    tanh_value = jnp.tanh(inner)
    value_out = 0.5 * preact * (1.0 + tanh_value)
    slope_out = 0.5 * (1.0 + tanh_value) + 0.5 * preact * (
        1.0 - tanh_value * tanh_value
    ) * root_two_pi * (1.0 + 3.0 * gelu_coef * preact * preact)
    return (value_out, slope_out)


def silu_slope(drawn_values):
    sigmoid_val = jax.nn.sigmoid(drawn_values)
    return sigmoid_val * (1.0 + drawn_values * (1.0 - sigmoid_val))


def adam_update(parameter, moment_one, moment_two, gradient, decay_factor):
    new_one = beta_one * moment_one + (1.0 - beta_one) * gradient
    new_two = beta_two * moment_two + (1.0 - beta_two) * gradient * gradient
    first_hat = new_one / (1.0 - beta_one**adam_step)
    second_hat = new_two / (1.0 - beta_two**adam_step)
    new_param = parameter - learn_rate * (
        first_hat / (jnp.sqrt(second_hat) + adam_eps) + decay_factor * parameter
    )
    return (new_param, new_one, new_two)


def dotf(a, b, dims, precision=None):
    return lax.dot_general(a, b, dims, preferred_element_type=f32, precision=precision)


def vm():
    return pl.BlockSpec(memory_space=pltpu.VMEM)


def sm():
    return pl.BlockSpec(memory_space=pltpu.SMEM)


def shape(dims, dtype=bf):
    return jax.ShapeDtypeStruct(dims, dtype)


def params(mib=58):
    return pltpu.CompilerParams(vmem_limit_bytes=mib * 2**20)


def cost(flops, nbytes, trans=0):
    return pl.CostEstimate(flops=1024, bytes_accessed=1024, transcendentals=0)


def full(dims):
    return pl.BlockSpec(dims, lambda *_: (0,) * len(dims), pipeline_mode=pl.Buffered(1))


def prep_kernel(a_ref, b_ref, one_ref, o_ref):
    hw = a_ref.shape[3] // 2
    cat = lambda x, y: jnp.concatenate([x, y], axis=-1)
    q, k = ([a_ref[s, j].astype(bf) for s in range(2)] for j in range(2))
    v, o = ([b_ref[s, j].astype(bf) for s in range(2)] for j in range(2))
    for c in range(2):
        half = lambda w: w[:, c * hw : (c + 1) * hw]
        one_ref[3 * c] = cat(half(k[0]), half(v[0]))
        one_ref[3 * c + 1] = cat(half(q[0]), half(q[1]))
        one_ref[3 * c + 2] = cat(half(k[1]), half(v[1]))
        o_ref[c] = cat(half(o[0]), half(o[1]))


def prep_one(wt):
    _, _, rows, cw = wt.shape
    seg = lambda k: pl.BlockSpec((2, 2, rows, cw), lambda i: (0, k, 0, 0))
    outs = [shape((6, rows, cw)), shape((2, rows, cw))]
    return pl.pallas_call(
        prep_kernel,
        grid=(1,),
        in_specs=[seg(3), seg(4)],
        out_specs=[full(o.shape) for o in outs],
        out_shape=outs,
        compiler_params=params(),
        cost_estimate=cost(0, 0),
        name="prep_one",
    )(wt, wt)


def mod_kernel(sc_ref, w_ref, o_ref):
    for j in range(2):
        o_ref[0, j] = dotf(sc_ref[...], w_ref[0, j].astype(bf), NN)


def mod_partial(sc, wt):
    _, _, rows, cw = wt.shape
    n = sc.shape[0]
    return pl.pallas_call(
        mod_kernel,
        grid=(2, 3),
        in_specs=[
            pl.BlockSpec((n, rows), lambda s, i: (0, 0)),
            pl.BlockSpec((1, 2, rows, cw), lambda s, i: (s, i, 0, 0)),
        ],
        out_specs=pl.BlockSpec((1, 2, n, cw), lambda s, i: (s, i, 0, 0)),
        out_shape=shape((2, 6, n, cw), f32),
        compiler_params=params(),
        cost_estimate=cost(0, 0),
        name="mod_partial",
    )(sc, wt)


def normed_of(x):
    center = x - jnp.mean(x, axis=-1, keepdims=True)
    inverse = lax.rsqrt(jnp.mean(center * center, axis=-1, keepdims=True) + norm_eps)
    return center * inverse, inverse


def qkv_kernel(n_img, txt, hw, core_ref, xi_ref, xt_ref, mod_ref, bq_ref, bkv_ref, w_ref, hi_ref, ht_ref, ni_ref, nt_ref, q_ref, kv_ref):
    i = pl.program_id(0)
    rows = xi_ref.shape[0]

    def run(s, x, h_ref, n_ref, at, live):
        size = x.shape[0]
        n, _ = normed_of(x.astype(f32))
        n_ref[...] = n.astype(bf)
        h = (n * (1.0 + mod_ref[6 * s + 1 : 6 * s + 2]) + mod_ref[6 * s : 6 * s + 1]).astype(bf)
        h_ref[...] = h
        q = dotf(h, w_ref[1, :, hw * s : hw * (s + 1)], NN) + bq_ref[s : s + 1]
        q = (q.astype(bf).astype(f32) * DH**-0.5).astype(bf)
        q_ref[pl.ds(at, size)] = jnp.concatenate([q, jnp.zeros((size, 256 - hw), bf)], axis=1)
        kv = dotf(h, w_ref[2 * s], NN) + bkv_ref[s : s + 1]
        kv_ref[pl.ds(at, size)] = (kv if live is None else jnp.where(live, kv, 0.0)).astype(bf)

    @pl.when(i < n_img)
    def _():
        run(0, xi_ref[...], hi_ref, ni_ref, pl.multiple_of(i * rows, rows), None)

    @pl.when(i >= n_img)
    def _():
        live = lax.broadcasted_iota(jnp.int32, (xt_ref.shape[0], 1), 0) < txt
        run(1, xt_ref[...], ht_ref, nt_ref, n_img * rows, live)


def qkv(core, xi, xt, txt, mod, bq, bkv, w):
    img, D = xi.shape
    tpad = xt.shape[0]
    n_img = 2
    rows = img // n_img
    T = img + tpad
    hw, cw = bq.shape[1], w.shape[2]
    x_spec = pl.BlockSpec((rows, D), lambda i, c: (jnp.minimum(i, n_img - 1), 0))
    outs = [shape((img, D)), shape((tpad, D))] * 2 + [shape((T, 256)), shape((T, cw))]
    return pl.pallas_call(
        functools.partial(qkv_kernel, n_img, txt, hw),
        grid_spec=pltpu.PrefetchScalarGridSpec(
            num_scalar_prefetch=1,
            grid=(n_img + 1,),
            in_specs=[
                x_spec,
                full((tpad, D)),
                full(mod.shape),
                full(bq.shape),
                full(bkv.shape),
                pl.BlockSpec((3, D, cw), lambda i, c: (c[0], 0, 0), pipeline_mode=pl.Buffered(1)),
            ],
            out_specs=[x_spec, full((tpad, D))] * 2 + [full(o.shape) for o in outs[4:]],
        ),
        out_shape=outs,
        compiler_params=params(),
        cost_estimate=cost(2 * T * D * 3 * hw, 4 * T * D),
        name="qkv",
    )(core, xi, xt, mod, bq, bkv, w)


def store_chunks(core, send_ref, keep_ref, src, lo):
    nt = send_ref.shape[0]
    n = src.shape[0] // (2 * nt)
    for ref, c in ((send_ref, 1 - core), (keep_ref, core)):
        for t in range(nt):
            ref[t, lo : lo + n] = src[pl.ds(pl.multiple_of((c * nt + t) * n, n), n)].astype(bf)


def chunk_blocks(nt, chunk, width):
    return [pl.BlockSpec((nt, chunk, width), lambda i, c: (0, 0, i))] * 2


def oproj_kernel(img, core_ref, a_ref, w_ref, send_ref, keep_ref, acc):
    hw = a_ref.shape[1]
    acc[:img] = dotf(a_ref[:img], w_ref[0, :, :hw], NT)
    acc[img:] = dotf(a_ref[img:], w_ref[0, :, hw:], NT)
    store_chunks(core_ref[0], send_ref, keep_ref, acc.at[:img], 0)
    store_chunks(core_ref[0], send_ref, keep_ref, acc.at[img:], img // (2 * send_ref.shape[0]))


def oproj(core, a, w, nt, img):
    T, hw = a.shape
    _, D, cw = w.shape
    width = D // 3
    return pl.pallas_call(
        functools.partial(oproj_kernel, img),
        grid_spec=pltpu.PrefetchScalarGridSpec(
            num_scalar_prefetch=1,
            grid=(3,),
            in_specs=[full(a.shape), pl.BlockSpec((1, width, cw), lambda i, c: (c[0], i, 0))],
            out_specs=chunk_blocks(nt, T // (2 * nt), width),
            scratch_shapes=[pltpu.VMEM((T, width), f32)],
        ),
        out_shape=[shape((nt, T // (2 * nt), D))] * 2,
        compiler_params=params(),
        cost_estimate=cost(2 * T * D * hw, 2 * T * D),
        name="oproj",
    )(core, a, w)


def total(ref):
    t = ref[0].astype(f32)
    for k in range(1, ref.shape[0]):
        t = t + ref[k].astype(f32)
    return t


def store_copies(ref, rows, x):
    for k in range(ref.shape[0]):
        ref[k, rows] = x


def own_specs(ci, ct, D):
    return [
        pl.BlockSpec((ci, D), lambda i, o: (o[0], 0)),
        pl.BlockSpec((ct, D), lambda i, o: (o[0], 0)),
    ]


def whole(dims):
    return pl.BlockSpec(dims, lambda i, o: (0,) * len(dims))


def row_call(kernel, name, own, ci, ct, D, tokens, wholes, outs, deps=()):
    specs = [s for _ in tokens for s in own_specs(ci, ct, D)] + [whole(w.shape) for w in wholes]
    flat = [x for pair in tokens for x in pair]
    n_in = 1 + len(specs)
    return pl.pallas_call(
        lambda *refs: kernel(*refs[:n_in], *refs[n_in + len(deps) :]),
        grid_spec=pltpu.PrefetchScalarGridSpec(
            num_scalar_prefetch=1,
            grid=(1,),
            in_specs=specs + [pl.BlockSpec(memory_space=pl.ANY)] * len(deps),
            out_specs=[whole(o.shape) for o in outs],
        ),
        out_shape=outs,
        compiler_params=params(),
        cost_estimate=cost(0, 0),
        name=name,
    )(own, *flat, *wholes, *deps)


def after_attn_kernel(ci, own_ref, xi_ref, xt_ref, mod_ref, b_ref, part_ref, h_ref, o_ref):
    sums = total(part_ref)
    for s, x_ref in enumerate((xi_ref, xt_ref)):
        rows = slice(0, ci) if s == 0 else slice(ci, sums.shape[0])
        m = lambda j: mod_ref[6 * s + j : 6 * s + j + 1]
        o = sums[rows] + b_ref[14 * s + 8 : 14 * s + 9]
        n, _ = normed_of(x_ref[...].astype(f32) + m(2) * o)
        store_copies(h_ref, rows, (n * (1.0 + m(4)) + m(3)).astype(bf))
        o_ref[rows] = o


def colsum(x):
    return jnp.sum(x, axis=0, keepdims=True)


def after_mlp_kernel(ci, own_ref, xi_ref, xt_ref, ci_ref, ct_ref, mod_ref, o_ref, part_ref, do_ref, dx_ref, sum_ref):
    sums = total(part_ref)
    for s, (x_ref, c_ref) in enumerate(((xi_ref, ci_ref), (xt_ref, ct_ref))):
        rows = slice(0, ci) if s == 0 else slice(ci, sums.shape[0])
        m = lambda j: mod_ref[6 * s + j : 6 * s + j + 1]
        o = o_ref[rows]
        n, inv = normed_of(x_ref[...].astype(f32) + m(2) * o)
        dh = sums[rows]
        cot = c_ref[...].astype(f32)
        dx = cot + norm_back(n, inv, dh * (1.0 + m(4)))
        do = dx * m(2)
        store_copies(do_ref, rows, do.astype(bf))
        dx_ref[rows] = dx
        rows_out = [colsum(dx * o), colsum(dh), colsum(dh * n), colsum(do), colsum(cot * m(5))]
        sum_ref[8 * s : 8 * s + 8] = jnp.concatenate(rows_out + [jnp.zeros((3, dx.shape[1]), f32)], axis=0)


def after_down_kernel(
    ci, own_ref, xi_ref, xt_ref, ci_ref, ct_ref, mod_ref, b_ref, live_ref, o_ref, part_ref, out_ref, sum_ref
):
    sums = total(part_ref)
    for s, (x_ref, c_ref) in enumerate(((xi_ref, ci_ref), (xt_ref, ct_ref))):
        rows = slice(0, ci) if s == 0 else slice(ci, sums.shape[0])
        m = lambda j: mod_ref[6 * s + j : 6 * s + j + 1]
        y = sums[rows] + b_ref[14 * s + 13 : 14 * s + 14]
        x1 = x_ref[...].astype(f32) + m(2) * o_ref[rows]
        store_copies(out_ref, rows, ((x1 + m(5) * y) * live_ref[...]).astype(bf))
        top = colsum(c_ref[...].astype(f32) * y)
        sum_ref[8 * s : 8 * s + 8] = jnp.concatenate([top, jnp.zeros((7, y.shape[1]), f32)], axis=0)


def after_back_kernel(ci, own_ref, xi_ref, xt_ref, mod_ref, dx_ref, part_ref, g_ref):
    sums = total(part_ref)
    for s, x_ref in enumerate((xi_ref, xt_ref)):
        rows = slice(0, ci) if s == 0 else slice(ci, sums.shape[0])
        n, inv = normed_of(x_ref[...].astype(f32))
        dh = sums[rows]
        g = dx_ref[rows] + norm_back(n, inv, dh * (1.0 + mod_ref[6 * s + 1 : 6 * s + 2]))
        store_copies(g_ref, rows, g.astype(bf))


def stream_blocks(img, tpad, width):
    return [
        pl.BlockSpec((1, img, width), lambda k, c: (jnp.minimum(k, 1), 0, 0)),
        pl.BlockSpec((1, tpad, width), lambda k, c: (jnp.maximum(k - 2, 0), 0, 0)),
    ]


def seg_call(kernel, name, core, ins, in_specs, outs, out_specs, scratch=(), est=None):
    return pl.pallas_call(
        kernel,
        grid_spec=pltpu.PrefetchScalarGridSpec(
            num_scalar_prefetch=1,
            grid=(4,),
            in_specs=in_specs,
            out_specs=out_specs,
            scratch_shapes=list(scratch),
        ),
        out_shape=outs,
        compiler_params=params(),
        cost_estimate=est or cost(0, 0),
        name=name,
    )(core, *ins)


def zeros_kernel(core_ref, o_ref):
    o_ref[...] = jnp.zeros_like(o_ref)


def zeros(core, n, D, cw):
    return pl.pallas_call(
        zeros_kernel,
        grid=(n,),
        in_specs=[sm()],
        out_specs=pl.BlockSpec((1, D, cw), lambda i: (i, 0, 0)),
        out_shape=shape((n, D, cw)),
        compiler_params=params(),
        cost_estimate=cost(0, 0),
        name="zeros",
    )(core)


def seg_of(base):
    return lambda k, c: ((k // 2) * 8 + base + 2 * c[0] + lax.rem(k, 2), 0, 0)


def grad_gate_kernel(core_ref, ci_ref, ct_ref, mod_ref, w_ref, dyi_ref, dyt_ref, dgi_ref, dgt_ref):
    k = pl.program_id(0)
    for s, (c, dy, dg) in enumerate(((ci_ref, dyi_ref, dgi_ref), (ct_ref, dyt_ref, dgt_ref))):

        @pl.when(k == 2 * s)
        def _():
            dy[...] = (c[...].astype(f32) * mod_ref[6 * s + 5 : 6 * s + 6]).astype(bf)

        @pl.when(jnp.right_shift(k, 1) == s)
        def _():
            dg[0] = dotf(dy[...], w_ref[0], NN)


def grad_gate(core, cot_i, cot_t, mod, w):
    img, D = cot_i.shape
    tpad = cot_t.shape[0]
    T = img + tpad
    cw = w.shape[2]
    return seg_call(
        grad_gate_kernel,
        "grad_gate",
        core,
        [cot_i, cot_t, mod, w],
        [full(cot_i.shape), full(cot_t.shape), full(mod.shape), pl.BlockSpec((1, D, cw), seg_of(4))],
        [shape((img, D)), shape((tpad, D)), shape((2, img, cw), f32), shape((2, tpad, cw), f32)],
        [full(cot_i.shape), full(cot_t.shape)] + stream_blocks(img, tpad, cw),
        est=cost(4 * T * D * cw, 4 * T * D),
    )


def place_chunks(core, mine, other, img_ref, txt_ref):
    nt = mine.shape[0]
    ci, ct = img_ref.shape[0] // (2 * nt), txt_ref.shape[0] // (2 * nt)
    for ref, c in ((mine, core), (other, 1 - core)):
        for t in range(nt):
            o = c * nt + t
            img_ref[pl.ds(pl.multiple_of(o * ci, ci), ci)] = ref[t, :ci]
            txt_ref[pl.ds(pl.multiple_of(o * ct, ct), ct)] = ref[t, ci:]


def mlp_kernel(core_ref, mine, other, dgi, dgt, w_ref, b_ref, hi, ht, gi, gt, dui, dut, send_ref, keep_ref, bias_ref, acc_i, acc_t):
    k = pl.program_id(0)

    @pl.when(k == 0)
    def _():
        place_chunks(core_ref[0], mine, other, hi, ht)
        bias_ref[...] = jnp.zeros_like(bias_ref)

    lo = 0
    for s, (h, dg, g, du_ref, acc) in enumerate(((hi, dgi, gi, dui, acc_i), (ht, dgt, gt, dut, acc_t))):

        @pl.when(jnp.right_shift(k, 1) == s)
        def _():
            size = min(256, h.shape[0])
            sums = None
            for r in range(0, h.shape[0], size):
                at = slice(r, r + size)
                u = dotf(h[at], w_ref[0], NN) + b_ref[pl.ds(k, 1)]
                val, slope = gelu_parts(u)
                g[0, at] = val.astype(bf)
                du = dg[0, at] * slope
                du_b = du.astype(bf)
                du_ref[0, at] = du_b
                sums = colsum(du) if sums is None else sums + colsum(du)
                acc[at] = jnp.where(k == 2 * s, 0.0, acc[at]) + dotf(du_b, w_ref[0], NT)

            bias_ref[pl.ds(k, 1)] = sums

            @pl.when(k == 2 * s + 1)
            def _():
                store_chunks(core_ref[0], send_ref, keep_ref, acc, lo)

        lo += acc.shape[0] // (2 * send_ref.shape[0])


def mlp(core, mine, other, dgi, dgt, w, b):
    nt, chunk, D = mine.shape
    img, tpad, cw = dgi.shape[1], dgt.shape[1], w.shape[2]
    T = img + tpad
    blocks = stream_blocks(img, tpad, cw)
    whole_outs = [shape((img, D)), shape((tpad, D))]
    ends = [shape((nt, chunk, D)), shape((nt, chunk, D)), shape((8, cw), f32)]
    return seg_call(
        mlp_kernel,
        "mlp",
        core,
        [mine, other, dgi, dgt, w, b],
        [full(mine.shape)] * 2 + blocks + [pl.BlockSpec((1, D, cw), seg_of(0)), full(b.shape)],
        whole_outs + [shape((2, img, cw)), shape((2, tpad, cw))] * 2 + ends,
        [full(o.shape) for o in whole_outs] + blocks + blocks + [full(o.shape) for o in ends],
        [pltpu.VMEM((img, D), f32), pltpu.VMEM((tpad, D), f32)],
        cost(8 * T * D * cw, 4 * T * D, 2 * T * cw),
    )


def down_kernel(core_ref, gi, gt, w_ref, send_ref, keep_ref, acc_i, acc_t):
    k = pl.program_id(0)
    lo = 0
    for s, (g, acc) in enumerate(((gi, acc_i), (gt, acc_t))):

        @pl.when(jnp.right_shift(k, 1) == s)
        def _():
            y = dotf(g[0], w_ref[0], NT)

            @pl.when(k == 2 * s)
            def _():
                acc[...] = y

            @pl.when(k == 2 * s + 1)
            def _():
                acc[...] += y
                store_chunks(core_ref[0], send_ref, keep_ref, acc, lo)

        lo += acc.shape[0] // (2 * send_ref.shape[0])


def down(core, gi, gt, w, nt):
    img, tpad = gi.shape[1], gt.shape[1]
    D, cw = w.shape[1:]
    T = img + tpad
    ends = [shape((nt, T // (2 * nt), D))] * 2
    return seg_call(
        down_kernel,
        "down",
        core,
        [gi, gt, w],
        stream_blocks(img, tpad, cw) + [pl.BlockSpec((1, D, cw), seg_of(4))],
        ends,
        [full(o.shape) for o in ends],
        [pltpu.VMEM((img, D), f32), pltpu.VMEM((tpad, D), f32)],
        cost(4 * T * D * cw, 2 * T * D),
    )


def grad_attn_kernel(core_ref, mine, other, w_ref, doi_ref, dot_ref, da_ref):
    img, hw = doi_ref.shape[0], da_ref.shape[1]
    place_chunks(core_ref[0], mine, other, doi_ref, dot_ref)
    da_ref[:img] = dotf(doi_ref[...], w_ref[0, :, :hw], NN).astype(bf)
    da_ref[img:] = dotf(dot_ref[...], w_ref[0, :, hw:], NN).astype(bf)


def grad_attn(core, mine, other, w, img, tpad):
    _, D, cw = w.shape
    hw = cw // 2
    T = img + tpad
    outs = [shape((img, D)), shape((tpad, D)), shape((T, hw))]
    return pl.pallas_call(
        grad_attn_kernel,
        grid_spec=pltpu.PrefetchScalarGridSpec(
            num_scalar_prefetch=1,
            grid=(1,),
            in_specs=[full(mine.shape)] * 2 + [pl.BlockSpec((1, D, cw), lambda i, c: (c[0], 0, 0))],
            out_specs=[full(o.shape) for o in outs],
        ),
        out_shape=outs,
        compiler_params=params(),
        cost_estimate=cost(2 * T * D * hw, 4 * T * D),
        name="grad_attn",
    )(core, mine, other, w)


def grad_in_kernel(
    img, txt, core_ref, dep_ref, dep_two_ref, q_ref, a_ref, b_ref, ni_ref, nt_ref, w_ref, send_ref, keep_ref, kvi_ref, kvt_ref, qv_ref, sum_ref, acc
):
    T, hw = q_ref.shape

    @pl.when(pl.program_id(0) == 0)
    def _():
        for s, (at, out) in enumerate(((slice(0, img), kvi_ref), (slice(img, T), kvt_ref))):
            kv = a_ref[at].astype(f32) + b_ref[at].astype(f32)
            if s == 1:
                kv = jnp.where(lax.broadcasted_iota(jnp.int32, (T - img, 1), 0) < txt, kv, 0.0)
            out[...] = kv.astype(bf)
            sums = jnp.concatenate([colsum(q_ref[at].astype(f32)), colsum(kv)[:, hw:]], axis=1)
            qv_ref[4 * s : 4 * s + 4] = jnp.broadcast_to(sums, (4, 2 * hw))

    acc[:img] = dotf(q_ref[:img], w_ref[1, :, :hw], NT) + dotf(kvi_ref[...], w_ref[0], NT)
    acc[img:] = dotf(q_ref[img:], w_ref[1, :, hw:], NT) + dotf(kvt_ref[...], w_ref[2], NT)
    rows = []
    for at, n_ref in ((slice(0, img), ni_ref), (slice(img, T), nt_ref)):
        rows += [colsum(acc[at]), colsum(acc[at] * n_ref[...].astype(f32))]
    sum_ref[...] = jnp.concatenate(rows + [jnp.zeros((4, acc.shape[1]), f32)], axis=0)
    store_chunks(core_ref[0], send_ref, keep_ref, acc.at[:img], 0)
    store_chunks(core_ref[0], send_ref, keep_ref, acc.at[img:], img // (2 * send_ref.shape[0]))


def grad_in(core, deps, dq, kv_a, kv_b, n_img, n_txt, w, nt, txt):
    T, hw = dq.shape
    img, tpad = n_img.shape[0], n_txt.shape[0]
    cw = kv_a.shape[1]
    D = w.shape[1]
    width = D // 3
    ends = [shape((img, cw)), shape((tpad, cw)), shape((8, cw), f32)]
    column = lambda n: pl.BlockSpec((n, width), lambda i, c: (0, i))
    return pl.pallas_call(
        functools.partial(grad_in_kernel, img, txt),
        grid_spec=pltpu.PrefetchScalarGridSpec(
            num_scalar_prefetch=1,
            grid=(3,),
            in_specs=[pl.BlockSpec(memory_space=pl.ANY)] * 2
            + [full(dq.shape), full(kv_a.shape), full(kv_b.shape), column(img), column(tpad)]
            + [pl.BlockSpec((3, width, cw), lambda i, c: (c[0], i, 0))],
            out_specs=chunk_blocks(nt, T // (2 * nt), width) + [full(o.shape) for o in ends] + [column(8)],
            scratch_shapes=[pltpu.VMEM((T, width), f32)],
        ),
        out_shape=[shape((nt, T // (2 * nt), D))] * 2 + ends + [shape((8, D), f32)],
        compiler_params=params(),
        cost_estimate=cost(2 * T * D * 3 * hw, 2 * T * D),
        name="grad_in",
    )(core, *deps, dq, kv_a, kv_b, n_img, n_txt, w)


def tokens_kernel(core_ref, flag_ref, mine, other, *refs):
    oi_ref, ot_ref = refs[-2:]
    on = flag_ref[0] != 0

    @pl.when(on)
    def _():
        place_chunks(core_ref[0], mine, other, oi_ref, ot_ref)

    @pl.when(jnp.logical_not(on))
    def _():
        oi_ref[...] = jnp.zeros_like(oi_ref)
        ot_ref[...] = jnp.zeros_like(ot_ref)


def join_tokens(core, flag, mine, other, img, tpad, deps=()):
    D = mine.shape[2]
    return pl.pallas_call(
        tokens_kernel,
        in_specs=[sm(), sm(), vm(), vm()] + [pl.BlockSpec(memory_space=pl.ANY)] * len(deps),
        out_specs=[vm()] * 2,
        out_shape=[shape((img, D)), shape((tpad, D))],
        compiler_params=params(),
        cost_estimate=cost(0, 4 * (img + tpad) * D),
        name="join_tokens",
    )(core, flag, mine, other, *deps)


def pack_kernel(picker_ref, place_ref, mid_ref, low_ref, end_ref, up_ref, qv_ref, out_ref):
    nseq = picker_ref.shape[0]
    z, core = place_ref[0], place_ref[1]
    D, cw = mid_ref.shape[1], up_ref.shape[1]
    hw = cw // 2
    out_ref[...] = jnp.zeros_like(out_ref)
    for s in range(2):
        rows = jnp.concatenate(
            [end_ref[2 * s : 2 * s + 2], mid_ref[8 * s : 8 * s + 3], low_ref[8 * s : 8 * s + 1]], axis=0
        )
        for n in range(nseq):
            out_ref[12 * n + 6 * s : 12 * n + 6 * s + 6] = rows * picker_ref[n]
        at = 12 * nseq
        out_ref[at + 2 * s : at + 2 * s + 2] = mid_ref[8 * s + 3 : 8 * s + 5]
        lane = lax.broadcasted_iota(jnp.int32, (1, D), 1)
        inside = jnp.logical_and(lane >= z * cw, lane < (z + 1) * cw)
        up = jnp.concatenate([up_ref[2 * s : 2 * s + 2]] * (D // cw), axis=1)
        up = jnp.where(inside, up, 0.0)
        none = jnp.zeros_like(up)
        first = core == 0
        up = jnp.concatenate([jnp.where(first, up, none), jnp.where(first, none, up)], axis=0)
        out_ref[at + 4 + 4 * s : at + 8 + 4 * s] = up
        row = qv_ref[4 * s : 4 * s + 1]
        start = z * cw + core * hw
        inside = jnp.logical_and(lane >= start, lane < start + hw)
        for k in range(2):
            part = row[:, k * hw : (k + 1) * hw]
            part = jnp.concatenate([part, part], axis=1)
            part = jnp.concatenate([part] * (D // cw), axis=1)
            out_ref[at + 12 + 2 * s + k : at + 13 + 2 * s + k] = jnp.where(inside, part, 0.0)


def pack_sums(picker, place, mid, low, end, up, qv):
    D = mid.shape[1]
    rows = -(-(12 * picker.shape[0] + 16) // 8) * 8
    return pl.pallas_call(
        pack_kernel,
        in_specs=[sm(), sm()] + [vm()] * 5,
        out_specs=vm(),
        out_shape=shape((rows, D), f32),
        compiler_params=params(),
        cost_estimate=cost(0, 0),
        name="pack_sums",
    )(picker, place, mid, low, end, up, qv)


def attn_fwd_kernel(heads, img, live, q_ref, ka_ref, kb_ref, a_ref, lse_ref):
    T = ka_ref.shape[0]
    bq = q_ref.shape[0]
    lane = lax.broadcasted_iota(jnp.int32, (1, 256), 1)
    lane1 = lax.broadcasted_iota(jnp.int32, (1, 128), 1)
    keep = lax.broadcasted_iota(jnp.int32, (1, T - img), 1) < live - img
    q = q_ref[...]
    acc = jnp.zeros((bq, 256), f32)
    lse_tile = jnp.zeros((bq, 128), f32)
    for h in range(heads):
        qm = jnp.where((lane >> 6) == h, q, jnp.zeros_like(q))
        parts = []
        for kv in (ka_ref, kb_ref):
            parts.append((dotf(qm, kv[:img, :256], NT), kv, 0, img))
            s = dotf(qm, kv[img:, :256], NT)
            parts.append((jnp.where(keep, s, -1e30), kv, img, T))
        m = functools.reduce(jnp.maximum, [jnp.max(p[0], axis=1, keepdims=True) for p in parts])
        l = jnp.zeros((bq, 1), f32)
        pv = jnp.zeros((bq, 256), f32)
        for s, kv, lo, hi in parts:
            e = jnp.exp(s - m)
            l = l + jnp.sum(e, axis=1, keepdims=True)
            pv = pv + dotf(e.astype(bf), kv[lo:hi, 128:384], NN)
        acc = jnp.where((lane >> 6) == h + 1, pv / l, acc)
        lse_tile = jnp.where(lane1 == h, m + jnp.log(l), lse_tile)
    a_ref[...] = acc[:, 64:256].astype(bf)
    lse_ref[...] = lse_tile.T[:8]


def attn_fwd(q, kv_a, kv_b, img, live, bq=384, heads=3):
    T = q.shape[0]
    return pl.pallas_call(
        functools.partial(attn_fwd_kernel, heads, img, live),
        grid=(T // bq,),
        in_specs=[pl.BlockSpec((bq, 256), lambda i: (i, 0)), full((T, 384)), full((T, 384))],
        out_specs=[pl.BlockSpec((bq, 192), lambda i: (i, 0)), pl.BlockSpec((8, bq), lambda i: (0, i))],
        out_shape=[shape((T, 192)), shape((8, T), f32)],
        compiler_params=params(),
        cost_estimate=cost(16 * T * T * 256, 4 * T * 384, T * T * 6),
        name="attn_fwd",
    )(q, kv_a, kv_b)


def attn_bwd_kernel(heads, q_ref, ka_ref, kb_ref, a_ref, da_ref, lse_ref, dq_ref, dka_ref, dkb_ref, daw, delta, dqa):
    step = pl.program_id(0)
    T = q_ref.shape[0]
    lane = lax.broadcasted_iota(jnp.int32, (1, 256), 1)

    @pl.when(step == 0)
    def _():
        da = da_ref[...]
        daw[...] = jnp.concatenate([jnp.zeros((T, 64), bf), da], axis=1)
        prod = da.astype(f32) * a_ref[...].astype(f32)
        col = lax.broadcasted_iota(jnp.int32, (8, 192), 1)
        hm = ((col >> 6) == lax.broadcasted_iota(jnp.int32, (8, 192), 0)).astype(f32)
        delta[...] = dotf(hm, prod, NT, lax.Precision.HIGHEST)
        dqa[...] = jnp.zeros_like(dqa)

    dq = jnp.zeros((T, 256), f32)
    for kv_ref, out_ref in ((ka_ref, dka_ref), (kb_ref, dkb_ref)):
        kw = kv_ref[:, :256]
        vw = kv_ref[:, 128:384]
        dk = jnp.zeros(kw.shape, f32)
        dv = jnp.zeros(kw.shape, f32)
        for h in range(heads):
            sel = (lane >> 6) == h
            qm = jnp.where(sel, q_ref[...], jnp.zeros((), bf))
            dam = jnp.where((lane >> 6) == h + 1, daw[...], jnp.zeros((), bf))
            p = jnp.exp(dotf(kw, qm, NT) - lse_ref[h : h + 1, :])
            dv = dv + dotf(p.astype(bf), dam, NN)
            ds = (p * (dotf(vw, dam, NT) - delta[h : h + 1, :])).astype(bf)
            dk = dk + dotf(ds, qm, NN)
            dq = dq + dotf(ds, jnp.where(sel, kw, jnp.zeros((), bf)), TN)
        out_ref[...] = jnp.concatenate([dk[:, :192], dv[:, 64:256]], axis=1).astype(bf)
    dqa[...] += dq

    @pl.when(step == pl.num_programs(0) - 1)
    def _():
        dq_ref[...] = (dqa[...][:, :192] * DH**-0.5).astype(bf)


def attn_bwd(q, kv_a, kv_b, a, da, lse, bk=384, heads=3):
    T = q.shape[0]
    block = pl.BlockSpec((bk, 384), lambda i: (i, 0))
    return pl.pallas_call(
        functools.partial(attn_bwd_kernel, heads),
        grid=(T // bk,),
        in_specs=[full((T, 256)), block, block, full((T, 192)), full((T, 192)), full((8, T))],
        out_specs=[full((T, 192)), block, block],
        out_shape=[shape((T, 192)), shape((T, 384)), shape((T, 384))],
        scratch_shapes=[pltpu.VMEM((T, 256), bf), pltpu.VMEM((8, T), f32), pltpu.VMEM((T, 256), f32)],
        compiler_params=params(),
        cost_estimate=cost(32 * T * T * 256, 8 * T * 384, T * T * 6),
        name="attn_bwd",
    )(q, kv_a, kv_b, a, da, lse)


def adam_kernel(f_ref, g_ref, w_ref, m_ref, v_ref, *refs):
    og, ow, om, ov = refs[-4:]
    g = g_ref[0, 0].astype(f32)
    og[0, 0] = g
    factor = f_ref[pl.program_id(0), pl.program_id(1)]
    ow[0, 0], om[0, 0], ov[0, 0] = adam_update(w_ref[0, 0], m_ref[0, 0], v_ref[0, 0], g * factor, decay_rate)


def adam_segments(factor, grad, start, w, m, v, before=None):
    _, count, rows, cw = grad.shape
    here = pl.BlockSpec((1, 1, rows, cw), lambda s, i: (s, i + start, 0, 0))
    before = [] if before is None else list(before)
    return pl.pallas_call(
        adam_kernel,
        grid=(2, count),
        in_specs=[sm(), pl.BlockSpec((1, 1, rows, cw), lambda s, i: (s, i, 0, 0))]
        + [here] * 3
        + [pl.BlockSpec(memory_space=pl.ANY)] * len(before),
        out_specs=[here] * 4,
        out_shape=[shape(w.shape, f32)] * 4,
        input_output_aliases={5 + k: k for k in range(len(before))},
        compiler_params=params(),
        cost_estimate=cost(0, 60 * rows * cw * count),
        name="adam",
    )(factor, grad, w, m, v, *before)


def adam_one_kernel(f_ref, one_ref, o_ref, w_ref, m_ref, v_ref, *refs):
    og, ow, om, ov = refs[-4:]
    hw = w_ref.shape[3] // 2
    cat = lambda ref, k0, k1, lo: jnp.concatenate([ref[k0, :, lo : lo + hw], ref[k1, :, lo : lo + hw]], axis=1)

    def run(j, base, grads):
        for s in range(2):
            g = grads[s].astype(f32)
            og[s, j] = g
            ow[s, j], om[s, j], ov[s, j] = adam_update(
                w_ref[s, j], m_ref[s, j], v_ref[s, j], g * f_ref[s, base + j], decay_rate
            )

    @pl.when(pl.program_id(0) == 0)
    def _():
        run(0, 0, [cat(one_ref, 1, 4, s * hw) for s in range(2)])
        run(1, 0, [cat(one_ref, 2 * s, 3 + 2 * s, 0) for s in range(2)])

    @pl.when(pl.program_id(0) == 1)
    def _():
        run(0, 2, [cat(one_ref, 2 * s, 3 + 2 * s, hw) for s in range(2)])
        run(1, 2, [cat(o_ref, 0, 1, s * hw) for s in range(2)])


def adam_one(factor, one, o, w, m, v, before):
    _, _, rows, cw = w.shape
    here = pl.BlockSpec((2, 2, rows, cw), lambda i: (0, i + 3, 0, 0))
    return pl.pallas_call(
        adam_one_kernel,
        grid=(2,),
        in_specs=[sm(), full(one.shape), full(o.shape)] + [here] * 3 + [pl.BlockSpec(memory_space=pl.ANY)] * 4,
        out_specs=[here] * 4,
        out_shape=[shape(w.shape, f32)] * 4,
        input_output_aliases={6 + k: k for k in range(4)},
        compiler_params=params(),
        cost_estimate=cost(0, 32 * rows * cw * 8),
        name="adam_one",
    )(factor, one, o, w, m, v, *before)


def adam_mod_kernel(sc_ref, d_ref, f_ref, w_ref, m_ref, v_ref, *refs):
    og, ow, om, ov = refs[-4:]
    s, i = pl.program_id(0), pl.program_id(1)
    nseq = d_ref.shape[2]
    for j in range(2):
        g = sc_ref[:, 0:1] * d_ref[0, j, 0:1]
        for n in range(1, nseq):
            g = g + sc_ref[:, n : n + 1] * d_ref[0, j, n : n + 1]
        og[0, j] = g
        ow[0, j], om[0, j], ov[0, j] = adam_update(
            w_ref[0, j], m_ref[0, j], v_ref[0, j], g * f_ref[s, 2 * i + j], decay_rate
        )


def adam_mod(sc, dmod, factor, w, m, v, before):
    _, _, rows, cw = w.shape
    nseq = sc.shape[1]
    here = pl.BlockSpec((1, 2, rows, cw), lambda s, i: (s, i, 0, 0))
    return pl.pallas_call(
        adam_mod_kernel,
        grid=(2, 3),
        in_specs=[
            pl.BlockSpec((rows, nseq), lambda s, i: (0, 0)),
            pl.BlockSpec((1, 2, nseq, cw), lambda s, i: (s, i, 0, 0)),
            sm(),
        ]
        + [here] * 3
        + [pl.BlockSpec(memory_space=pl.ANY)] * 4,
        out_specs=[here] * 4,
        out_shape=[shape(w.shape, f32)] * 4,
        input_output_aliases={6 + k: k for k in range(4)},
        compiler_params=params(),
        cost_estimate=cost(0, 28 * rows * cw * 12),
        name="adam_mod",
    )(sc, dmod, factor, w, m, v, *before)


def make_shards(sizes):
    ns, nc, nt = sizes["shard"], sizes["ctx"], sizes["tensor"]
    owners = 2 * nt
    blocks = ns * nc
    hops = [("shard", 1)]
    hops += [("shard", 1 << b) for b in range(1, ns.bit_length() - 1)]
    hops += [("ctx", 1 << b) for b in range(nc.bit_length() - 1)]
    hops += [("tensor", 1 << b) for b in range(nt.bit_length() - 1)]

    def pp(x, axis, xor):
        return lax.ppermute(x, axis, [(i, i ^ xor) for i in range(sizes[axis])])

    def swap(x, axis):
        return lax.all_to_all(x, axis, 0, 0, tiled=True)

    def all_sum(x):
        for axis, xor in hops:
            x = x + pp(x, axis, xor)
        return x

    def after(x, *deps):
        return lax.optimization_barrier((x,) + deps)[0]

    def dyn(x, i, axis=0):
        return lax.dynamic_index_in_dim(x, i, axis, keepdims=False)

    def shards(
        image_rows,
        text_rows,
        condition,
        slot_table,
        weights,
        mom_one,
        mom_two,
        biases,
        bias_one,
        bias_two,
        image_cot,
        text_cot,
    ):
        hp = lax.Precision.HIGHEST
        nseq, D = condition.shape
        img = image_rows.shape[1]
        txt = text_rows.shape[1]
        ct = -(-txt // (owners * 16)) * 16
        ci = img // owners
        tpad = ct * owners
        T = img + tpad
        live_rows = img + txt
        cw = weights.shape[3]
        hw = cw // 2
        rows = weights.shape[1]
        shard_i, ctx_i, z = (lax.axis_index(a) for a in ("shard", "ctx", "tensor"))
        core = shard_i % 2
        first = core == 0
        me = shard_i * nc + ctx_i
        own = core * nt + z
        i32 = jnp.int32
        core_arr = core.reshape(1).astype(i32)
        own_arr = own.reshape(1).astype(i32)
        wt, m1, m2 = (jnp.moveaxis(x, 2, 1) for x in (weights, mom_one, mom_two))

        everyone = ("shard", "ctx")

        def gather(w):
            return lax.all_gather(w, everyone, axis=1, tiled=True)

        one_mine, o_mine = prep_one(wt)
        w_one = gather(one_mine)
        silu_all = jax.nn.silu(condition).astype(bf)
        sc_rows = lax.dynamic_slice_in_dim(silu_all, me * rows, rows, 1)
        mod = mod_partial(after(sc_rows, one_mine), wt)

        fixed = nseq == 2

        def pair(x):
            other = pp(x, "shard", 1)
            even = jnp.where(first, x, other)
            return [even] if fixed else [even, jnp.where(first, other, x)]

        tables = [t[0] for t in pair(slot_table)]
        lives = [(t >= 0).astype(f32) for t in tables]
        pickers = [(t == jnp.arange(nseq, dtype=i32)).astype(f32) for t in tables]
        pad_txt = lambda x: jnp.pad(x, ((0, tpad - txt), (0, 0)))
        x_img = [x[0] for x in pair(image_rows)]
        x_txt = [pad_txt(x[0]) for x in pair(text_rows)]
        mod = mod + pp(mod, "shard", 1)
        others = [r for r in range(1, blocks) if not r & nc]
        mod = sum(
            [lax.ppermute(mod, everyone, [(i, i ^ r) for i in range(blocks)]) for r in others], mod
        )
        mod = jnp.stack([mod] + [pp(mod, "tensor", k) for k in range(1, nt)])
        mod = jnp.concatenate([dyn(mod, z ^ k) for k in range(nt)], axis=-1)
        mods = [
            (jnp.einsum("n,sjne->sje", p, mod, precision=hp) + biases[:, :6]).reshape(12, D)
            for p in pickers
        ]
        col = z * cw
        bias_half = lax.dynamic_slice_in_dim(biases, col + core * hw, hw, 2)
        bias_cols = lax.dynamic_slice_in_dim(biases, col, cw, 2)
        bq = bias_half[:, 6]
        bkv = jnp.concatenate([jnp.zeros((2, hw), f32), bias_half[:, 7]], axis=1)
        b_up = lax.dynamic_slice_in_dim(bias_cols, 9 + 2 * core, 2, 1).reshape(4, cw)
        b_flat = biases.reshape(28, D)

        c_img = [(x[0] * l.astype(bf)) for x, l in zip(pair(image_cot), lives)]
        c_txt = [pad_txt(x[0] * l.astype(bf)) for x, l in zip(pair(text_cot), lives)]
        w_o = gather(after(o_mine, *mods))
        w_one = after(w_one, *mods, *x_img, *c_img)

        slots = range(len(tables))
        his, hts, nis, nts, qs, kvs, kv_gots = [], [], [], [], [], [], []
        for n in slots:
            hi, ht, ni, nt_, q, kv = qkv(core_arr, x_img[n], x_txt[n], txt, mods[n], bq, bkv, w_one)
            his.append(hi)
            hts.append(ht)
            nis.append(ni)
            nts.append(nt_)
            qs.append(q)
            kvs.append(kv)
            kv_gots.append(pp(kv, "ctx", 1))
        w_mlp = gather(after(wt[:, 10:18].astype(bf).reshape(16, rows, cw), kv_gots[-1]))

        def fold(send, keep):
            return (keep.astype(f32) + pp(send, "shard", 1).astype(f32)).astype(bf)

        def own_call(kernel, name, n, tokens, wholes, outs, deps=()):
            return row_call(functools.partial(kernel, ci), name, own_arr, ci, ct, D, tokens, wholes, outs, deps)

        chunk = ci + ct
        copies = shape((nt, chunk, D))
        attns, lses, o_parts = [], [], []
        for n in slots:
            a, lse = attn_fwd(qs[n], kvs[n], kv_gots[n], img, live_rows)
            attns.append(a)
            lses.append(lse)
            o_parts.append(swap(fold(*oproj(core_arr, a, w_o, nt, img)), "tensor"))

        mlp_all = zeros(after(core_arr, lses[-1]), 16, D, cw).reshape(2, 2, 2, 2, D, cw)
        dyis, dyts, gs, dus, up_sums, dh_parts, h2is, h2ts, o_sums = [], [], [], [], [], [], [], [], []
        for n in slots:
            h2, o_sum = own_call(
                after_attn_kernel,
                "after_attn",
                n,
                [(x_img[n], x_txt[n])],
                [mods[n], b_flat, after(o_parts[n], mlp_all)],
                [copies, shape((chunk, D), f32)],
            )
            o_sums.append(o_sum)
            dyi, dyt, *dg = grad_gate(core_arr, after(c_img[n], o_sum), c_txt[n], mods[n], w_mlp)
            mine = after(swap(h2, "tensor"), dyi)
            h2i, h2t, gi, gt, dui, dut, send, keep, up_sum = mlp(
                core_arr, mine, pp(mine, "shard", 1), *dg, w_mlp, b_up
            )
            dyis.append(dyi)
            dyts.append(dyt)
            h2is.append(h2i)
            h2ts.append(h2t)
            gs.append((gi, gt))
            dus.append((dui, dut))
            up_sums.append(up_sum)
            tie = fold(send, keep)
            dh_parts.append(swap(tie, "tensor"))

        def outer_sum(pairs):
            t = None
            for a, b in pairs:
                g = dotf(a, b, TN)
                t = g if t is None else t + g
            return t.astype(bf)

        def scatter(grads):
            return lax.psum_scatter(grads, everyone, scatter_dimension=1, tiled=True)

        def put(into, g, *at):
            return lax.dynamic_update_slice(into, g.reshape((1,) * len(at) + g.shape), at + (0, 0))

        for s, h2 in enumerate((h2is, h2ts)):
            for j in range(2):
                g = outer_sum([(h2[n], after(dus[n][s], tie)[j]) for n in slots])
                mlp_all = put(mlp_all, g, s, 0, core, j)
        for s, dy in enumerate((dyis, dyts)):
            for j in range(2):
                g = outer_sum([(dy[n], after(gs[n][s], tie)[j]) for n in slots])
                mlp_all = put(mlp_all, g, s, 1, core, j)
        mlp_sum = scatter(mlp_all.reshape(16, D, cw))
        do_owns, dxs, mid_sums = [], [], []
        for n in slots:
            do_own, dx, sums = own_call(
                after_mlp_kernel,
                "after_mlp",
                n,
                [(x_img[n], x_txt[n]), (c_img[n], c_txt[n])],
                [mods[n], o_sums[n], dh_parts[n]],
                [copies, shape((chunk, D), f32), shape((16, D), f32)],
                deps=[mlp_all],
            )
            dxs.append(dx)
            mid_sums.append(sums)
            do_owns.append(do_own)
        tie = do_owns[-1]
        y_halves = [fold(*down(core_arr, *(after(g, tie) for g in gs[n]), w_mlp, nt)) for n in slots]
        dois, dots, dqs, dkv_own, dkv_gots, out_owns, low_sums = [], [], [], [], [], [], []
        for n in slots:
            mine = after(swap(do_owns[n], "tensor"), y_halves[n])
            y_part = swap(after(y_halves[n], mine), "tensor")
            doi, dot, da = grad_attn(core_arr, mine, pp(mine, "shard", 1), w_o, img, tpad)
            dois.append(doi)
            dots.append(dot)
            dq, dkv_a, dkv_b = attn_bwd(qs[n], kvs[n], kv_gots[n], attns[n], da, lses[n])
            dqs.append(dq)
            dkv_own.append(dkv_a)
            dkv_gots.append(pp(after(dkv_b, y_part), "ctx", 1))
            out_own, sums = own_call(
                after_down_kernel,
                "after_down",
                n,
                [(x_img[n], x_txt[n]), (c_img[n], c_txt[n])],
                [mods[n], b_flat, lives[n].reshape(1, 1), o_sums[n], after(y_part, dq)],
                [copies, shape((16, D), f32)],
            )
            low_sums.append(sums)
            out_owns.append(swap(out_own, "tensor"))
        tie = dqs[-1]
        o_grads = [
            outer_sum([(after(dois[n], tie), attns[n][:img]) for n in slots]),
            outer_sum([(after(dots[n], tie), attns[n][img:]) for n in slots]),
        ]
        cat = lambda a, b: jnp.concatenate([a, b], axis=1)
        o_all = put(jnp.zeros((2, D, cw), bf), cat(*o_grads), core)
        o_rows = scatter(o_all)
        clip = lambda sq: jnp.minimum(1.0, clip_unit * D / jnp.sqrt(sq + clip_eps))

        def pad_row(x):
            x = x.reshape(1, -1)
            return jnp.pad(x, ((0, 0), (0, -x.shape[1] % 128)))

        mlp_sq = jnp.sum(jnp.sum(jnp.square(mlp_sum.astype(f32)), axis=1), axis=1)
        mlp_sq = all_sum(pad_row(mlp_sq))
        d_parts, dkv_img, dkv_txt, qv_sums, end_sums = [], [], [], [], []
        for n in slots:
            send, keep, kvi, kvt, qv, sums = grad_in(
                core_arr, [out_owns[n], mlp_sq], dqs[n], dkv_own[n], dkv_gots[n], nis[n], nts[n], w_one, nt, txt
            )
            dkv_img.append(kvi)
            dkv_txt.append(kvt)
            qv_sums.append(qv)
            end_sums.append(sums)
            tie = fold(send, keep)
            d_parts.append(swap(tie, "tensor"))
        q_grads, one_all = [], jnp.zeros((2, 3, D, cw), bf)
        for s, (part, left, right) in enumerate(((slice(0, img), his, dkv_img), (slice(img, T), hts, dkv_txt))):
            q_grads.append(outer_sum([(left[n], after(dqs[n], tie)[part]) for n in slots]))
            one_all = put(one_all, outer_sum([(left[n], right[n]) for n in slots]), core, 2 * s)
        one_all = put(one_all, cat(*q_grads), core, 1)
        one_rows = scatter(one_all.reshape(6, D, cw))

        place_arr = jnp.stack([z, core]).astype(i32)
        packed = all_sum(
            sum(
                pack_sums(pickers[n], place_arr, mid_sums[n], low_sums[n], end_sums[n], up_sums[n], qv_sums[n])
                for n in slots
            )
        )
        grad_owns = []
        for n in slots:
            (g,) = row_call(
                functools.partial(after_back_kernel, ci),
                "after_back",
                own_arr,
                ci,
                ct,
                D,
                [(x_img[n], x_txt[n])],
                [mods[n], dxs[n], d_parts[n]],
                [copies],
                deps=[one_all, packed],
            )
            grad_owns.append(swap(g, "tensor"))
        state = adam_segments(
            clip(mlp_sq[0, :16].reshape(2, 8)), mlp_sum.reshape(2, 8, rows, cw), 10, wt, m1, m2
        )
        e = nseq * 12
        dmod = packed[:e].reshape(nseq, 2, 6, D)
        od = packed[e : e + 4].reshape(2, 2, D)
        up_rows = packed[e + 4 : e + 12].reshape(2, 4, D)
        qv = packed[e + 12 : e + 16].reshape(2, 2, D)
        bias_grad = jnp.concatenate(
            [jnp.sum(dmod, axis=0), qv, od[:, :1], up_rows, od[:, 1:]], axis=1
        )
        wide = silu_all.astype(f32)
        gram_a = jnp.einsum("ni,mi->nm", wide, wide, precision=hp)
        gram_b = jnp.einsum("nsje,msje->sjnm", dmod, dmod, precision=hp)
        mod_sq = jnp.maximum(jnp.sum(gram_b * gram_a, axis=(2, 3)), 0.0)
        mod_cols = lax.dynamic_slice_in_dim(dmod, col, cw, 3)
        mod_cols = jnp.transpose(mod_cols, (1, 2, 0, 3))
        sc_wide = sc_rows.astype(f32)
        cond_rows = jnp.einsum("sjne,sjie->ni", mod_cols, wt[:, :6].astype(bf).astype(f32), precision=hp)
        cond_part = lax.dynamic_update_slice_in_dim(jnp.zeros((nseq, D), f32), cond_rows, me * rows, 1)

        def hsum(x, n):
            t = jnp.sum(jnp.square(x.astype(f32)), axis=1)
            t = t[:n] + t[n:]
            return jnp.stack([jnp.sum(t[:, :hw], axis=1), jnp.sum(t[:, hw:], axis=1)], axis=1)

        one_sq, o_sq = hsum(one_rows, 3), hsum(o_rows, 1)
        one_sq = jnp.stack(
            [jnp.stack([one_sq[1, s], one_sq[2 * s, 0], one_sq[2 * s, 1], o_sq[0, s]]) for s in range(2)]
        )
        tail = jnp.concatenate([cond_part.reshape(-1), one_sq.reshape(-1)])
        state = adam_mod(jnp.transpose(sc_wide), mod_cols, clip(mod_sq), wt, m1, m2, state)
        mod_state = state[0]
        tail = all_sum(tail)
        cond_grad = tail[: nseq * D].reshape(nseq, D) * silu_slope(condition)
        one_sq = tail[nseq * D :].reshape(2, 4)
        state = adam_one(clip(one_sq), one_rows, o_rows, wt, m1, m2, state)
        weight_grad, new_w, new_one, new_two = (jnp.moveaxis(x, 1, 2) for x in state)

        bias_sq = jnp.sum(bias_grad * bias_grad, axis=2)
        bias_factor = jnp.minimum(1.0, clip_unit * D**0.5 / jnp.sqrt(bias_sq + clip_eps))
        new_b, new_b1, new_b2 = adam_update(
            biases, bias_one, bias_two, bias_grad * bias_factor[:, :, None], 0.0
        )

        def finish(mine, deps=()):
            flag = first.astype(i32).reshape(1) if fixed else jnp.ones((1,), i32)
            done = [join_tokens(core_arr, flag, x, pp(x, "shard", 1), img, tpad, deps) for x in mine]
            return done[0] if fixed else [jnp.where(first, a, b) for a, b in zip(*done)]

        out_img, out_txt = finish(out_owns)
        grad_img, grad_txt = finish(grad_owns, [mod_state])
        return (
            out_img[None],
            out_txt[None, :txt],
            grad_img[None],
            grad_txt[None, :txt],
            cond_grad,
            weight_grad,
            new_w,
            new_one,
            new_two,
            bias_grad,
            new_b,
            new_b1,
            new_b2,
        )

    return shards


def solution(mesh):
    sizes = dict(mesh.shape)
    rows = P("shard", "ctx", None)
    mat = P(None, ("shard", "ctx"), None, "tensor")
    return jax.shard_map(
        make_shards(sizes),
        mesh=mesh,
        in_specs=(rows, rows, P(), P("shard"), mat, mat, mat, P(), P(), P(), rows, rows),
        out_specs=(rows, rows, rows, rows, P(), mat, mat, mat, mat, P(), P(), P(), P()),
        check_vma=False,
    )
```

```python
import functools
import jax
import jax.numpy as jnp
from jax import lax
from jax.experimental import pallas as pl
from jax.experimental.pallas import tpu as pltpu
from jax.sharding import PartitionSpec as P

DH = 64
NT = (((1,), (1,)), ((), ()))
TN = (((0,), (0,)), ((), ()))
NN = (((1,), (0,)), ((), ()))
bf = jnp.bfloat16
f32 = jnp.float32

beta_one = 0.9
beta_two = 0.95
learn_rate = 0.1
decay_rate = 0.1
adam_eps = 1e-08
adam_step = 10.0
norm_eps = 1e-06
gelu_coef = 0.044715
root_two_pi = 0.7978845608028654
clip_unit = 0.0001
clip_eps = 1e-12


def norm_back(normed, inverse, upstream):
    mean_grad = jnp.mean(upstream, axis=-1, keepdims=True)
    mean_dot = jnp.mean(upstream * normed, axis=-1, keepdims=True)
    return inverse * (upstream - mean_grad - normed * mean_dot)


def gelu_parts(preact):
    inner = root_two_pi * (preact + gelu_coef * preact * preact * preact)
    tanh_value = jnp.tanh(inner)
    value_out = 0.5 * preact * (1.0 + tanh_value)
    slope_out = 0.5 * (1.0 + tanh_value) + 0.5 * preact * (
        1.0 - tanh_value * tanh_value
    ) * root_two_pi * (1.0 + 3.0 * gelu_coef * preact * preact)
    return (value_out, slope_out)


def silu_slope(drawn_values):
    sigmoid_val = jax.nn.sigmoid(drawn_values)
    return sigmoid_val * (1.0 + drawn_values * (1.0 - sigmoid_val))


def adam_update(parameter, moment_one, moment_two, gradient, decay_factor):
    new_one = beta_one * moment_one + (1.0 - beta_one) * gradient
    new_two = beta_two * moment_two + (1.0 - beta_two) * gradient * gradient
    first_hat = new_one / (1.0 - beta_one**adam_step)
    second_hat = new_two / (1.0 - beta_two**adam_step)
    new_param = parameter - learn_rate * (
        first_hat / (jnp.sqrt(second_hat) + adam_eps) + decay_factor * parameter
    )
    return (new_param, new_one, new_two)


def dotf(a, b, dims, precision=None):
    return lax.dot_general(a, b, dims, preferred_element_type=f32, precision=precision)


def vm():
    return pl.BlockSpec(memory_space=pltpu.VMEM)


def sm():
    return pl.BlockSpec(memory_space=pltpu.SMEM)


def shape(dims, dtype=bf):
    return jax.ShapeDtypeStruct(dims, dtype)


def params(mib=58):
    return pltpu.CompilerParams(vmem_limit_bytes=mib * 2**20)


def cost(flops, nbytes, trans=0):
    return pl.CostEstimate(flops=1024, bytes_accessed=1024, transcendentals=0)


def full(dims):
    return pl.BlockSpec(dims, lambda *_: (0,) * len(dims), pipeline_mode=pl.Buffered(1))


def prep_kernel(a_ref, b_ref, one_ref, o_ref):
    hw = a_ref.shape[3] // 2
    cat = lambda x, y: jnp.concatenate([x, y], axis=-1)
    q, k = ([a_ref[s, j].astype(bf) for s in range(2)] for j in range(2))
    v, o = ([b_ref[s, j].astype(bf) for s in range(2)] for j in range(2))
    for c in range(2):
        half = lambda w: w[:, c * hw : (c + 1) * hw]
        one_ref[3 * c] = cat(half(k[0]), half(v[0]))
        one_ref[3 * c + 1] = cat(half(q[0]), half(q[1]))
        one_ref[3 * c + 2] = cat(half(k[1]), half(v[1]))
        o_ref[c] = cat(half(o[0]), half(o[1]))


def prep_one(wt):
    _, _, rows, cw = wt.shape
    seg = lambda k: pl.BlockSpec((2, 2, rows, cw), lambda i: (0, k, 0, 0))
    outs = [shape((6, rows, cw)), shape((2, rows, cw))]
    return pl.pallas_call(
        prep_kernel,
        grid=(1,),
        in_specs=[seg(3), seg(4)],
        out_specs=[full(o.shape) for o in outs],
        out_shape=outs,
        compiler_params=params(),
        cost_estimate=cost(0, 0),
        name="prep_one",
    )(wt, wt)


def mod_kernel(sc_ref, w_ref, o_ref):
    for j in range(2):
        o_ref[0, j] = dotf(sc_ref[...], w_ref[0, j].astype(bf), NN)


def mod_partial(sc, wt):
    _, _, rows, cw = wt.shape
    n = sc.shape[0]
    return pl.pallas_call(
        mod_kernel,
        grid=(2, 3),
        in_specs=[
            pl.BlockSpec((n, rows), lambda s, i: (0, 0)),
            pl.BlockSpec((1, 2, rows, cw), lambda s, i: (s, i, 0, 0)),
        ],
        out_specs=pl.BlockSpec((1, 2, n, cw), lambda s, i: (s, i, 0, 0)),
        out_shape=shape((2, 6, n, cw), f32),
        compiler_params=params(),
        cost_estimate=cost(0, 0),
        name="mod_partial",
    )(sc, wt)


def normed_of(x):
    center = x - jnp.mean(x, axis=-1, keepdims=True)
    inverse = lax.rsqrt(jnp.mean(center * center, axis=-1, keepdims=True) + norm_eps)
    return center * inverse, inverse


def qkv_kernel(n_img, txt, hw, core_ref, xi_ref, xt_ref, mod_ref, bq_ref, bkv_ref, w_ref, hi_ref, ht_ref, ni_ref, nt_ref, q_ref, kv_ref):
    i = pl.program_id(0)
    rows = xi_ref.shape[0]

    def run(s, x, h_ref, n_ref, at, live):
        size = x.shape[0]
        n, _ = normed_of(x.astype(f32))
        n_ref[...] = n.astype(bf)
        h = (n * (1.0 + mod_ref[6 * s + 1 : 6 * s + 2]) + mod_ref[6 * s : 6 * s + 1]).astype(bf)
        h_ref[...] = h
        q = dotf(h, w_ref[1, :, hw * s : hw * (s + 1)], NN) + bq_ref[s : s + 1]
        q = (q.astype(bf).astype(f32) * DH**-0.5).astype(bf)
        q_ref[pl.ds(at, size)] = jnp.concatenate([q, jnp.zeros((size, 256 - hw), bf)], axis=1)
        kv = dotf(h, w_ref[2 * s], NN) + bkv_ref[s : s + 1]
        kv_ref[pl.ds(at, size)] = (kv if live is None else jnp.where(live, kv, 0.0)).astype(bf)

    @pl.when(i < n_img)
    def _():
        run(0, xi_ref[...], hi_ref, ni_ref, pl.multiple_of(i * rows, rows), None)

    @pl.when(i >= n_img)
    def _():
        live = lax.broadcasted_iota(jnp.int32, (xt_ref.shape[0], 1), 0) < txt
        run(1, xt_ref[...], ht_ref, nt_ref, n_img * rows, live)


def qkv(core, xi, xt, txt, mod, bq, bkv, w):
    img, D = xi.shape
    tpad = xt.shape[0]
    n_img = 2
    rows = img // n_img
    T = img + tpad
    hw, cw = bq.shape[1], w.shape[2]
    x_spec = pl.BlockSpec((rows, D), lambda i, c: (jnp.minimum(i, n_img - 1), 0))
    outs = [shape((img, D)), shape((tpad, D))] * 2 + [shape((T, 256)), shape((T, cw))]
    return pl.pallas_call(
        functools.partial(qkv_kernel, n_img, txt, hw),
        grid_spec=pltpu.PrefetchScalarGridSpec(
            num_scalar_prefetch=1,
            grid=(n_img + 1,),
            in_specs=[
                x_spec,
                full((tpad, D)),
                full(mod.shape),
                full(bq.shape),
                full(bkv.shape),
                pl.BlockSpec((3, D, cw), lambda i, c: (c[0], 0, 0), pipeline_mode=pl.Buffered(1)),
            ],
            out_specs=[x_spec, full((tpad, D))] * 2 + [full(o.shape) for o in outs[4:]],
        ),
        out_shape=outs,
        compiler_params=params(),
        cost_estimate=cost(2 * T * D * 3 * hw, 4 * T * D),
        name="qkv",
    )(core, xi, xt, mod, bq, bkv, w)


def store_chunks(core, send_ref, keep_ref, src, lo):
    nt = send_ref.shape[0]
    n = src.shape[0] // (2 * nt)
    for ref, c in ((send_ref, 1 - core), (keep_ref, core)):
        for t in range(nt):
            ref[t, lo : lo + n] = src[pl.ds(pl.multiple_of((c * nt + t) * n, n), n)].astype(bf)


def chunk_blocks(nt, chunk, width):
    return [pl.BlockSpec((nt, chunk, width), lambda i, c: (0, 0, i))] * 2


def oproj_kernel(img, core_ref, a_ref, w_ref, send_ref, keep_ref, acc):
    hw = a_ref.shape[1]
    acc[:img] = dotf(a_ref[:img], w_ref[0, :, :hw], NT)
    acc[img:] = dotf(a_ref[img:], w_ref[0, :, hw:], NT)
    store_chunks(core_ref[0], send_ref, keep_ref, acc.at[:img], 0)
    store_chunks(core_ref[0], send_ref, keep_ref, acc.at[img:], img // (2 * send_ref.shape[0]))


def oproj(core, a, w, nt, img):
    T, hw = a.shape
    _, D, cw = w.shape
    width = D // 3
    return pl.pallas_call(
        functools.partial(oproj_kernel, img),
        grid_spec=pltpu.PrefetchScalarGridSpec(
            num_scalar_prefetch=1,
            grid=(3,),
            in_specs=[full(a.shape), pl.BlockSpec((1, width, cw), lambda i, c: (c[0], i, 0))],
            out_specs=chunk_blocks(nt, T // (2 * nt), width),
            scratch_shapes=[pltpu.VMEM((T, width), f32)],
        ),
        out_shape=[shape((nt, T // (2 * nt), D))] * 2,
        compiler_params=params(),
        cost_estimate=cost(2 * T * D * hw, 2 * T * D),
        name="oproj",
    )(core, a, w)


def total(ref):
    t = ref[0].astype(f32)
    for k in range(1, ref.shape[0]):
        t = t + ref[k].astype(f32)
    return t


def store_copies(ref, rows, x):
    for k in range(ref.shape[0]):
        ref[k, rows] = x


def copy_kernel(x_ref, dep_ref, o_ref):
    o_ref[...] = x_ref[...]


def copy_after(x, dep):
    return pl.pallas_call(
        copy_kernel,
        in_specs=[vm(), pl.BlockSpec(memory_space=pl.ANY)],
        out_specs=vm(),
        out_shape=shape(x.shape),
        compiler_params=params(),
        cost_estimate=cost(0, 0),
        name="copy_after",
    )(x, dep)


def own_specs(ci, ct, D):
    return [
        pl.BlockSpec((ci, D), lambda i, o: (o[0], 0)),
        pl.BlockSpec((ct, D), lambda i, o: (o[0], 0)),
    ]


def whole(dims):
    return pl.BlockSpec(dims, lambda i, o: (0,) * len(dims))


def row_call(kernel, name, own, ci, ct, D, tokens, wholes, outs, deps=()):
    specs = [s for _ in tokens for s in own_specs(ci, ct, D)] + [whole(w.shape) for w in wholes]
    flat = [x for pair in tokens for x in pair]
    n_in = 1 + len(specs)
    return pl.pallas_call(
        lambda *refs: kernel(*refs[:n_in], *refs[n_in + len(deps) :]),
        grid_spec=pltpu.PrefetchScalarGridSpec(
            num_scalar_prefetch=1,
            grid=(1,),
            in_specs=specs + [pl.BlockSpec(memory_space=pl.ANY)] * len(deps),
            out_specs=[whole(o.shape) for o in outs],
        ),
        out_shape=outs,
        compiler_params=params(),
        cost_estimate=cost(0, 0),
        name=name,
    )(own, *flat, *wholes, *deps)


def after_attn_kernel(ci, own_ref, xi_ref, xt_ref, mod_ref, b_ref, part_ref, h_ref, o_ref):
    sums = total(part_ref)
    for s, x_ref in enumerate((xi_ref, xt_ref)):
        rows = slice(0, ci) if s == 0 else slice(ci, sums.shape[0])
        m = lambda j: mod_ref[6 * s + j : 6 * s + j + 1]
        o = sums[rows] + b_ref[14 * s + 8 : 14 * s + 9]
        n, _ = normed_of(x_ref[...].astype(f32) + m(2) * o)
        store_copies(h_ref, rows, (n * (1.0 + m(4)) + m(3)).astype(bf))
        o_ref[rows] = o


def colsum(x):
    return jnp.sum(x, axis=0, keepdims=True)


def after_mlp_kernel(ci, own_ref, xi_ref, xt_ref, ci_ref, ct_ref, mod_ref, o_ref, part_ref, do_ref, dx_ref, sum_ref):
    sums = total(part_ref)
    for s, (x_ref, c_ref) in enumerate(((xi_ref, ci_ref), (xt_ref, ct_ref))):
        rows = slice(0, ci) if s == 0 else slice(ci, sums.shape[0])
        m = lambda j: mod_ref[6 * s + j : 6 * s + j + 1]
        o = o_ref[rows]
        n, inv = normed_of(x_ref[...].astype(f32) + m(2) * o)
        dh = sums[rows]
        cot = c_ref[...].astype(f32)
        dx = cot + norm_back(n, inv, dh * (1.0 + m(4)))
        do = dx * m(2)
        store_copies(do_ref, rows, do.astype(bf))
        dx_ref[rows] = dx
        rows_out = [colsum(dx * o), colsum(dh), colsum(dh * n), colsum(do), colsum(cot * m(5))]
        sum_ref[8 * s : 8 * s + 8] = jnp.concatenate(rows_out + [jnp.zeros((3, dx.shape[1]), f32)], axis=0)


def after_down_kernel(
    ci, own_ref, xi_ref, xt_ref, ci_ref, ct_ref, mod_ref, b_ref, live_ref, o_ref, part_ref, out_ref, sum_ref
):
    sums = total(part_ref)
    for s, (x_ref, c_ref) in enumerate(((xi_ref, ci_ref), (xt_ref, ct_ref))):
        rows = slice(0, ci) if s == 0 else slice(ci, sums.shape[0])
        m = lambda j: mod_ref[6 * s + j : 6 * s + j + 1]
        y = sums[rows] + b_ref[14 * s + 13 : 14 * s + 14]
        x1 = x_ref[...].astype(f32) + m(2) * o_ref[rows]
        store_copies(out_ref, rows, ((x1 + m(5) * y) * live_ref[...]).astype(bf))
        top = colsum(c_ref[...].astype(f32) * y)
        sum_ref[8 * s : 8 * s + 8] = jnp.concatenate([top, jnp.zeros((7, y.shape[1]), f32)], axis=0)


def after_back_kernel(ci, own_ref, xi_ref, xt_ref, mod_ref, dx_ref, part_ref, g_ref):
    sums = total(part_ref)
    for s, x_ref in enumerate((xi_ref, xt_ref)):
        rows = slice(0, ci) if s == 0 else slice(ci, sums.shape[0])
        n, inv = normed_of(x_ref[...].astype(f32))
        dh = sums[rows]
        g = dx_ref[rows] + norm_back(n, inv, dh * (1.0 + mod_ref[6 * s + 1 : 6 * s + 2]))
        store_copies(g_ref, rows, g.astype(bf))


def stream_blocks(img, tpad, width):
    return [
        pl.BlockSpec((1, img, width), lambda k, c: (jnp.minimum(k, 1), 0, 0)),
        pl.BlockSpec((1, tpad, width), lambda k, c: (jnp.maximum(k - 2, 0), 0, 0)),
    ]


def seg_call(kernel, name, core, ins, in_specs, outs, out_specs, scratch=(), est=None):
    return pl.pallas_call(
        kernel,
        grid_spec=pltpu.PrefetchScalarGridSpec(
            num_scalar_prefetch=1,
            grid=(4,),
            in_specs=in_specs,
            out_specs=out_specs,
            scratch_shapes=list(scratch),
        ),
        out_shape=outs,
        compiler_params=params(),
        cost_estimate=est or cost(0, 0),
        name=name,
    )(core, *ins)


def zeros_kernel(core_ref, *outs):
    for o in outs:
        o[...] = jnp.zeros_like(o)


def zeros(core, counts, D, cw):
    n = 8
    height = lambda c: c * D // n
    flat = pl.pallas_call(
        zeros_kernel,
        grid=(n,),
        in_specs=[sm()],
        out_specs=[pl.BlockSpec((height(c), cw), lambda i: (i, 0)) for c in counts],
        out_shape=[shape((c * D, cw)) for c in counts],
        compiler_params=params(),
        cost_estimate=cost(0, 0),
        name="zeros",
    )(core)
    return [x.reshape(-1, D, cw) for x in flat]


def seg_of(base):
    return lambda k, c: ((k // 2) * 8 + base + 2 * c[0] + lax.rem(k, 2), 0, 0)


def grad_gate_kernel(core_ref, ci_ref, ct_ref, mod_ref, w_ref, dyi_ref, dyt_ref, dgi_ref, dgt_ref):
    k = pl.program_id(0)
    for s, (c, dy, dg) in enumerate(((ci_ref, dyi_ref, dgi_ref), (ct_ref, dyt_ref, dgt_ref))):

        @pl.when(k == 2 * s)
        def _():
            dy[...] = (c[...].astype(f32) * mod_ref[6 * s + 5 : 6 * s + 6]).astype(bf)

        @pl.when(jnp.right_shift(k, 1) == s)
        def _():
            dg[0] = dotf(dy[...], w_ref[0], NN)


def grad_gate(core, cot_i, cot_t, mod, w):
    img, D = cot_i.shape
    tpad = cot_t.shape[0]
    T = img + tpad
    cw = w.shape[2]
    return seg_call(
        grad_gate_kernel,
        "grad_gate",
        core,
        [cot_i, cot_t, mod, w],
        [full(cot_i.shape), full(cot_t.shape), full(mod.shape), pl.BlockSpec((1, D, cw), seg_of(4))],
        [shape((img, D)), shape((tpad, D)), shape((2, img, cw), f32), shape((2, tpad, cw), f32)],
        [full(cot_i.shape), full(cot_t.shape)] + stream_blocks(img, tpad, cw),
        est=cost(4 * T * D * cw, 4 * T * D),
    )


def place_chunks(core, mine, other, img_ref, txt_ref):
    nt = mine.shape[0]
    ci, ct = img_ref.shape[0] // (2 * nt), txt_ref.shape[0] // (2 * nt)
    for ref, c in ((mine, core), (other, 1 - core)):
        for t in range(nt):
            o = c * nt + t
            img_ref[pl.ds(pl.multiple_of(o * ci, ci), ci)] = ref[t, :ci]
            txt_ref[pl.ds(pl.multiple_of(o * ct, ct), ct)] = ref[t, ci:]


def mlp_kernel(core_ref, mine, other, dgi, dgt, w_ref, b_ref, hi, ht, gi, gt, dui, dut, send_ref, keep_ref, bias_ref, acc_i, acc_t):
    k = pl.program_id(0)

    @pl.when(k == 0)
    def _():
        place_chunks(core_ref[0], mine, other, hi, ht)
        bias_ref[...] = jnp.zeros_like(bias_ref)

    lo = 0
    for s, (h, dg, g, du_ref, acc) in enumerate(((hi, dgi, gi, dui, acc_i), (ht, dgt, gt, dut, acc_t))):

        @pl.when(jnp.right_shift(k, 1) == s)
        def _():
            size = min(256, h.shape[0])
            sums = None
            for r in range(0, h.shape[0], size):
                at = slice(r, r + size)
                u = dotf(h[at], w_ref[0], NN) + b_ref[pl.ds(k, 1)]
                val, slope = gelu_parts(u)
                g[0, at] = val.astype(bf)
                du = dg[0, at] * slope
                du_b = du.astype(bf)
                du_ref[0, at] = du_b
                sums = colsum(du) if sums is None else sums + colsum(du)
                acc[at] = jnp.where(k == 2 * s, 0.0, acc[at]) + dotf(du_b, w_ref[0], NT)

            bias_ref[pl.ds(k, 1)] = sums

            @pl.when(k == 2 * s + 1)
            def _():
                store_chunks(core_ref[0], send_ref, keep_ref, acc, lo)

        lo += acc.shape[0] // (2 * send_ref.shape[0])


def mlp(core, mine, other, dgi, dgt, w, b):
    nt, chunk, D = mine.shape
    img, tpad, cw = dgi.shape[1], dgt.shape[1], w.shape[2]
    T = img + tpad
    blocks = stream_blocks(img, tpad, cw)
    whole_outs = [shape((img, D)), shape((tpad, D))]
    ends = [shape((nt, chunk, D)), shape((nt, chunk, D)), shape((8, cw), f32)]
    return seg_call(
        mlp_kernel,
        "mlp",
        core,
        [mine, other, dgi, dgt, w, b],
        [full(mine.shape)] * 2 + blocks + [pl.BlockSpec((1, D, cw), seg_of(0)), full(b.shape)],
        whole_outs + [shape((2, img, cw)), shape((2, tpad, cw))] * 2 + ends,
        [full(o.shape) for o in whole_outs] + blocks + blocks + [full(o.shape) for o in ends],
        [pltpu.VMEM((img, D), f32), pltpu.VMEM((tpad, D), f32)],
        cost(8 * T * D * cw, 4 * T * D, 2 * T * cw),
    )


def down_kernel(core_ref, gi, gt, w_ref, send_ref, keep_ref, acc_i, acc_t):
    k = pl.program_id(0)
    lo = 0
    for s, (g, acc) in enumerate(((gi, acc_i), (gt, acc_t))):

        @pl.when(jnp.right_shift(k, 1) == s)
        def _():
            y = dotf(g[0], w_ref[0], NT)

            @pl.when(k == 2 * s)
            def _():
                acc[...] = y

            @pl.when(k == 2 * s + 1)
            def _():
                acc[...] += y
                store_chunks(core_ref[0], send_ref, keep_ref, acc, lo)

        lo += acc.shape[0] // (2 * send_ref.shape[0])


def down(core, gi, gt, w, nt):
    img, tpad = gi.shape[1], gt.shape[1]
    D, cw = w.shape[1:]
    T = img + tpad
    ends = [shape((nt, T // (2 * nt), D))] * 2
    return seg_call(
        down_kernel,
        "down",
        core,
        [gi, gt, w],
        stream_blocks(img, tpad, cw) + [pl.BlockSpec((1, D, cw), seg_of(4))],
        ends,
        [full(o.shape) for o in ends],
        [pltpu.VMEM((img, D), f32), pltpu.VMEM((tpad, D), f32)],
        cost(4 * T * D * cw, 2 * T * D),
    )


def grad_attn_kernel(core_ref, mine, other, w_ref, doi_ref, dot_ref, da_ref):
    img, hw = doi_ref.shape[0], da_ref.shape[1]
    place_chunks(core_ref[0], mine, other, doi_ref, dot_ref)
    da_ref[:img] = dotf(doi_ref[...], w_ref[0, :, :hw], NN).astype(bf)
    da_ref[img:] = dotf(dot_ref[...], w_ref[0, :, hw:], NN).astype(bf)


def grad_attn(core, mine, other, w, img, tpad):
    _, D, cw = w.shape
    hw = cw // 2
    T = img + tpad
    outs = [shape((img, D)), shape((tpad, D)), shape((T, hw))]
    return pl.pallas_call(
        grad_attn_kernel,
        grid_spec=pltpu.PrefetchScalarGridSpec(
            num_scalar_prefetch=1,
            grid=(1,),
            in_specs=[full(mine.shape)] * 2 + [pl.BlockSpec((1, D, cw), lambda i, c: (c[0], 0, 0))],
            out_specs=[full(o.shape) for o in outs],
        ),
        out_shape=outs,
        compiler_params=params(),
        cost_estimate=cost(2 * T * D * hw, 4 * T * D),
        name="grad_attn",
    )(core, mine, other, w)


def grad_in_kernel(
    img, txt, core_ref, dep_ref, dep_two_ref, q_ref, a_ref, b_ref, ni_ref, nt_ref, w_ref, send_ref, keep_ref, kvi_ref, kvt_ref, qv_ref, sum_ref, acc
):
    T, hw = q_ref.shape

    @pl.when(pl.program_id(0) == 0)
    def _():
        for s, (at, out) in enumerate(((slice(0, img), kvi_ref), (slice(img, T), kvt_ref))):
            kv = a_ref[at].astype(f32) + b_ref[at].astype(f32)
            if s == 1:
                kv = jnp.where(lax.broadcasted_iota(jnp.int32, (T - img, 1), 0) < txt, kv, 0.0)
            out[...] = kv.astype(bf)
            sums = jnp.concatenate([colsum(q_ref[at].astype(f32)), colsum(kv)[:, hw:]], axis=1)
            qv_ref[4 * s : 4 * s + 4] = jnp.broadcast_to(sums, (4, 2 * hw))

    acc[:img] = dotf(q_ref[:img], w_ref[1, :, :hw], NT) + dotf(kvi_ref[...], w_ref[0], NT)
    acc[img:] = dotf(q_ref[img:], w_ref[1, :, hw:], NT) + dotf(kvt_ref[...], w_ref[2], NT)
    rows = []
    for at, n_ref in ((slice(0, img), ni_ref), (slice(img, T), nt_ref)):
        rows += [colsum(acc[at]), colsum(acc[at] * n_ref[...].astype(f32))]
    sum_ref[...] = jnp.concatenate(rows + [jnp.zeros((4, acc.shape[1]), f32)], axis=0)
    store_chunks(core_ref[0], send_ref, keep_ref, acc.at[:img], 0)
    store_chunks(core_ref[0], send_ref, keep_ref, acc.at[img:], img // (2 * send_ref.shape[0]))


def grad_in(core, deps, dq, kv_a, kv_b, n_img, n_txt, w, nt, txt):
    T, hw = dq.shape
    img, tpad = n_img.shape[0], n_txt.shape[0]
    cw = kv_a.shape[1]
    D = w.shape[1]
    width = D // 3
    ends = [shape((img, cw)), shape((tpad, cw)), shape((8, cw), f32)]
    column = lambda n: pl.BlockSpec((n, width), lambda i, c: (0, i))
    return pl.pallas_call(
        functools.partial(grad_in_kernel, img, txt),
        grid_spec=pltpu.PrefetchScalarGridSpec(
            num_scalar_prefetch=1,
            grid=(3,),
            in_specs=[pl.BlockSpec(memory_space=pl.ANY)] * 2
            + [full(dq.shape), full(kv_a.shape), full(kv_b.shape), column(img), column(tpad)]
            + [pl.BlockSpec((3, width, cw), lambda i, c: (c[0], i, 0))],
            out_specs=chunk_blocks(nt, T // (2 * nt), width) + [full(o.shape) for o in ends] + [column(8)],
            scratch_shapes=[pltpu.VMEM((T, width), f32)],
        ),
        out_shape=[shape((nt, T // (2 * nt), D))] * 2 + ends + [shape((8, D), f32)],
        compiler_params=params(),
        cost_estimate=cost(2 * T * D * 3 * hw, 2 * T * D),
        name="grad_in",
    )(core, *deps, dq, kv_a, kv_b, n_img, n_txt, w)


def tokens_kernel(core_ref, flag_ref, mine, other, *refs):
    oi_ref, ot_ref = refs[-2:]
    on = flag_ref[0] != 0

    @pl.when(on)
    def _():
        place_chunks(core_ref[0], mine, other, oi_ref, ot_ref)

    @pl.when(jnp.logical_not(on))
    def _():
        oi_ref[...] = jnp.zeros_like(oi_ref)
        ot_ref[...] = jnp.zeros_like(ot_ref)


def join_tokens(core, flag, mine, other, img, tpad, deps=()):
    D = mine.shape[2]
    return pl.pallas_call(
        tokens_kernel,
        in_specs=[sm(), sm(), vm(), vm()] + [pl.BlockSpec(memory_space=pl.ANY)] * len(deps),
        out_specs=[vm()] * 2,
        out_shape=[shape((img, D)), shape((tpad, D))],
        compiler_params=params(),
        cost_estimate=cost(0, 4 * (img + tpad) * D),
        name="join_tokens",
    )(core, flag, mine, other, *deps)


def pack_kernel(picker_ref, place_ref, mid_ref, low_ref, end_ref, up_ref, qv_ref, sq_ref, out_ref):
    nseq = picker_ref.shape[0]
    z, core = place_ref[0], place_ref[1]
    D, cw = mid_ref.shape[1], up_ref.shape[1]
    hw = cw // 2
    out_ref[...] = jnp.zeros_like(out_ref)
    at = 12 * nseq + 16
    out_ref[at : at + 1, :128] = sq_ref[...]
    for s in range(2):
        rows = jnp.concatenate(
            [end_ref[2 * s : 2 * s + 2], mid_ref[8 * s : 8 * s + 3], low_ref[8 * s : 8 * s + 1]], axis=0
        )
        for n in range(nseq):
            out_ref[12 * n + 6 * s : 12 * n + 6 * s + 6] = rows * picker_ref[n]
        at = 12 * nseq
        out_ref[at + 2 * s : at + 2 * s + 2] = mid_ref[8 * s + 3 : 8 * s + 5]
        lane = lax.broadcasted_iota(jnp.int32, (1, D), 1)
        inside = jnp.logical_and(lane >= z * cw, lane < (z + 1) * cw)
        up = jnp.concatenate([up_ref[2 * s : 2 * s + 2]] * (D // cw), axis=1)
        up = jnp.where(inside, up, 0.0)
        none = jnp.zeros_like(up)
        first = core == 0
        up = jnp.concatenate([jnp.where(first, up, none), jnp.where(first, none, up)], axis=0)
        out_ref[at + 4 + 4 * s : at + 8 + 4 * s] = up
        row = qv_ref[4 * s : 4 * s + 1]
        start = z * cw + core * hw
        inside = jnp.logical_and(lane >= start, lane < start + hw)
        for k in range(2):
            part = row[:, k * hw : (k + 1) * hw]
            part = jnp.concatenate([part, part], axis=1)
            part = jnp.concatenate([part] * (D // cw), axis=1)
            out_ref[at + 12 + 2 * s + k : at + 13 + 2 * s + k] = jnp.where(inside, part, 0.0)


def pack_sums(picker, place, mid, low, end, up, qv, sq):
    D = mid.shape[1]
    rows = -(-(12 * picker.shape[0] + 17) // 8) * 8
    return pl.pallas_call(
        pack_kernel,
        in_specs=[sm(), sm()] + [vm()] * 6,
        out_specs=vm(),
        out_shape=shape((rows, D), f32),
        compiler_params=params(),
        cost_estimate=cost(0, 0),
        name="pack_sums",
    )(picker, place, mid, low, end, up, qv, sq)


def squares_kernel(x_ref, dep_ref, o_ref):
    for p in range(x_ref.shape[0]):
        x = x_ref[p].astype(f32)
        o_ref[p : p + 1] = colsum(x * x)


def column_squares(x, dep):
    n, _, cw = x.shape
    return pl.pallas_call(
        squares_kernel,
        in_specs=[vm(), pl.BlockSpec(memory_space=pl.ANY)],
        out_specs=vm(),
        out_shape=shape((n, cw), f32),
        compiler_params=params(),
        cost_estimate=cost(0, 0),
        name="column_squares",
    )(x, dep)


def attn_fwd_kernel(heads, img, live, q_ref, ka_ref, kb_ref, a_ref, lse_ref):
    T = ka_ref.shape[0]
    bq = q_ref.shape[0]
    lane = lax.broadcasted_iota(jnp.int32, (1, 256), 1)
    lane1 = lax.broadcasted_iota(jnp.int32, (1, 128), 1)
    keep = lax.broadcasted_iota(jnp.int32, (1, T - img), 1) < live - img
    q = q_ref[...]
    acc = jnp.zeros((bq, 256), f32)
    lse_tile = jnp.zeros((bq, 128), f32)
    for h in range(heads):
        qm = jnp.where((lane >> 6) == h, q, jnp.zeros_like(q))
        parts = []
        for kv in (ka_ref, kb_ref):
            parts.append((dotf(qm, kv[:img, :256], NT), kv, 0, img))
            s = dotf(qm, kv[img:, :256], NT)
            parts.append((jnp.where(keep, s, -1e30), kv, img, T))
        m = functools.reduce(jnp.maximum, [jnp.max(p[0], axis=1, keepdims=True) for p in parts])
        l = jnp.zeros((bq, 1), f32)
        pv = jnp.zeros((bq, 256), f32)
        for s, kv, lo, hi in parts:
            e = jnp.exp(s - m)
            l = l + jnp.sum(e, axis=1, keepdims=True)
            pv = pv + dotf(e.astype(bf), kv[lo:hi, 128:384], NN)
        acc = jnp.where((lane >> 6) == h + 1, pv / l, acc)
        lse_tile = jnp.where(lane1 == h, m + jnp.log(l), lse_tile)
    a_ref[...] = acc[:, 64:256].astype(bf)
    lse_ref[...] = lse_tile.T[:8]


def attn_fwd(q, kv_a, kv_b, img, live, bq=384, heads=3):
    T = q.shape[0]
    return pl.pallas_call(
        functools.partial(attn_fwd_kernel, heads, img, live),
        grid=(T // bq,),
        in_specs=[pl.BlockSpec((bq, 256), lambda i: (i, 0)), full((T, 384)), full((T, 384))],
        out_specs=[pl.BlockSpec((bq, 192), lambda i: (i, 0)), pl.BlockSpec((8, bq), lambda i: (0, i))],
        out_shape=[shape((T, 192)), shape((8, T), f32)],
        compiler_params=params(),
        cost_estimate=cost(16 * T * T * 256, 4 * T * 384, T * T * 6),
        name="attn_fwd",
    )(q, kv_a, kv_b)


def attn_bwd_kernel(heads, q_ref, ka_ref, kb_ref, a_ref, da_ref, lse_ref, dq_ref, dka_ref, dkb_ref, daw, delta, dqa):
    step = pl.program_id(0)
    T = q_ref.shape[0]
    lane = lax.broadcasted_iota(jnp.int32, (1, 256), 1)

    @pl.when(step == 0)
    def _():
        da = da_ref[...]
        daw[...] = jnp.concatenate([jnp.zeros((T, 64), bf), da], axis=1)
        prod = da.astype(f32) * a_ref[...].astype(f32)
        col = lax.broadcasted_iota(jnp.int32, (8, 192), 1)
        hm = ((col >> 6) == lax.broadcasted_iota(jnp.int32, (8, 192), 0)).astype(f32)
        delta[...] = dotf(hm, prod, NT, lax.Precision.HIGHEST)
        dqa[...] = jnp.zeros_like(dqa)

    dq = jnp.zeros((T, 256), f32)
    for kv_ref, out_ref in ((ka_ref, dka_ref), (kb_ref, dkb_ref)):
        kw = kv_ref[:, :256]
        vw = kv_ref[:, 128:384]
        dk = jnp.zeros(kw.shape, f32)
        dv = jnp.zeros(kw.shape, f32)
        for h in range(heads):
            sel = (lane >> 6) == h
            qm = jnp.where(sel, q_ref[...], jnp.zeros((), bf))
            dam = jnp.where((lane >> 6) == h + 1, daw[...], jnp.zeros((), bf))
            p = jnp.exp(dotf(kw, qm, NT) - lse_ref[h : h + 1, :])
            dv = dv + dotf(p.astype(bf), dam, NN)
            ds = (p * (dotf(vw, dam, NT) - delta[h : h + 1, :])).astype(bf)
            dk = dk + dotf(ds, qm, NN)
            dq = dq + dotf(ds, jnp.where(sel, kw, jnp.zeros((), bf)), TN)
        out_ref[...] = jnp.concatenate([dk[:, :192], dv[:, 64:256]], axis=1).astype(bf)
    dqa[...] += dq

    @pl.when(step == pl.num_programs(0) - 1)
    def _():
        dq_ref[...] = (dqa[...][:, :192] * DH**-0.5).astype(bf)


def attn_bwd(q, kv_a, kv_b, a, da, lse, bk=384, heads=3):
    T = q.shape[0]
    block = pl.BlockSpec((bk, 384), lambda i: (i, 0))
    return pl.pallas_call(
        functools.partial(attn_bwd_kernel, heads),
        grid=(T // bk,),
        in_specs=[full((T, 256)), block, block, full((T, 192)), full((T, 192)), full((8, T))],
        out_specs=[full((T, 192)), block, block],
        out_shape=[shape((T, 192)), shape((T, 384)), shape((T, 384))],
        scratch_shapes=[pltpu.VMEM((T, 256), bf), pltpu.VMEM((8, T), f32), pltpu.VMEM((T, 256), f32)],
        compiler_params=params(),
        cost_estimate=cost(32 * T * T * 256, 8 * T * 384, T * T * 6),
        name="attn_bwd",
    )(q, kv_a, kv_b, a, da, lse)


def adam_kernel(f_ref, g_ref, w_ref, m_ref, v_ref, *refs):
    og, ow, om, ov = refs[-4:]
    g = g_ref[0, 0].astype(f32)
    og[0, 0] = g
    factor = f_ref[pl.program_id(0), pl.program_id(1)]
    ow[0, 0], om[0, 0], ov[0, 0] = adam_update(w_ref[0, 0], m_ref[0, 0], v_ref[0, 0], g * factor, decay_rate)


def adam_segments(factor, grad, start, w, m, v, before=None):
    _, count, rows, cw = grad.shape
    here = pl.BlockSpec((1, 1, rows, cw), lambda s, i: (s, i + start, 0, 0))
    before = [] if before is None else list(before)
    return pl.pallas_call(
        adam_kernel,
        grid=(2, count),
        in_specs=[sm(), pl.BlockSpec((1, 1, rows, cw), lambda s, i: (s, i, 0, 0))]
        + [here] * 3
        + [pl.BlockSpec(memory_space=pl.ANY)] * len(before),
        out_specs=[here] * 4,
        out_shape=[shape(w.shape, f32)] * 4,
        input_output_aliases={5 + k: k for k in range(len(before))},
        compiler_params=params(),
        cost_estimate=cost(0, 60 * rows * cw * count),
        name="adam",
    )(factor, grad, w, m, v, *before)


def adam_one_kernel(f_ref, one_ref, w_ref, m_ref, v_ref, *refs):
    og, ow, om, ov = refs[-4:]
    hw = w_ref.shape[3] // 2
    cat = lambda ref, k0, k1, lo: jnp.concatenate([ref[k0, :, lo : lo + hw], ref[k1, :, lo : lo + hw]], axis=1)

    def run(j, base, grads):
        for s in range(2):
            g = grads[s].astype(f32)
            og[s, j] = g
            ow[s, j], om[s, j], ov[s, j] = adam_update(
                w_ref[s, j], m_ref[s, j], v_ref[s, j], g * f_ref[s, base + j], decay_rate
            )

    @pl.when(pl.program_id(0) == 0)
    def _():
        run(0, 0, [cat(one_ref, 1, 5, s * hw) for s in range(2)])
        run(1, 0, [cat(one_ref, 2 * s, 4 + 2 * s, 0) for s in range(2)])

    @pl.when(pl.program_id(0) == 1)
    def _():
        run(0, 2, [cat(one_ref, 2 * s, 4 + 2 * s, hw) for s in range(2)])
        run(1, 2, [cat(one_ref, 3, 7, s * hw) for s in range(2)])


def adam_one(factor, one, w, m, v, before):
    _, _, rows, cw = w.shape
    here = pl.BlockSpec((2, 2, rows, cw), lambda i: (0, i + 3, 0, 0))
    return pl.pallas_call(
        adam_one_kernel,
        grid=(2,),
        in_specs=[sm(), full(one.shape)] + [here] * 3 + [pl.BlockSpec(memory_space=pl.ANY)] * 4,
        out_specs=[here] * 4,
        out_shape=[shape(w.shape, f32)] * 4,
        input_output_aliases={5 + k: k for k in range(4)},
        compiler_params=params(),
        cost_estimate=cost(0, 32 * rows * cw * 8),
        name="adam_one",
    )(factor, one, w, m, v, *before)


def adam_mod_kernel(sc_ref, d_ref, f_ref, w_ref, m_ref, v_ref, *refs):
    og, ow, om, ov = refs[-4:]
    s, i = pl.program_id(0), pl.program_id(1)
    nseq = d_ref.shape[2]
    for j in range(2):
        g = sc_ref[:, 0:1] * d_ref[0, j, 0:1]
        for n in range(1, nseq):
            g = g + sc_ref[:, n : n + 1] * d_ref[0, j, n : n + 1]
        og[0, j] = g
        ow[0, j], om[0, j], ov[0, j] = adam_update(
            w_ref[0, j], m_ref[0, j], v_ref[0, j], g * f_ref[s, 2 * i + j], decay_rate
        )


def adam_mod(sc, dmod, factor, w, m, v, before):
    _, _, rows, cw = w.shape
    nseq = sc.shape[1]
    here = pl.BlockSpec((1, 2, rows, cw), lambda s, i: (s, i, 0, 0))
    return pl.pallas_call(
        adam_mod_kernel,
        grid=(2, 3),
        in_specs=[
            pl.BlockSpec((rows, nseq), lambda s, i: (0, 0)),
            pl.BlockSpec((1, 2, nseq, cw), lambda s, i: (s, i, 0, 0)),
            sm(),
        ]
        + [here] * 3
        + [pl.BlockSpec(memory_space=pl.ANY)] * 4,
        out_specs=[here] * 4,
        out_shape=[shape(w.shape, f32)] * 4,
        input_output_aliases={6 + k: k for k in range(4)},
        compiler_params=params(),
        cost_estimate=cost(0, 28 * rows * cw * 12),
        name="adam_mod",
    )(sc, dmod, factor, w, m, v, *before)


def make_shards(sizes):
    ns, nc, nt = sizes["shard"], sizes["ctx"], sizes["tensor"]
    owners = 2 * nt
    blocks = ns * nc
    hops = [("shard", 1)]
    hops += [("shard", 1 << b) for b in range(1, ns.bit_length() - 1)]
    hops += [("ctx", 1 << b) for b in range(nc.bit_length() - 1)]
    hops += [("tensor", 1 << b) for b in range(nt.bit_length() - 1)]

    def pp(x, axis, xor):
        return lax.ppermute(x, axis, [(i, i ^ xor) for i in range(sizes[axis])])

    def swap(x, axis):
        return lax.all_to_all(x, axis, 0, 0, tiled=True)

    def all_sum(x):
        for axis, xor in hops:
            x = x + pp(x, axis, xor)
        return x

    def all_sum_halved(x):
        core = lax.axis_index("shard") % 2
        half = x.shape[0] // 2
        part = lambda c: lax.dynamic_slice_in_dim(x, c * half, half, 0)
        mine = part(core) + pp(part(1 - core), "shard", 1)
        for axis, xor in hops[1:]:
            mine = mine + pp(mine, axis, xor)
        other = pp(mine, "shard", 1)
        return jnp.concatenate([jnp.where(core == 0, mine, other), jnp.where(core == 0, other, mine)], axis=0)

    def after(x, *deps):
        return lax.optimization_barrier((x,) + deps)[0]

    def dyn(x, i, axis=0):
        return lax.dynamic_index_in_dim(x, i, axis, keepdims=False)

    def shards(
        image_rows,
        text_rows,
        condition,
        slot_table,
        weights,
        mom_one,
        mom_two,
        biases,
        bias_one,
        bias_two,
        image_cot,
        text_cot,
    ):
        hp = lax.Precision.HIGHEST
        nseq, D = condition.shape
        img = image_rows.shape[1]
        txt = text_rows.shape[1]
        ct = -(-txt // (owners * 16)) * 16
        ci = img // owners
        tpad = ct * owners
        T = img + tpad
        live_rows = img + txt
        cw = weights.shape[3]
        hw = cw // 2
        rows = weights.shape[1]
        shard_i, ctx_i, z = (lax.axis_index(a) for a in ("shard", "ctx", "tensor"))
        core = shard_i % 2
        first = core == 0
        me = shard_i * nc + ctx_i
        own = core * nt + z
        i32 = jnp.int32
        core_arr = core.reshape(1).astype(i32)
        own_arr = own.reshape(1).astype(i32)
        wt, m1, m2 = (jnp.moveaxis(x, 2, 1) for x in (weights, mom_one, mom_two))

        everyone = ("shard", "ctx")

        def gather(w):
            return lax.all_gather(w, everyone, axis=1, tiled=True)

        one_mine, o_mine = prep_one(wt)
        w_one = gather(one_mine)
        silu_all = jax.nn.silu(condition).astype(bf)
        sc_rows = lax.dynamic_slice_in_dim(silu_all, me * rows, rows, 1)
        mod = mod_partial(after(sc_rows, one_mine), wt)

        fixed = nseq == 2

        def pair(x):
            other = pp(x, "shard", 1)
            even = jnp.where(first, x, other)
            return [even] if fixed else [even, jnp.where(first, other, x)]

        tables = [t[0] for t in pair(slot_table)]
        lives = [(t >= 0).astype(f32) for t in tables]
        pickers = [(t == jnp.arange(nseq, dtype=i32)).astype(f32) for t in tables]
        pad_txt = lambda x: jnp.pad(x, ((0, tpad - txt), (0, 0)))
        x_img = [x[0] for x in pair(image_rows)]
        x_txt = [pad_txt(x[0]) for x in pair(text_rows)]
        mod = mod + pp(mod, "shard", 1)
        others = [r for r in range(1, blocks) if not r & nc]
        mod = sum(
            [lax.ppermute(mod, everyone, [(i, i ^ r) for i in range(blocks)]) for r in others], mod
        )
        mod = jnp.stack([mod] + [pp(mod, "tensor", k) for k in range(1, nt)])
        mod = jnp.concatenate([dyn(mod, z ^ k) for k in range(nt)], axis=-1)
        mods = [
            (jnp.einsum("n,sjne->sje", p, mod, precision=hp) + biases[:, :6]).reshape(12, D)
            for p in pickers
        ]
        col = z * cw
        bias_half = lax.dynamic_slice_in_dim(biases, col + core * hw, hw, 2)
        bias_cols = lax.dynamic_slice_in_dim(biases, col, cw, 2)
        bq = bias_half[:, 6]
        bkv = jnp.concatenate([jnp.zeros((2, hw), f32), bias_half[:, 7]], axis=1)
        b_up = lax.dynamic_slice_in_dim(bias_cols, 9 + 2 * core, 2, 1).reshape(4, cw)
        b_flat = biases.reshape(28, D)

        c_img = [(x[0] * l.astype(bf)) for x, l in zip(pair(image_cot), lives)]
        c_txt = [pad_txt(x[0] * l.astype(bf)) for x, l in zip(pair(text_cot), lives)]
        w_o = gather(after(o_mine, *mods))
        w_one = after(w_one, *mods, *x_img, *c_img)

        slots = range(len(tables))
        his, hts, nis, nts, qs, kvs, kv_gots = [], [], [], [], [], [], []
        for n in slots:
            hi, ht, ni, nt_, q, kv = qkv(core_arr, x_img[n], x_txt[n], txt, mods[n], bq, bkv, w_one)
            his.append(hi)
            hts.append(ht)
            nis.append(ni)
            nts.append(nt_)
            qs.append(q)
            kvs.append(kv)
            kv_gots.append(pp(kv, "ctx", 1))
        w_mlp = gather(after(wt[:, 10:18].astype(bf).reshape(16, rows, cw), kv_gots[-1]))

        def fold(send, keep):
            return (keep.astype(f32) + pp(send, "shard", 1).astype(f32)).astype(bf)

        def own_call(kernel, name, n, tokens, wholes, outs, deps=()):
            return row_call(functools.partial(kernel, ci), name, own_arr, ci, ct, D, tokens, wholes, outs, deps)

        chunk = ci + ct
        copies = shape((nt, chunk, D))
        attns, lses, o_parts = [], [], []
        for n in slots:
            a, lse = attn_fwd(qs[n], kvs[n], kv_gots[n], img, live_rows)
            attns.append(a)
            lses.append(lse)
            o_parts.append(swap(fold(*oproj(core_arr, a, w_o, nt, img)), "tensor"))

        mlp_all, one_all = zeros(after(core_arr, lses[-1]), (16, 8), D, cw)
        mlp_all = mlp_all.reshape(2, 2, 2, 2, D, cw)
        one_all = one_all.reshape(2, 4, D, cw)
        dyis, dyts, gs, dus, up_sums, dh_parts, h2is, h2ts, o_sums = [], [], [], [], [], [], [], [], []
        for n in slots:
            h2, o_sum = own_call(
                after_attn_kernel,
                "after_attn",
                n,
                [(x_img[n], x_txt[n])],
                [mods[n], b_flat, after(o_parts[n], mlp_all)],
                [copies, shape((chunk, D), f32)],
            )
            o_sums.append(o_sum)
            dyi, dyt, *dg = grad_gate(core_arr, after(c_img[n], o_sum), c_txt[n], mods[n], w_mlp)
            mine = after(swap(h2, "tensor"), dyi)
            h2i, h2t, gi, gt, dui, dut, send, keep, up_sum = mlp(
                core_arr, mine, pp(mine, "shard", 1), *dg, w_mlp, b_up
            )
            dyis.append(dyi)
            dyts.append(dyt)
            h2is.append(h2i)
            h2ts.append(h2t)
            gs.append((gi, gt))
            dus.append((dui, dut))
            up_sums.append(up_sum)
            tie = fold(send, keep)
            dh_parts.append(swap(tie, "tensor"))

        def outer_sum(pairs):
            t = None
            for a, b in pairs:
                g = dotf(a, b, TN)
                t = g if t is None else t + g
            return t.astype(bf)

        def scatter(grads):
            return lax.psum_scatter(grads, everyone, scatter_dimension=1, tiled=True)

        def put(into, g, *at):
            return lax.dynamic_update_slice(into, g.reshape((1,) * len(at) + g.shape), at + (0, 0))

        for s, (h2, dy) in enumerate(((h2is, dyis), (h2ts, dyts))):
            for j in range(2):
                up = outer_sum([(h2[n], dus[n][s][j]) for n in slots])
                mlp_all = put(mlp_all, up, s, 0, core, j)
                dn = outer_sum([(dy[n], gs[n][s][j]) for n in slots])
                if (s, j) != (1, 1):
                    mlp_all = put(mlp_all, dn, s, 1, core, j)
        do_owns, dxs, mid_sums = [], [], []
        for n in slots:
            do_own, dx, sums = own_call(
                after_mlp_kernel,
                "after_mlp",
                n,
                [(x_img[n], x_txt[n]), (c_img[n], c_txt[n])],
                [mods[n], o_sums[n], dh_parts[n]],
                [copies, shape((chunk, D), f32), shape((16, D), f32)],
                deps=[mlp_all, dn],
            )
            dxs.append(dx)
            mid_sums.append(sums)
            do_owns.append(do_own)
        probe = mid_sums[-1][0, 0]
        mlp_all = put(mlp_all, dn, 1, 1, core + (probe != probe).astype(core.dtype), 1)
        mlp_sum = scatter(mlp_all.reshape(16, D, cw))
        tie = do_owns[-1]
        y_halves = [fold(*down(core_arr, *(after(g, tie) for g in gs[n]), w_mlp, nt)) for n in slots]
        dois, dots, dqs, dkv_own, dkv_gots, out_owns, low_sums = [], [], [], [], [], [], []
        for n in slots:
            mine = after(swap(do_owns[n], "tensor"), y_halves[n])
            y_part = swap(after(y_halves[n], mine), "tensor")
            doi, dot, da = grad_attn(core_arr, mine, pp(mine, "shard", 1), w_o, img, tpad)
            dois.append(doi)
            dots.append(dot)
            dq, dkv_a, dkv_b = attn_bwd(qs[n], kvs[n], kv_gots[n], attns[n], da, lses[n])
            dqs.append(dq)
            dkv_own.append(dkv_a)
            dkv_gots.append(pp(after(dkv_b, y_part), "ctx", 1))
            out_own, sums = own_call(
                after_down_kernel,
                "after_down",
                n,
                [(x_img[n], x_txt[n]), (c_img[n], c_txt[n])],
                [mods[n], b_flat, lives[n].reshape(1, 1), o_sums[n], after(y_part, dq)],
                [copies, shape((16, D), f32)],
            )
            low_sums.append(sums)
            out_owns.append(swap(out_own, "tensor"))
        tie = dqs[-1]
        o_grads = [
            outer_sum([(after(dois[n], tie), attns[n][:img]) for n in slots]),
            outer_sum([(after(dots[n], tie), attns[n][img:]) for n in slots]),
        ]
        cat = lambda a, b: jnp.concatenate([a, b], axis=1)
        one_all = put(one_all, cat(*o_grads), core, 3)
        clip = lambda sq: jnp.minimum(1.0, clip_unit * D / jnp.sqrt(sq + clip_eps))

        def pad_row(x):
            x = x.reshape(1, -1)
            return jnp.pad(x, ((0, 0), (0, -x.shape[1] % 128)))

        d_parts, dkv_img, dkv_txt, qv_sums, end_sums = [], [], [], [], []
        for n in slots:
            send, keep, kvi, kvt, qv, sums = grad_in(
                core_arr, [out_owns[n], one_all], dqs[n], dkv_own[n], dkv_gots[n], nis[n], nts[n], w_one, nt, txt
            )
            dkv_img.append(kvi)
            dkv_txt.append(kvt)
            qv_sums.append(qv)
            end_sums.append(sums)
            tie = fold(send, keep)
            d_parts.append(swap(tie, "tensor"))
        q_grads = []
        for s, (part, left, right) in enumerate(((slice(0, img), his, dkv_img), (slice(img, T), hts, dkv_txt))):
            q_grads.append(outer_sum([(left[n], after(dqs[n], tie)[part]) for n in slots]))
            one_all = put(one_all, outer_sum([(left[n], right[n]) for n in slots]), core, 2 * s)
        one_all = put(one_all, cat(*q_grads), core, 1)
        one_rows = scatter(one_all.reshape(8, D, cw))

        mlp_sq = pad_row(jnp.sum(jnp.sum(jnp.square(mlp_sum.astype(f32)), axis=1), axis=1))
        place_arr = jnp.stack([z, core]).astype(i32)
        packed = all_sum_halved(
            sum(
                pack_sums(
                    pickers[n], place_arr, mid_sums[n], low_sums[n], end_sums[n], up_sums[n], qv_sums[n], mlp_sq if n == 0 else jnp.zeros_like(mlp_sq)
                )
                for n in slots
            )
        )
        grad_owns = []
        for n in slots:
            (g,) = row_call(
                functools.partial(after_back_kernel, ci),
                "after_back",
                own_arr,
                ci,
                ct,
                D,
                [(x_img[n], x_txt[n])],
                [mods[n], dxs[n], d_parts[n]],
                [copies],
                deps=[one_all],
            )
            grad_owns.append(swap(g, "tensor"))
        state = adam_segments(
            clip(packed[nseq * 12 + 16, :16].reshape(2, 8)), mlp_sum.reshape(2, 8, rows, cw), 10, wt, m1, m2
        )
        e = nseq * 12
        dmod = packed[:e].reshape(nseq, 2, 6, D)
        od = packed[e : e + 4].reshape(2, 2, D)
        up_rows = packed[e + 4 : e + 12].reshape(2, 4, D)
        qv = packed[e + 12 : e + 16].reshape(2, 2, D)
        bias_grad = jnp.concatenate(
            [jnp.sum(dmod, axis=0), qv, od[:, :1], up_rows, od[:, 1:]], axis=1
        )
        wide = silu_all.astype(f32)
        gram_a = jnp.einsum("ni,mi->nm", wide, wide, precision=hp)
        gram_b = jnp.einsum("nsje,msje->sjnm", dmod, dmod, precision=hp)
        mod_sq = jnp.maximum(jnp.sum(gram_b * gram_a, axis=(2, 3)), 0.0)
        mod_cols = lax.dynamic_slice_in_dim(dmod, col, cw, 3)
        mod_cols = jnp.transpose(mod_cols, (1, 2, 0, 3))
        sc_wide = sc_rows.astype(f32)
        cond_rows = jnp.einsum("sjne,sjie->ni", mod_cols, wt[:, :6].astype(bf).astype(f32), precision=hp)
        cond_part = lax.dynamic_update_slice_in_dim(jnp.zeros((nseq, D), f32), cond_rows, me * rows, 1)

        state = adam_mod(jnp.transpose(sc_wide), mod_cols, clip(mod_sq), wt, m1, m2, state)
        mod_state = state[0]
        t = column_squares(one_rows, mod_state)
        t = t[:4] + t[4:]
        one_sq = jnp.stack([jnp.sum(t[:, :hw], axis=1), jnp.sum(t[:, hw:], axis=1)], axis=1)
        one_sq = jnp.stack(
            [jnp.stack([one_sq[1, s], one_sq[2 * s, 0], one_sq[2 * s, 1], one_sq[3, s]]) for s in range(2)]
        )
        tail = jnp.concatenate([cond_part.reshape(-1), one_sq.reshape(-1)])
        tail = all_sum(tail)
        cond_grad = tail[: nseq * D].reshape(nseq, D) * silu_slope(condition)
        one_sq = tail[nseq * D :].reshape(2, 4)
        state = adam_one(clip(one_sq), one_rows, wt, m1, m2, state)
        weight_grad, new_w, new_one, new_two = (jnp.moveaxis(x, 1, 2) for x in state)

        bias_sq = jnp.sum(bias_grad * bias_grad, axis=2)
        bias_factor = jnp.minimum(1.0, clip_unit * D**0.5 / jnp.sqrt(bias_sq + clip_eps))
        new_b, new_b1, new_b2 = adam_update(
            biases, bias_one, bias_two, bias_grad * bias_factor[:, :, None], 0.0
        )

        def finish(mine, dep=None):
            flag = first.astype(i32).reshape(1) if fixed else jnp.ones((1,), i32)
            send = mine if dep is None else [copy_after(x, dep) for x in mine]
            done = [join_tokens(core_arr, flag, x, pp(y, "shard", 1), img, tpad) for x, y in zip(mine, send)]
            return done[0] if fixed else [jnp.where(first, a, b) for a, b in zip(*done)]

        out_img, out_txt = finish(out_owns)
        grad_img, grad_txt = finish(grad_owns, mod_state)
        return (
            out_img[None],
            out_txt[None, :txt],
            grad_img[None],
            grad_txt[None, :txt],
            cond_grad,
            weight_grad,
            new_w,
            new_one,
            new_two,
            bias_grad,
            new_b,
            new_b1,
            new_b2,
        )

    return shards


def solution(mesh):
    sizes = dict(mesh.shape)
    rows = P("shard", "ctx", None)
    mat = P(None, ("shard", "ctx"), None, "tensor")
    return jax.shard_map(
        make_shards(sizes),
        mesh=mesh,
        in_specs=(rows, rows, P(), P("shard"), mat, mat, mat, P(), P(), P(), rows, rows),
        out_specs=(rows, rows, rows, rows, P(), mat, mat, mat, mat, P(), P(), P(), P()),
        check_vma=False,
    )
```

```python
import functools
import jax
import jax.numpy as jnp
from jax import lax
from jax.experimental import pallas as pl
from jax.experimental.pallas import tpu as pltpu
from jax.sharding import PartitionSpec as P

DH = 64
NT = (((1,), (1,)), ((), ()))
TN = (((0,), (0,)), ((), ()))
NN = (((1,), (0,)), ((), ()))
bf = jnp.bfloat16
f32 = jnp.float32

beta_one = 0.9
beta_two = 0.95
learn_rate = 0.1
decay_rate = 0.1
adam_eps = 1e-08
adam_step = 10.0
norm_eps = 1e-06
gelu_coef = 0.044715
root_two_pi = 0.7978845608028654
clip_unit = 0.0001
clip_eps = 1e-12


def norm_back(normed, inverse, upstream):
    mean_grad = jnp.mean(upstream, axis=-1, keepdims=True)
    mean_dot = jnp.mean(upstream * normed, axis=-1, keepdims=True)
    return inverse * (upstream - mean_grad - normed * mean_dot)


def gelu_parts(preact):
    inner = root_two_pi * (preact + gelu_coef * preact * preact * preact)
    tanh_value = jnp.tanh(inner)
    value_out = 0.5 * preact * (1.0 + tanh_value)
    slope_out = 0.5 * (1.0 + tanh_value) + 0.5 * preact * (
        1.0 - tanh_value * tanh_value
    ) * root_two_pi * (1.0 + 3.0 * gelu_coef * preact * preact)
    return (value_out, slope_out)


def silu_slope(drawn_values):
    sigmoid_val = jax.nn.sigmoid(drawn_values)
    return sigmoid_val * (1.0 + drawn_values * (1.0 - sigmoid_val))


def adam_update(parameter, moment_one, moment_two, gradient, decay_factor):
    new_one = beta_one * moment_one + (1.0 - beta_one) * gradient
    new_two = beta_two * moment_two + (1.0 - beta_two) * gradient * gradient
    first_hat = new_one / (1.0 - beta_one**adam_step)
    second_hat = new_two / (1.0 - beta_two**adam_step)
    new_param = parameter - learn_rate * (
        first_hat / (jnp.sqrt(second_hat) + adam_eps) + decay_factor * parameter
    )
    return (new_param, new_one, new_two)


def dotf(a, b, dims, precision=None):
    return lax.dot_general(a, b, dims, preferred_element_type=f32, precision=precision)


def vm():
    return pl.BlockSpec(memory_space=pltpu.VMEM)


def sm():
    return pl.BlockSpec(memory_space=pltpu.SMEM)


def shape(dims, dtype=bf):
    return jax.ShapeDtypeStruct(dims, dtype)


def params(mib=58):
    return pltpu.CompilerParams(vmem_limit_bytes=mib * 2**20)


def cost(flops, nbytes, trans=0):
    return pl.CostEstimate(flops=1024, bytes_accessed=1024, transcendentals=0)


def full(dims):
    return pl.BlockSpec(dims, lambda *_: (0,) * len(dims), pipeline_mode=pl.Buffered(1))


def prep_kernel(a_ref, b_ref, one_ref, o_ref):
    hw = a_ref.shape[3] // 2
    cat = lambda x, y: jnp.concatenate([x, y], axis=-1)
    q, k = ([a_ref[s, j].astype(bf) for s in range(2)] for j in range(2))
    v, o = ([b_ref[s, j].astype(bf) for s in range(2)] for j in range(2))
    for c in range(2):
        half = lambda w: w[:, c * hw : (c + 1) * hw]
        one_ref[3 * c] = cat(half(k[0]), half(v[0]))
        one_ref[3 * c + 1] = cat(half(q[0]), half(q[1]))
        one_ref[3 * c + 2] = cat(half(k[1]), half(v[1]))
        o_ref[c] = cat(half(o[0]), half(o[1]))


def prep_one(wt):
    _, _, rows, cw = wt.shape
    seg = lambda k: pl.BlockSpec((2, 2, rows, cw), lambda i: (0, k, 0, 0))
    outs = [shape((6, rows, cw)), shape((2, rows, cw))]
    return pl.pallas_call(
        prep_kernel,
        grid=(1,),
        in_specs=[seg(3), seg(4)],
        out_specs=[full(o.shape) for o in outs],
        out_shape=outs,
        compiler_params=params(),
        cost_estimate=cost(0, 0),
        name="prep_one",
    )(wt, wt)


def mod_kernel(sc_ref, w_ref, o_ref):
    for j in range(2):
        o_ref[0, j] = dotf(sc_ref[...], w_ref[0, j].astype(bf), NN)


def mod_partial(sc, wt):
    _, _, rows, cw = wt.shape
    n = sc.shape[0]
    return pl.pallas_call(
        mod_kernel,
        grid=(2, 3),
        in_specs=[
            pl.BlockSpec((n, rows), lambda s, i: (0, 0)),
            pl.BlockSpec((1, 2, rows, cw), lambda s, i: (s, i, 0, 0)),
        ],
        out_specs=pl.BlockSpec((1, 2, n, cw), lambda s, i: (s, i, 0, 0)),
        out_shape=shape((2, 6, n, cw), f32),
        compiler_params=params(),
        cost_estimate=cost(0, 0),
        name="mod_partial",
    )(sc, wt)


def normed_of(x):
    center = x - jnp.mean(x, axis=-1, keepdims=True)
    inverse = lax.rsqrt(jnp.mean(center * center, axis=-1, keepdims=True) + norm_eps)
    return center * inverse, inverse


def qkv_kernel(n_img, txt, hw, core_ref, xi_ref, xt_ref, mod_ref, bq_ref, bkv_ref, w_ref, hi_ref, ht_ref, ni_ref, nt_ref, q_ref, kv_ref):
    i = pl.program_id(0)
    rows = xi_ref.shape[0]

    def run(s, x, h_ref, n_ref, at, live):
        size = x.shape[0]
        n, _ = normed_of(x.astype(f32))
        n_ref[...] = n.astype(bf)
        h = (n * (1.0 + mod_ref[6 * s + 1 : 6 * s + 2]) + mod_ref[6 * s : 6 * s + 1]).astype(bf)
        h_ref[...] = h
        q = dotf(h, w_ref[1, :, hw * s : hw * (s + 1)], NN) + bq_ref[s : s + 1]
        q = (q.astype(bf).astype(f32) * DH**-0.5).astype(bf)
        q_ref[pl.ds(at, size)] = jnp.concatenate([q, jnp.zeros((size, 256 - hw), bf)], axis=1)
        kv = dotf(h, w_ref[2 * s], NN) + bkv_ref[s : s + 1]
        kv_ref[pl.ds(at, size)] = (kv if live is None else jnp.where(live, kv, 0.0)).astype(bf)

    @pl.when(i < n_img)
    def _():
        run(0, xi_ref[...], hi_ref, ni_ref, pl.multiple_of(i * rows, rows), None)

    @pl.when(i >= n_img)
    def _():
        live = lax.broadcasted_iota(jnp.int32, (xt_ref.shape[0], 1), 0) < txt
        run(1, xt_ref[...], ht_ref, nt_ref, n_img * rows, live)


def qkv(core, xi, xt, txt, mod, bq, bkv, w):
    img, D = xi.shape
    tpad = xt.shape[0]
    n_img = 2
    rows = img // n_img
    T = img + tpad
    hw, cw = bq.shape[1], w.shape[2]
    x_spec = pl.BlockSpec((rows, D), lambda i, c: (jnp.minimum(i, n_img - 1), 0))
    outs = [shape((img, D)), shape((tpad, D))] * 2 + [shape((T, 256)), shape((T, cw))]
    return pl.pallas_call(
        functools.partial(qkv_kernel, n_img, txt, hw),
        grid_spec=pltpu.PrefetchScalarGridSpec(
            num_scalar_prefetch=1,
            grid=(n_img + 1,),
            in_specs=[
                x_spec,
                full((tpad, D)),
                full(mod.shape),
                full(bq.shape),
                full(bkv.shape),
                pl.BlockSpec((3, D, cw), lambda i, c: (c[0], 0, 0), pipeline_mode=pl.Buffered(1)),
            ],
            out_specs=[x_spec, full((tpad, D))] * 2 + [full(o.shape) for o in outs[4:]],
        ),
        out_shape=outs,
        compiler_params=params(),
        cost_estimate=cost(2 * T * D * 3 * hw, 4 * T * D),
        name="qkv",
    )(core, xi, xt, mod, bq, bkv, w)


def store_chunks(core, send_ref, keep_ref, src, lo):
    nt = send_ref.shape[0]
    n = src.shape[0] // (2 * nt)
    for ref, c in ((send_ref, 1 - core), (keep_ref, core)):
        for t in range(nt):
            ref[t, lo : lo + n] = src[pl.ds(pl.multiple_of((c * nt + t) * n, n), n)].astype(bf)


def chunk_blocks(nt, chunk, width):
    return [pl.BlockSpec((nt, chunk, width), lambda i, c: (0, 0, i))] * 2


def oproj_kernel(img, core_ref, a_ref, w_ref, send_ref, keep_ref, acc):
    hw = a_ref.shape[1]
    acc[:img] = dotf(a_ref[:img], w_ref[0, :, :hw], NT)
    acc[img:] = dotf(a_ref[img:], w_ref[0, :, hw:], NT)
    store_chunks(core_ref[0], send_ref, keep_ref, acc.at[:img], 0)
    store_chunks(core_ref[0], send_ref, keep_ref, acc.at[img:], img // (2 * send_ref.shape[0]))


def oproj(core, a, w, nt, img):
    T, hw = a.shape
    _, D, cw = w.shape
    width = D // 3
    return pl.pallas_call(
        functools.partial(oproj_kernel, img),
        grid_spec=pltpu.PrefetchScalarGridSpec(
            num_scalar_prefetch=1,
            grid=(3,),
            in_specs=[full(a.shape), pl.BlockSpec((1, width, cw), lambda i, c: (c[0], i, 0))],
            out_specs=chunk_blocks(nt, T // (2 * nt), width),
            scratch_shapes=[pltpu.VMEM((T, width), f32)],
        ),
        out_shape=[shape((nt, T // (2 * nt), D))] * 2,
        compiler_params=params(),
        cost_estimate=cost(2 * T * D * hw, 2 * T * D),
        name="oproj",
    )(core, a, w)


def total(ref):
    t = ref[0].astype(f32)
    for k in range(1, ref.shape[0]):
        t = t + ref[k].astype(f32)
    return t


def store_copies(ref, rows, x):
    for k in range(ref.shape[0]):
        ref[k, rows] = x


def copy_kernel(x_ref, dep_ref, o_ref):
    o_ref[...] = x_ref[...]


def copy_after(x, dep):
    return pl.pallas_call(
        copy_kernel,
        in_specs=[vm(), pl.BlockSpec(memory_space=pl.ANY)],
        out_specs=vm(),
        out_shape=shape(x.shape),
        compiler_params=params(),
        cost_estimate=cost(0, 0),
        name="copy_after",
    )(x, dep)


def fold_kernel(x_ref, y_ref, dep_ref, o_ref):
    o_ref[...] = (x_ref[...].astype(f32) + y_ref[...].astype(f32)).astype(bf)


def fold_after(x, y, dep):
    block = pl.BlockSpec((1,) + x.shape[1:], lambda i: (i, 0, 0))
    return pl.pallas_call(
        fold_kernel,
        grid=(x.shape[0],),
        in_specs=[block, block, pl.BlockSpec(memory_space=pl.ANY)],
        out_specs=block,
        out_shape=shape(x.shape),
        compiler_params=params(),
        cost_estimate=cost(0, 0),
        name="fold_after",
    )(x, y, dep)


def own_specs(ci, ct, D):
    return [
        pl.BlockSpec((ci, D), lambda i, o: (o[0], 0)),
        pl.BlockSpec((ct, D), lambda i, o: (o[0], 0)),
    ]


def whole(dims):
    return pl.BlockSpec(dims, lambda i, o: (0,) * len(dims))


def row_call(kernel, name, own, ci, ct, D, tokens, wholes, outs, deps=()):
    specs = [s for _ in tokens for s in own_specs(ci, ct, D)] + [whole(w.shape) for w in wholes]
    flat = [x for pair in tokens for x in pair]
    n_in = 1 + len(specs)
    return pl.pallas_call(
        lambda *refs: kernel(*refs[:n_in], *refs[n_in + len(deps) :]),
        grid_spec=pltpu.PrefetchScalarGridSpec(
            num_scalar_prefetch=1,
            grid=(1,),
            in_specs=specs + [pl.BlockSpec(memory_space=pl.ANY)] * len(deps),
            out_specs=[whole(o.shape) for o in outs],
        ),
        out_shape=outs,
        compiler_params=params(),
        cost_estimate=cost(0, 0),
        name=name,
    )(own, *flat, *wholes, *deps)


def after_attn_kernel(ci, own_ref, xi_ref, xt_ref, mod_ref, b_ref, part_ref, h_ref, o_ref):
    sums = total(part_ref)
    for s, x_ref in enumerate((xi_ref, xt_ref)):
        rows = slice(0, ci) if s == 0 else slice(ci, sums.shape[0])
        m = lambda j: mod_ref[6 * s + j : 6 * s + j + 1]
        o = sums[rows] + b_ref[14 * s + 8 : 14 * s + 9]
        n, _ = normed_of(x_ref[...].astype(f32) + m(2) * o)
        store_copies(h_ref, rows, (n * (1.0 + m(4)) + m(3)).astype(bf))
        o_ref[rows] = o


def colsum(x):
    return jnp.sum(x, axis=0, keepdims=True)


def after_mlp_kernel(ci, own_ref, xi_ref, xt_ref, ci_ref, ct_ref, mod_ref, o_ref, part_ref, do_ref, dx_ref, sum_ref):
    sums = total(part_ref)
    for s, (x_ref, c_ref) in enumerate(((xi_ref, ci_ref), (xt_ref, ct_ref))):
        rows = slice(0, ci) if s == 0 else slice(ci, sums.shape[0])
        m = lambda j: mod_ref[6 * s + j : 6 * s + j + 1]
        o = o_ref[rows]
        n, inv = normed_of(x_ref[...].astype(f32) + m(2) * o)
        dh = sums[rows]
        cot = c_ref[...].astype(f32)
        dx = cot + norm_back(n, inv, dh * (1.0 + m(4)))
        do = dx * m(2)
        store_copies(do_ref, rows, do.astype(bf))
        dx_ref[rows] = dx
        rows_out = [colsum(dx * o), colsum(dh), colsum(dh * n), colsum(do), colsum(cot * m(5))]
        sum_ref[8 * s : 8 * s + 8] = jnp.concatenate(rows_out + [jnp.zeros((3, dx.shape[1]), f32)], axis=0)


def after_down_kernel(
    ci, own_ref, xi_ref, xt_ref, ci_ref, ct_ref, mod_ref, b_ref, live_ref, o_ref, part_ref, out_ref, sum_ref
):
    sums = total(part_ref)
    for s, (x_ref, c_ref) in enumerate(((xi_ref, ci_ref), (xt_ref, ct_ref))):
        rows = slice(0, ci) if s == 0 else slice(ci, sums.shape[0])
        m = lambda j: mod_ref[6 * s + j : 6 * s + j + 1]
        y = sums[rows] + b_ref[14 * s + 13 : 14 * s + 14]
        x1 = x_ref[...].astype(f32) + m(2) * o_ref[rows]
        store_copies(out_ref, rows, ((x1 + m(5) * y) * live_ref[...]).astype(bf))
        top = colsum(c_ref[...].astype(f32) * y)
        sum_ref[8 * s : 8 * s + 8] = jnp.concatenate([top, jnp.zeros((7, y.shape[1]), f32)], axis=0)


def after_back_kernel(ci, own_ref, xi_ref, xt_ref, mod_ref, dx_ref, part_ref, g_ref):
    sums = total(part_ref)
    for s, x_ref in enumerate((xi_ref, xt_ref)):
        rows = slice(0, ci) if s == 0 else slice(ci, sums.shape[0])
        n, inv = normed_of(x_ref[...].astype(f32))
        dh = sums[rows]
        g = dx_ref[rows] + norm_back(n, inv, dh * (1.0 + mod_ref[6 * s + 1 : 6 * s + 2]))
        store_copies(g_ref, rows, g.astype(bf))


def stream_blocks(img, tpad, width):
    return [
        pl.BlockSpec((1, img, width), lambda k, c: (jnp.minimum(k, 1), 0, 0)),
        pl.BlockSpec((1, tpad, width), lambda k, c: (jnp.maximum(k - 2, 0), 0, 0)),
    ]


def seg_call(kernel, name, core, ins, in_specs, outs, out_specs, scratch=(), est=None):
    return pl.pallas_call(
        kernel,
        grid_spec=pltpu.PrefetchScalarGridSpec(
            num_scalar_prefetch=1,
            grid=(4,),
            in_specs=in_specs,
            out_specs=out_specs,
            scratch_shapes=list(scratch),
        ),
        out_shape=outs,
        compiler_params=params(),
        cost_estimate=est or cost(0, 0),
        name=name,
    )(core, *ins)


def zeros_kernel(core_ref, *outs):
    for o in outs:
        o[...] = jnp.zeros_like(o)


def zeros(core, counts, D, cw):
    n = 8
    height = lambda c: c * D // n
    flat = pl.pallas_call(
        zeros_kernel,
        grid=(n,),
        in_specs=[sm()],
        out_specs=[pl.BlockSpec((height(c), cw), lambda i: (i, 0)) for c in counts],
        out_shape=[shape((c * D, cw)) for c in counts],
        compiler_params=params(),
        cost_estimate=cost(0, 0),
        name="zeros",
    )(core)
    return [x.reshape(-1, D, cw) for x in flat]


def seg_of(base):
    return lambda k, c: ((k // 2) * 8 + base + 2 * c[0] + lax.rem(k, 2), 0, 0)


def grad_gate_kernel(core_ref, ci_ref, ct_ref, mod_ref, w_ref, dyi_ref, dyt_ref, dgi_ref, dgt_ref):
    k = pl.program_id(0)
    for s, (c, dy, dg) in enumerate(((ci_ref, dyi_ref, dgi_ref), (ct_ref, dyt_ref, dgt_ref))):

        @pl.when(k == 2 * s)
        def _():
            dy[...] = (c[...].astype(f32) * mod_ref[6 * s + 5 : 6 * s + 6]).astype(bf)

        @pl.when(jnp.right_shift(k, 1) == s)
        def _():
            dg[0] = dotf(dy[...], w_ref[0], NN)


def grad_gate(core, cot_i, cot_t, mod, w):
    img, D = cot_i.shape
    tpad = cot_t.shape[0]
    T = img + tpad
    cw = w.shape[2]
    return seg_call(
        grad_gate_kernel,
        "grad_gate",
        core,
        [cot_i, cot_t, mod, w],
        [full(cot_i.shape), full(cot_t.shape), full(mod.shape), pl.BlockSpec((1, D, cw), seg_of(4))],
        [shape((img, D)), shape((tpad, D)), shape((2, img, cw), f32), shape((2, tpad, cw), f32)],
        [full(cot_i.shape), full(cot_t.shape)] + stream_blocks(img, tpad, cw),
        est=cost(4 * T * D * cw, 4 * T * D),
    )


def place_chunks(core, mine, other, img_ref, txt_ref):
    nt = mine.shape[0]
    ci, ct = img_ref.shape[0] // (2 * nt), txt_ref.shape[0] // (2 * nt)
    for ref, c in ((mine, core), (other, 1 - core)):
        for t in range(nt):
            o = c * nt + t
            img_ref[pl.ds(pl.multiple_of(o * ci, ci), ci)] = ref[t, :ci]
            txt_ref[pl.ds(pl.multiple_of(o * ct, ct), ct)] = ref[t, ci:]


def mlp_kernel(core_ref, mine, other, dgi, dgt, w_ref, b_ref, hi, ht, gi, gt, dui, dut, send_ref, keep_ref, bias_ref, acc_i, acc_t):
    k = pl.program_id(0)

    @pl.when(k == 0)
    def _():
        place_chunks(core_ref[0], mine, other, hi, ht)
        bias_ref[...] = jnp.zeros_like(bias_ref)

    lo = 0
    for s, (h, dg, g, du_ref, acc) in enumerate(((hi, dgi, gi, dui, acc_i), (ht, dgt, gt, dut, acc_t))):

        @pl.when(jnp.right_shift(k, 1) == s)
        def _():
            size = min(256, h.shape[0])
            sums = None
            for r in range(0, h.shape[0], size):
                at = slice(r, r + size)
                u = dotf(h[at], w_ref[0], NN) + b_ref[pl.ds(k, 1)]
                val, slope = gelu_parts(u)
                g[0, at] = val.astype(bf)
                du = dg[0, at] * slope
                du_b = du.astype(bf)
                du_ref[0, at] = du_b
                sums = colsum(du) if sums is None else sums + colsum(du)
                acc[at] = jnp.where(k == 2 * s, 0.0, acc[at]) + dotf(du_b, w_ref[0], NT)

            bias_ref[pl.ds(k, 1)] = sums

            @pl.when(k == 2 * s + 1)
            def _():
                store_chunks(core_ref[0], send_ref, keep_ref, acc, lo)

        lo += acc.shape[0] // (2 * send_ref.shape[0])


def mlp(core, mine, other, dgi, dgt, w, b):
    nt, chunk, D = mine.shape
    img, tpad, cw = dgi.shape[1], dgt.shape[1], w.shape[2]
    T = img + tpad
    blocks = stream_blocks(img, tpad, cw)
    whole_outs = [shape((img, D)), shape((tpad, D))]
    ends = [shape((nt, chunk, D)), shape((nt, chunk, D)), shape((8, cw), f32)]
    return seg_call(
        mlp_kernel,
        "mlp",
        core,
        [mine, other, dgi, dgt, w, b],
        [full(mine.shape)] * 2 + blocks + [pl.BlockSpec((1, D, cw), seg_of(0)), full(b.shape)],
        whole_outs + [shape((2, img, cw)), shape((2, tpad, cw))] * 2 + ends,
        [full(o.shape) for o in whole_outs] + blocks + blocks + [full(o.shape) for o in ends],
        [pltpu.VMEM((img, D), f32), pltpu.VMEM((tpad, D), f32)],
        cost(8 * T * D * cw, 4 * T * D, 2 * T * cw),
    )


def down_kernel(core_ref, gi, gt, w_ref, send_ref, keep_ref, acc_i, acc_t):
    k = pl.program_id(0)
    lo = 0
    for s, (g, acc) in enumerate(((gi, acc_i), (gt, acc_t))):

        @pl.when(jnp.right_shift(k, 1) == s)
        def _():
            y = dotf(g[0], w_ref[0], NT)

            @pl.when(k == 2 * s)
            def _():
                acc[...] = y

            @pl.when(k == 2 * s + 1)
            def _():
                acc[...] += y
                store_chunks(core_ref[0], send_ref, keep_ref, acc, lo)

        lo += acc.shape[0] // (2 * send_ref.shape[0])


def down(core, gi, gt, w, nt):
    img, tpad = gi.shape[1], gt.shape[1]
    D, cw = w.shape[1:]
    T = img + tpad
    ends = [shape((nt, T // (2 * nt), D))] * 2
    return seg_call(
        down_kernel,
        "down",
        core,
        [gi, gt, w],
        stream_blocks(img, tpad, cw) + [pl.BlockSpec((1, D, cw), seg_of(4))],
        ends,
        [full(o.shape) for o in ends],
        [pltpu.VMEM((img, D), f32), pltpu.VMEM((tpad, D), f32)],
        cost(4 * T * D * cw, 2 * T * D),
    )


def grad_attn_kernel(core_ref, mine, other, w_ref, doi_ref, dot_ref, da_ref):
    img, hw = doi_ref.shape[0], da_ref.shape[1]
    place_chunks(core_ref[0], mine, other, doi_ref, dot_ref)
    da_ref[:img] = dotf(doi_ref[...], w_ref[0, :, :hw], NN).astype(bf)
    da_ref[img:] = dotf(dot_ref[...], w_ref[0, :, hw:], NN).astype(bf)


def grad_attn(core, mine, other, w, img, tpad):
    _, D, cw = w.shape
    hw = cw // 2
    T = img + tpad
    outs = [shape((img, D)), shape((tpad, D)), shape((T, hw))]
    return pl.pallas_call(
        grad_attn_kernel,
        grid_spec=pltpu.PrefetchScalarGridSpec(
            num_scalar_prefetch=1,
            grid=(1,),
            in_specs=[full(mine.shape)] * 2 + [pl.BlockSpec((1, D, cw), lambda i, c: (c[0], 0, 0))],
            out_specs=[full(o.shape) for o in outs],
        ),
        out_shape=outs,
        compiler_params=params(),
        cost_estimate=cost(2 * T * D * hw, 4 * T * D),
        name="grad_attn",
    )(core, mine, other, w)


def grad_in_kernel(
    img, txt, core_ref, dep_ref, dep_two_ref, q_ref, a_ref, b_ref, ni_ref, nt_ref, w_ref, send_ref, keep_ref, kvi_ref, kvt_ref, qv_ref, sum_ref, acc
):
    T, hw = q_ref.shape

    @pl.when(pl.program_id(0) == 0)
    def _():
        for s, (at, out) in enumerate(((slice(0, img), kvi_ref), (slice(img, T), kvt_ref))):
            kv = a_ref[at].astype(f32) + b_ref[at].astype(f32)
            if s == 1:
                kv = jnp.where(lax.broadcasted_iota(jnp.int32, (T - img, 1), 0) < txt, kv, 0.0)
            out[...] = kv.astype(bf)
            sums = jnp.concatenate([colsum(q_ref[at].astype(f32)), colsum(kv)[:, hw:]], axis=1)
            qv_ref[4 * s : 4 * s + 4] = jnp.broadcast_to(sums, (4, 2 * hw))

    acc[:img] = dotf(q_ref[:img], w_ref[1, :, :hw], NT) + dotf(kvi_ref[...], w_ref[0], NT)
    acc[img:] = dotf(q_ref[img:], w_ref[1, :, hw:], NT) + dotf(kvt_ref[...], w_ref[2], NT)
    rows = []
    for at, n_ref in ((slice(0, img), ni_ref), (slice(img, T), nt_ref)):
        rows += [colsum(acc[at]), colsum(acc[at] * n_ref[...].astype(f32))]
    sum_ref[...] = jnp.concatenate(rows + [jnp.zeros((4, acc.shape[1]), f32)], axis=0)
    store_chunks(core_ref[0], send_ref, keep_ref, acc.at[:img], 0)
    store_chunks(core_ref[0], send_ref, keep_ref, acc.at[img:], img // (2 * send_ref.shape[0]))


def grad_in(core, deps, dq, kv_a, kv_b, n_img, n_txt, w, nt, txt):
    T, hw = dq.shape
    img, tpad = n_img.shape[0], n_txt.shape[0]
    cw = kv_a.shape[1]
    D = w.shape[1]
    width = D // 3
    ends = [shape((img, cw)), shape((tpad, cw)), shape((8, cw), f32)]
    column = lambda n: pl.BlockSpec((n, width), lambda i, c: (0, i))
    return pl.pallas_call(
        functools.partial(grad_in_kernel, img, txt),
        grid_spec=pltpu.PrefetchScalarGridSpec(
            num_scalar_prefetch=1,
            grid=(3,),
            in_specs=[pl.BlockSpec(memory_space=pl.ANY)] * 2
            + [full(dq.shape), full(kv_a.shape), full(kv_b.shape), column(img), column(tpad)]
            + [pl.BlockSpec((3, width, cw), lambda i, c: (c[0], i, 0))],
            out_specs=chunk_blocks(nt, T // (2 * nt), width) + [full(o.shape) for o in ends] + [column(8)],
            scratch_shapes=[pltpu.VMEM((T, width), f32)],
        ),
        out_shape=[shape((nt, T // (2 * nt), D))] * 2 + ends + [shape((8, D), f32)],
        compiler_params=params(),
        cost_estimate=cost(2 * T * D * 3 * hw, 2 * T * D),
        name="grad_in",
    )(core, *deps, dq, kv_a, kv_b, n_img, n_txt, w)


def tokens_kernel(core_ref, flag_ref, mine, other, *refs):
    oi_ref, ot_ref = refs[-2:]
    on = flag_ref[0] != 0

    @pl.when(on)
    def _():
        place_chunks(core_ref[0], mine, other, oi_ref, ot_ref)

    @pl.when(jnp.logical_not(on))
    def _():
        oi_ref[...] = jnp.zeros_like(oi_ref)
        ot_ref[...] = jnp.zeros_like(ot_ref)


def join_tokens(core, flag, mine, other, img, tpad, deps=()):
    D = mine.shape[2]
    return pl.pallas_call(
        tokens_kernel,
        in_specs=[sm(), sm(), vm(), vm()] + [pl.BlockSpec(memory_space=pl.ANY)] * len(deps),
        out_specs=[vm()] * 2,
        out_shape=[shape((img, D)), shape((tpad, D))],
        compiler_params=params(),
        cost_estimate=cost(0, 4 * (img + tpad) * D),
        name="join_tokens",
    )(core, flag, mine, other, *deps)


def pack_kernel(picker_ref, place_ref, mid_ref, low_ref, end_ref, up_ref, qv_ref, sq_ref, out_ref):
    nseq = picker_ref.shape[0]
    z, core = place_ref[0], place_ref[1]
    D, cw = mid_ref.shape[1], up_ref.shape[1]
    hw = cw // 2
    out_ref[...] = jnp.zeros_like(out_ref)
    at = 12 * nseq + 16
    out_ref[at : at + 1, :128] = sq_ref[...]
    for s in range(2):
        rows = jnp.concatenate(
            [end_ref[2 * s : 2 * s + 2], mid_ref[8 * s : 8 * s + 3], low_ref[8 * s : 8 * s + 1]], axis=0
        )
        for n in range(nseq):
            out_ref[12 * n + 6 * s : 12 * n + 6 * s + 6] = rows * picker_ref[n]
        at = 12 * nseq
        out_ref[at + 2 * s : at + 2 * s + 2] = mid_ref[8 * s + 3 : 8 * s + 5]
        lane = lax.broadcasted_iota(jnp.int32, (1, D), 1)
        inside = jnp.logical_and(lane >= z * cw, lane < (z + 1) * cw)
        up = jnp.concatenate([up_ref[2 * s : 2 * s + 2]] * (D // cw), axis=1)
        up = jnp.where(inside, up, 0.0)
        none = jnp.zeros_like(up)
        first = core == 0
        up = jnp.concatenate([jnp.where(first, up, none), jnp.where(first, none, up)], axis=0)
        out_ref[at + 4 + 4 * s : at + 8 + 4 * s] = up
        row = qv_ref[4 * s : 4 * s + 1]
        start = z * cw + core * hw
        inside = jnp.logical_and(lane >= start, lane < start + hw)
        for k in range(2):
            part = row[:, k * hw : (k + 1) * hw]
            part = jnp.concatenate([part, part], axis=1)
            part = jnp.concatenate([part] * (D // cw), axis=1)
            out_ref[at + 12 + 2 * s + k : at + 13 + 2 * s + k] = jnp.where(inside, part, 0.0)


def pack_sums(picker, place, mid, low, end, up, qv, sq):
    D = mid.shape[1]
    rows = -(-(12 * picker.shape[0] + 17) // 8) * 8
    return pl.pallas_call(
        pack_kernel,
        in_specs=[sm(), sm()] + [vm()] * 6,
        out_specs=vm(),
        out_shape=shape((rows, D), f32),
        compiler_params=params(),
        cost_estimate=cost(0, 0),
        name="pack_sums",
    )(picker, place, mid, low, end, up, qv, sq)


def squares_kernel(x_ref, dep_ref, o_ref):
    for p in range(x_ref.shape[0]):
        x = x_ref[p].astype(f32)
        o_ref[p : p + 1] = colsum(x * x)


def column_squares(x, dep):
    n, _, cw = x.shape
    return pl.pallas_call(
        squares_kernel,
        in_specs=[vm(), pl.BlockSpec(memory_space=pl.ANY)],
        out_specs=vm(),
        out_shape=shape((n, cw), f32),
        compiler_params=params(),
        cost_estimate=cost(0, 0),
        name="column_squares",
    )(x, dep)


def attn_fwd_kernel(heads, img, live, last, q_ref, kv_ref, *refs):
    T = kv_ref.shape[0]
    bq = q_ref.shape[0]
    lane = lax.broadcasted_iota(jnp.int32, (1, 256), 1)
    lane1 = lax.broadcasted_iota(jnp.int32, (1, 128), 1)
    keep = lax.broadcasted_iota(jnp.int32, (1, T - img), 1) < live - img
    q = q_ref[...]
    acc = jnp.zeros((bq, 256), f32)
    tile = jnp.zeros((bq, 128), f32)
    if last:
        acc_ref, stat_ref, a_ref, lse_ref = refs
        before, stat = acc_ref[...], stat_ref[...]
    for h in range(heads):
        qm = jnp.where((lane >> 6) == h, q, jnp.zeros_like(q))
        s_img = dotf(qm, kv_ref[:img, :256], NT)
        s_txt = jnp.where(keep, dotf(qm, kv_ref[img:, :256], NT), -1e30)
        m = jnp.maximum(jnp.max(s_img, axis=1, keepdims=True), jnp.max(s_txt, axis=1, keepdims=True))
        if last:
            m_old = stat[:, h : h + 1]
            m = jnp.maximum(m, m_old)
        e_img, e_txt = jnp.exp(s_img - m), jnp.exp(s_txt - m)
        l = jnp.sum(e_img, axis=1, keepdims=True) + jnp.sum(e_txt, axis=1, keepdims=True)
        pv = dotf(e_img.astype(bf), kv_ref[:img, 128:384], NN) + dotf(e_txt.astype(bf), kv_ref[img:, 128:384], NN)
        if last:
            scale = jnp.exp(m_old - m)
            l = l + stat[:, heads + h : heads + h + 1] * scale
            pv = (pv + before * scale) / l
            tile = jnp.where(lane1 == h, m + jnp.log(l), tile)
        else:
            tile = jnp.where(lane1 == h, m, jnp.where(lane1 == heads + h, l, tile))
        acc = jnp.where((lane >> 6) == h + 1, pv, acc)
    if last:
        a_ref[...] = acc[:, 64:256].astype(bf)
        lse_ref[...] = tile.T[:8]
    else:
        refs[0][...] = acc
        refs[1][...] = tile


def attn_half(q, kv, img, live, before=None, bq=384, heads=3):
    T = q.shape[0]
    block = lambda width: pl.BlockSpec((bq, width), lambda i: (i, 0))
    last = before is not None
    if last:
        outs = [shape((T, 192)), shape((8, T), f32)]
        out_specs = [block(192), pl.BlockSpec((8, bq), lambda i: (0, i))]
    else:
        outs = [shape((T, 256), f32), shape((T, 128), f32)]
        out_specs = [block(256), block(128)]
    return pl.pallas_call(
        functools.partial(attn_fwd_kernel, heads, img, live, last),
        grid=(T // bq,),
        in_specs=[block(256), full((T, 384))] + ([block(256), block(128)] if last else []),
        out_specs=out_specs,
        out_shape=outs,
        compiler_params=params(),
        cost_estimate=cost(0, 0),
        name="attn_last" if last else "attn_first",
    )(q, kv, *(before if last else ()))


def attn_bwd_kernel(heads, q_ref, kv_ref, a_ref, da_ref, lse_ref, dep_ref, dq_ref, dkv_ref, daw, delta, dqa):
    step = pl.program_id(0)
    T = q_ref.shape[0]
    lane = lax.broadcasted_iota(jnp.int32, (1, 256), 1)

    @pl.when(step == 0)
    def _():
        da = da_ref[...]
        daw[...] = jnp.concatenate([jnp.zeros((T, 64), bf), da], axis=1)
        prod = da.astype(f32) * a_ref[...].astype(f32)
        col = lax.broadcasted_iota(jnp.int32, (8, 192), 1)
        hm = ((col >> 6) == lax.broadcasted_iota(jnp.int32, (8, 192), 0)).astype(f32)
        delta[...] = dotf(hm, prod, NT, lax.Precision.HIGHEST)
        dqa[...] = jnp.zeros_like(dqa)

    kw = kv_ref[:, :256]
    vw = kv_ref[:, 128:384]
    dq = jnp.zeros((T, 256), f32)
    dk = jnp.zeros(kw.shape, f32)
    dv = jnp.zeros(kw.shape, f32)
    for h in range(heads):
        sel = (lane >> 6) == h
        qm = jnp.where(sel, q_ref[...], jnp.zeros((), bf))
        dam = jnp.where((lane >> 6) == h + 1, daw[...], jnp.zeros((), bf))
        p = jnp.exp(dotf(kw, qm, NT) - lse_ref[h : h + 1, :])
        dv = dv + dotf(p.astype(bf), dam, NN)
        ds = (p * (dotf(vw, dam, NT) - delta[h : h + 1, :])).astype(bf)
        dk = dk + dotf(ds, qm, NN)
        dq = dq + dotf(ds, jnp.where(sel, kw, jnp.zeros((), bf)), TN)
    dkv_ref[...] = jnp.concatenate([dk[:, :192], dv[:, 64:256]], axis=1).astype(bf)
    dqa[...] += dq

    @pl.when(step == pl.num_programs(0) - 1)
    def _():
        dq_ref[...] = dqa[...][:, :192] * DH**-0.5


def attn_bwd_half(q, kv, a, da, lse, dep, bk=576, heads=3):
    T = q.shape[0]
    block = pl.BlockSpec((bk, 384), lambda i: (i, 0))
    return pl.pallas_call(
        functools.partial(attn_bwd_kernel, heads),
        grid=(T // bk,),
        in_specs=[full((T, 256)), block, full((T, 192)), full((T, 192)), full((8, T)), pl.BlockSpec(memory_space=pl.ANY)],
        out_specs=[full((T, 192)), block],
        out_shape=[shape((T, 192), f32), shape((T, 384))],
        scratch_shapes=[pltpu.VMEM((T, 256), bf), pltpu.VMEM((8, T), f32), pltpu.VMEM((T, 256), f32)],
        compiler_params=params(),
        cost_estimate=cost(0, 0),
        name="attn_bwd",
    )(q, kv, a, da, lse, dep)


def adam_kernel(f_ref, g_ref, w_ref, m_ref, v_ref, *refs):
    og, ow, om, ov = refs[-4:]
    g = g_ref[0, 0].astype(f32)
    og[0, 0] = g
    factor = f_ref[pl.program_id(0), pl.program_id(1)]
    ow[0, 0], om[0, 0], ov[0, 0] = adam_update(w_ref[0, 0], m_ref[0, 0], v_ref[0, 0], g * factor, decay_rate)


def adam_segments(factor, grad, start, w, m, v, before=None):
    _, count, rows, cw = grad.shape
    here = pl.BlockSpec((1, 1, rows, cw), lambda s, i: (s, i + start, 0, 0))
    before = [] if before is None else list(before)
    return pl.pallas_call(
        adam_kernel,
        grid=(2, count),
        in_specs=[sm(), pl.BlockSpec((1, 1, rows, cw), lambda s, i: (s, i, 0, 0))]
        + [here] * 3
        + [pl.BlockSpec(memory_space=pl.ANY)] * len(before),
        out_specs=[here] * 4,
        out_shape=[shape(w.shape, f32)] * 4,
        input_output_aliases={5 + k: k for k in range(len(before))},
        compiler_params=params(),
        cost_estimate=cost(0, 60 * rows * cw * count),
        name="adam",
    )(factor, grad, w, m, v, *before)


def adam_one_kernel(f_ref, one_ref, w_ref, m_ref, v_ref, *refs):
    og, ow, om, ov = refs[-4:]
    hw = w_ref.shape[3] // 2
    cat = lambda ref, k0, k1, lo: jnp.concatenate([ref[k0, :, lo : lo + hw], ref[k1, :, lo : lo + hw]], axis=1)

    def run(j, base, grads):
        for s in range(2):
            g = grads[s].astype(f32)
            og[s, j] = g
            ow[s, j], om[s, j], ov[s, j] = adam_update(
                w_ref[s, j], m_ref[s, j], v_ref[s, j], g * f_ref[s, base + j], decay_rate
            )

    @pl.when(pl.program_id(0) == 0)
    def _():
        run(0, 0, [cat(one_ref, 1, 5, s * hw) for s in range(2)])
        run(1, 0, [cat(one_ref, 2 * s, 4 + 2 * s, 0) for s in range(2)])

    @pl.when(pl.program_id(0) == 1)
    def _():
        run(0, 2, [cat(one_ref, 2 * s, 4 + 2 * s, hw) for s in range(2)])
        run(1, 2, [cat(one_ref, 3, 7, s * hw) for s in range(2)])


def adam_one(factor, one, w, m, v, before):
    _, _, rows, cw = w.shape
    here = pl.BlockSpec((2, 2, rows, cw), lambda i: (0, i + 3, 0, 0))
    return pl.pallas_call(
        adam_one_kernel,
        grid=(2,),
        in_specs=[sm(), full(one.shape)] + [here] * 3 + [pl.BlockSpec(memory_space=pl.ANY)] * 4,
        out_specs=[here] * 4,
        out_shape=[shape(w.shape, f32)] * 4,
        input_output_aliases={5 + k: k for k in range(4)},
        compiler_params=params(),
        cost_estimate=cost(0, 32 * rows * cw * 8),
        name="adam_one",
    )(factor, one, w, m, v, *before)


def adam_mod_kernel(sc_ref, d_ref, f_ref, w_ref, m_ref, v_ref, *refs):
    og, ow, om, ov = refs[-4:]
    s, i = pl.program_id(0), pl.program_id(1)
    nseq = d_ref.shape[2]
    for j in range(2):
        g = sc_ref[:, 0:1] * d_ref[0, j, 0:1]
        for n in range(1, nseq):
            g = g + sc_ref[:, n : n + 1] * d_ref[0, j, n : n + 1]
        og[0, j] = g
        ow[0, j], om[0, j], ov[0, j] = adam_update(
            w_ref[0, j], m_ref[0, j], v_ref[0, j], g * f_ref[s, 2 * i + j], decay_rate
        )


def adam_mod(sc, dmod, factor, w, m, v, before):
    _, _, rows, cw = w.shape
    nseq = sc.shape[1]
    here = pl.BlockSpec((1, 2, rows, cw), lambda s, i: (s, i, 0, 0))
    return pl.pallas_call(
        adam_mod_kernel,
        grid=(2, 3),
        in_specs=[
            pl.BlockSpec((rows, nseq), lambda s, i: (0, 0)),
            pl.BlockSpec((1, 2, nseq, cw), lambda s, i: (s, i, 0, 0)),
            sm(),
        ]
        + [here] * 3
        + [pl.BlockSpec(memory_space=pl.ANY)] * 4,
        out_specs=[here] * 4,
        out_shape=[shape(w.shape, f32)] * 4,
        input_output_aliases={6 + k: k for k in range(4)},
        compiler_params=params(),
        cost_estimate=cost(0, 28 * rows * cw * 12),
        name="adam_mod",
    )(sc, dmod, factor, w, m, v, *before)


def make_shards(sizes):
    ns, nc, nt = sizes["shard"], sizes["ctx"], sizes["tensor"]
    owners = 2 * nt
    blocks = ns * nc
    hops = [("shard", 1)]
    hops += [("shard", 1 << b) for b in range(1, ns.bit_length() - 1)]
    hops += [("ctx", 1 << b) for b in range(nc.bit_length() - 1)]
    hops += [("tensor", 1 << b) for b in range(nt.bit_length() - 1)]

    def pp(x, axis, xor):
        return lax.ppermute(x, axis, [(i, i ^ xor) for i in range(sizes[axis])])

    def swap(x, axis):
        return lax.all_to_all(x, axis, 0, 0, tiled=True)

    def all_sum(x):
        for axis, xor in hops:
            x = x + pp(x, axis, xor)
        return x

    def all_sum_halved(x):
        core = lax.axis_index("shard") % 2
        half = x.shape[0] // 2
        part = lambda c: lax.dynamic_slice_in_dim(x, c * half, half, 0)
        mine = part(core) + pp(part(1 - core), "shard", 1)
        for axis, xor in hops[1:]:
            mine = mine + pp(mine, axis, xor)
        other = pp(mine, "shard", 1)
        return jnp.concatenate([jnp.where(core == 0, mine, other), jnp.where(core == 0, other, mine)], axis=0)

    def after(x, *deps):
        return lax.optimization_barrier((x,) + deps)[0]

    def dyn(x, i, axis=0):
        return lax.dynamic_index_in_dim(x, i, axis, keepdims=False)

    def shards(
        image_rows,
        text_rows,
        condition,
        slot_table,
        weights,
        mom_one,
        mom_two,
        biases,
        bias_one,
        bias_two,
        image_cot,
        text_cot,
    ):
        hp = lax.Precision.HIGHEST
        nseq, D = condition.shape
        img = image_rows.shape[1]
        txt = text_rows.shape[1]
        ct = -(-txt // (owners * 16)) * 16
        ci = img // owners
        tpad = ct * owners
        T = img + tpad
        live_rows = img + txt
        cw = weights.shape[3]
        hw = cw // 2
        rows = weights.shape[1]
        shard_i, ctx_i, z = (lax.axis_index(a) for a in ("shard", "ctx", "tensor"))
        core = shard_i % 2
        first = core == 0
        me = shard_i * nc + ctx_i
        own = core * nt + z
        i32 = jnp.int32
        core_arr = core.reshape(1).astype(i32)
        own_arr = own.reshape(1).astype(i32)
        wt, m1, m2 = (jnp.moveaxis(x, 2, 1) for x in (weights, mom_one, mom_two))

        everyone = ("shard", "ctx")

        def gather(w):
            return lax.all_gather(w, everyone, axis=1, tiled=True)

        one_mine, o_mine = prep_one(wt)
        w_one = gather(one_mine)
        silu_all = jax.nn.silu(condition).astype(bf)
        sc_rows = lax.dynamic_slice_in_dim(silu_all, me * rows, rows, 1)
        mod = mod_partial(after(sc_rows, one_mine), wt)

        fixed = nseq == 2

        def pair(x):
            other = pp(x, "shard", 1)
            even = jnp.where(first, x, other)
            return [even] if fixed else [even, jnp.where(first, other, x)]

        tables = [t[0] for t in pair(slot_table)]
        lives = [(t >= 0).astype(f32) for t in tables]
        pickers = [(t == jnp.arange(nseq, dtype=i32)).astype(f32) for t in tables]
        pad_txt = lambda x: jnp.pad(x, ((0, tpad - txt), (0, 0)))
        x_img = [x[0] for x in pair(image_rows)]
        x_txt = [pad_txt(x[0]) for x in pair(text_rows)]
        mod = mod + pp(mod, "shard", 1)
        others = [r for r in range(1, blocks) if not r & nc]
        mod = sum(
            [lax.ppermute(mod, everyone, [(i, i ^ r) for i in range(blocks)]) for r in others], mod
        )
        mod = jnp.stack([mod] + [pp(mod, "tensor", k) for k in range(1, nt)])
        mod = jnp.concatenate([dyn(mod, z ^ k) for k in range(nt)], axis=-1)
        mods = [
            (jnp.einsum("n,sjne->sje", p, mod, precision=hp) + biases[:, :6]).reshape(12, D)
            for p in pickers
        ]
        col = z * cw
        bias_half = lax.dynamic_slice_in_dim(biases, col + core * hw, hw, 2)
        bias_cols = lax.dynamic_slice_in_dim(biases, col, cw, 2)
        bq = bias_half[:, 6]
        bkv = jnp.concatenate([jnp.zeros((2, hw), f32), bias_half[:, 7]], axis=1)
        b_up = lax.dynamic_slice_in_dim(bias_cols, 9 + 2 * core, 2, 1).reshape(4, cw)
        b_flat = biases.reshape(28, D)

        c_img = [(x[0] * l.astype(bf)) for x, l in zip(pair(image_cot), lives)]
        c_txt = [pad_txt(x[0] * l.astype(bf)) for x, l in zip(pair(text_cot), lives)]
        w_o = gather(after(o_mine, *mods))
        w_one = after(w_one, *mods, *x_img, *c_img)

        slots = range(len(tables))
        his, hts, nis, nts, qs, kvs, kv_gots = [], [], [], [], [], [], []
        for n in slots:
            hi, ht, ni, nt_, q, kv = qkv(core_arr, x_img[n], x_txt[n], txt, mods[n], bq, bkv, w_one)
            his.append(hi)
            hts.append(ht)
            nis.append(ni)
            nts.append(nt_)
            qs.append(q)
            kvs.append(kv)
            kv_gots.append(pp(kv, "ctx", 1))
        firsts = [attn_half(qs[n], kvs[n], img, live_rows) for n in slots]
        w_mlp = gather(after(wt[:, 10:18].astype(bf).reshape(16, rows, cw), kv_gots[-1], firsts[-1][0]))

        def fold(send, keep):
            return (keep.astype(f32) + pp(send, "shard", 1).astype(f32)).astype(bf)

        def own_call(kernel, name, n, tokens, wholes, outs, deps=()):
            return row_call(functools.partial(kernel, ci), name, own_arr, ci, ct, D, tokens, wholes, outs, deps)

        chunk = ci + ct
        copies = shape((nt, chunk, D))
        attns, lses, o_parts = [], [], []
        for n in slots:
            a, lse = attn_half(qs[n], kv_gots[n], img, live_rows, firsts[n])
            attns.append(a)
            lses.append(lse)
            o_parts.append(swap(fold(*oproj(core_arr, a, w_o, nt, img)), "tensor"))

        mlp_all, one_all = zeros(after(core_arr, lses[-1]), (16, 8), D, cw)
        mlp_all = mlp_all.reshape(2, 2, 2, 2, D, cw)
        one_all = one_all.reshape(2, 4, D, cw)
        dyis, dyts, gs, dus, up_sums, dh_parts, h2is, h2ts, o_sums = [], [], [], [], [], [], [], [], []
        for n in slots:
            h2, o_sum = own_call(
                after_attn_kernel,
                "after_attn",
                n,
                [(x_img[n], x_txt[n])],
                [mods[n], b_flat, after(o_parts[n], mlp_all)],
                [copies, shape((chunk, D), f32)],
            )
            o_sums.append(o_sum)
            dyi, dyt, *dg = grad_gate(core_arr, after(c_img[n], o_sum), c_txt[n], mods[n], w_mlp)
            mine = after(swap(h2, "tensor"), dyi)
            h2i, h2t, gi, gt, dui, dut, send, keep, up_sum = mlp(
                core_arr, mine, pp(mine, "shard", 1), *dg, w_mlp, b_up
            )
            dyis.append(dyi)
            dyts.append(dyt)
            h2is.append(h2i)
            h2ts.append(h2t)
            gs.append((gi, gt))
            dus.append((dui, dut))
            up_sums.append(up_sum)
            tie = fold(send, keep)
            dh_parts.append(swap(tie, "tensor"))

        def outer_sum(pairs):
            t = None
            for a, b in pairs:
                g = dotf(a, b, TN)
                t = g if t is None else t + g
            return t.astype(bf)

        def scatter(grads):
            return lax.psum_scatter(grads, everyone, scatter_dimension=1, tiled=True)

        def put(into, g, *at):
            return lax.dynamic_update_slice(into, g.reshape((1,) * len(at) + g.shape), at + (0, 0))

        for s, (h2, dy) in enumerate(((h2is, dyis), (h2ts, dyts))):
            for j in range(2):
                up = outer_sum([(h2[n], dus[n][s][j]) for n in slots])
                mlp_all = put(mlp_all, up, s, 0, core, j)
                dn = outer_sum([(dy[n], gs[n][s][j]) for n in slots])
                if (s, j) != (1, 1):
                    mlp_all = put(mlp_all, dn, s, 1, core, j)
        do_owns, dxs, mid_sums = [], [], []
        for n in slots:
            do_own, dx, sums = own_call(
                after_mlp_kernel,
                "after_mlp",
                n,
                [(x_img[n], x_txt[n]), (c_img[n], c_txt[n])],
                [mods[n], o_sums[n], dh_parts[n]],
                [copies, shape((chunk, D), f32), shape((16, D), f32)],
                deps=[mlp_all, dn],
            )
            dxs.append(dx)
            mid_sums.append(sums)
            do_owns.append(do_own)
        probe = mid_sums[-1][0, 0]
        mlp_all = put(mlp_all, dn, 1, 1, core + (probe != probe).astype(core.dtype), 1)
        mlp_sum = scatter(mlp_all.reshape(16, D, cw))
        tie = do_owns[-1]
        y_halves = [fold(*down(core_arr, *(after(g, tie) for g in gs[n]), w_mlp, nt)) for n in slots]
        dois, dots, dqs, dkv_own, dkv_gots, out_owns, low_sums = [], [], [], [], [], [], []
        for n in slots:
            mine = after(swap(do_owns[n], "tensor"), y_halves[n])
            y_part = swap(after(y_halves[n], mine), "tensor")
            doi, dot, da = grad_attn(core_arr, mine, pp(mine, "shard", 1), w_o, img, tpad)
            dois.append(doi)
            dots.append(dot)
            dq_b, dkv_b = attn_bwd_half(qs[n], kv_gots[n], attns[n], da, lses[n], da)
            dq_a, dkv_a = attn_bwd_half(qs[n], kvs[n], attns[n], da, lses[n], dkv_b)
            dq = (dq_a + dq_b).astype(bf)
            dqs.append(dq)
            dkv_own.append(dkv_a)
            dkv_gots.append(pp(dkv_b, "ctx", 1))
            out_own, sums = own_call(
                after_down_kernel,
                "after_down",
                n,
                [(x_img[n], x_txt[n]), (c_img[n], c_txt[n])],
                [mods[n], b_flat, lives[n].reshape(1, 1), o_sums[n], after(y_part, dq)],
                [copies, shape((16, D), f32)],
            )
            low_sums.append(sums)
            out_owns.append(swap(out_own, "tensor"))
        tie = dqs[-1]
        o_grads = [
            outer_sum([(after(dois[n], tie), attns[n][:img]) for n in slots]),
            outer_sum([(after(dots[n], tie), attns[n][img:]) for n in slots]),
        ]
        cat = lambda a, b: jnp.concatenate([a, b], axis=1)
        one_all = put(one_all, cat(*o_grads), core, 3)
        clip = lambda sq: jnp.minimum(1.0, clip_unit * D / jnp.sqrt(sq + clip_eps))

        def pad_row(x):
            x = x.reshape(1, -1)
            return jnp.pad(x, ((0, 0), (0, -x.shape[1] % 128)))

        d_parts, dkv_img, dkv_txt, qv_sums, end_sums = [], [], [], [], []
        for n in slots:
            send, keep, kvi, kvt, qv, sums = grad_in(
                core_arr, [low_sums[n], one_all], dqs[n], dkv_own[n], dkv_gots[n], nis[n], nts[n], w_one, nt, txt
            )
            dkv_img.append(kvi)
            dkv_txt.append(kvt)
            qv_sums.append(qv)
            end_sums.append(sums)
            tie = fold_after(keep, pp(send, "shard", 1), out_owns[n])
            d_parts.append(swap(tie, "tensor"))
        q_grads = []
        for s, (part, left, right) in enumerate(((slice(0, img), his, dkv_img), (slice(img, T), hts, dkv_txt))):
            q_grads.append(outer_sum([(left[n], after(dqs[n], tie)[part]) for n in slots]))
            one_all = put(one_all, outer_sum([(left[n], right[n]) for n in slots]), core, 2 * s)
        one_all = put(one_all, cat(*q_grads), core, 1)
        one_rows = scatter(one_all.reshape(8, D, cw))

        mlp_sq = pad_row(jnp.sum(jnp.sum(jnp.square(mlp_sum.astype(f32)), axis=1), axis=1))
        place_arr = jnp.stack([z, core]).astype(i32)
        packed = all_sum_halved(
            sum(
                pack_sums(
                    pickers[n], place_arr, mid_sums[n], low_sums[n], end_sums[n], up_sums[n], qv_sums[n], mlp_sq if n == 0 else jnp.zeros_like(mlp_sq)
                )
                for n in slots
            )
        )
        grad_owns = []
        for n in slots:
            (g,) = row_call(
                functools.partial(after_back_kernel, ci),
                "after_back",
                own_arr,
                ci,
                ct,
                D,
                [(x_img[n], x_txt[n])],
                [mods[n], dxs[n], d_parts[n]],
                [copies],
                deps=[one_all],
            )
            grad_owns.append(swap(g, "tensor"))
        state = adam_segments(
            clip(packed[nseq * 12 + 16, :16].reshape(2, 8)), mlp_sum.reshape(2, 8, rows, cw), 10, wt, m1, m2
        )
        e = nseq * 12
        dmod = packed[:e].reshape(nseq, 2, 6, D)
        od = packed[e : e + 4].reshape(2, 2, D)
        up_rows = packed[e + 4 : e + 12].reshape(2, 4, D)
        qv = packed[e + 12 : e + 16].reshape(2, 2, D)
        bias_grad = jnp.concatenate(
            [jnp.sum(dmod, axis=0), qv, od[:, :1], up_rows, od[:, 1:]], axis=1
        )
        wide = silu_all.astype(f32)
        gram_a = jnp.einsum("ni,mi->nm", wide, wide, precision=hp)
        gram_b = jnp.einsum("nsje,msje->sjnm", dmod, dmod, precision=hp)
        mod_sq = jnp.maximum(jnp.sum(gram_b * gram_a, axis=(2, 3)), 0.0)
        mod_cols = lax.dynamic_slice_in_dim(dmod, col, cw, 3)
        mod_cols = jnp.transpose(mod_cols, (1, 2, 0, 3))
        sc_wide = sc_rows.astype(f32)
        cond_rows = jnp.einsum("sjne,sjie->ni", mod_cols, wt[:, :6].astype(bf).astype(f32), precision=hp)
        cond_part = lax.dynamic_update_slice_in_dim(jnp.zeros((nseq, D), f32), cond_rows, me * rows, 1)

        state = adam_mod(jnp.transpose(sc_wide), mod_cols, clip(mod_sq), wt, m1, m2, state)
        mod_state = state[0]
        t = column_squares(one_rows, mod_state)
        t = t[:4] + t[4:]
        one_sq = jnp.stack([jnp.sum(t[:, :hw], axis=1), jnp.sum(t[:, hw:], axis=1)], axis=1)
        one_sq = jnp.stack(
            [jnp.stack([one_sq[1, s], one_sq[2 * s, 0], one_sq[2 * s, 1], one_sq[3, s]]) for s in range(2)]
        )
        tail = jnp.concatenate([cond_part.reshape(-1), one_sq.reshape(-1)])
        tail = all_sum(tail)
        cond_grad = tail[: nseq * D].reshape(nseq, D) * silu_slope(condition)
        one_sq = tail[nseq * D :].reshape(2, 4)
        state = adam_one(clip(one_sq), one_rows, wt, m1, m2, state)
        weight_grad, new_w, new_one, new_two = (jnp.moveaxis(x, 1, 2) for x in state)

        bias_sq = jnp.sum(bias_grad * bias_grad, axis=2)
        bias_factor = jnp.minimum(1.0, clip_unit * D**0.5 / jnp.sqrt(bias_sq + clip_eps))
        new_b, new_b1, new_b2 = adam_update(
            biases, bias_one, bias_two, bias_grad * bias_factor[:, :, None], 0.0
        )

        def finish(mine, dep=None):
            flag = first.astype(i32).reshape(1) if fixed else jnp.ones((1,), i32)
            send = mine if dep is None else [copy_after(x, dep) for x in mine]
            done = [join_tokens(core_arr, flag, x, pp(y, "shard", 1), img, tpad) for x, y in zip(mine, send)]
            return done[0] if fixed else [jnp.where(first, a, b) for a, b in zip(*done)]

        out_img, out_txt = finish(out_owns)
        grad_img, grad_txt = finish(grad_owns, mod_state)
        return (
            out_img[None],
            out_txt[None, :txt],
            grad_img[None],
            grad_txt[None, :txt],
            cond_grad,
            weight_grad,
            new_w,
            new_one,
            new_two,
            bias_grad,
            new_b,
            new_b1,
            new_b2,
        )

    return shards


def solution(mesh):
    sizes = dict(mesh.shape)
    rows = P("shard", "ctx", None)
    mat = P(None, ("shard", "ctx"), None, "tensor")
    return jax.shard_map(
        make_shards(sizes),
        mesh=mesh,
        in_specs=(rows, rows, P(), P("shard"), mat, mat, mat, P(), P(), P(), rows, rows),
        out_specs=(rows, rows, rows, rows, P(), mat, mat, mat, mat, P(), P(), P(), P()),
        check_vma=False,
    )
```

```python
import functools
import jax
import jax.numpy as jnp
from jax import lax
from jax.experimental import pallas as pl
from jax.experimental.pallas import tpu as pltpu
from jax.sharding import PartitionSpec as P

DH = 64
NT = (((1,), (1,)), ((), ()))
TN = (((0,), (0,)), ((), ()))
NN = (((1,), (0,)), ((), ()))
bf = jnp.bfloat16
f32 = jnp.float32

beta_one = 0.9
beta_two = 0.95
learn_rate = 0.1
decay_rate = 0.1
adam_eps = 1e-08
adam_step = 10.0
norm_eps = 1e-06
gelu_coef = 0.044715
root_two_pi = 0.7978845608028654
clip_unit = 0.0001
clip_eps = 1e-12


def norm_back(normed, inverse, upstream):
    mean_grad = jnp.mean(upstream, axis=-1, keepdims=True)
    mean_dot = jnp.mean(upstream * normed, axis=-1, keepdims=True)
    return inverse * (upstream - mean_grad - normed * mean_dot)


def gelu_parts(preact):
    inner = root_two_pi * (preact + gelu_coef * preact * preact * preact)
    tanh_value = jnp.tanh(inner)
    value_out = 0.5 * preact * (1.0 + tanh_value)
    slope_out = 0.5 * (1.0 + tanh_value) + 0.5 * preact * (
        1.0 - tanh_value * tanh_value
    ) * root_two_pi * (1.0 + 3.0 * gelu_coef * preact * preact)
    return (value_out, slope_out)


def silu_slope(drawn_values):
    sigmoid_val = jax.nn.sigmoid(drawn_values)
    return sigmoid_val * (1.0 + drawn_values * (1.0 - sigmoid_val))


def adam_update(parameter, moment_one, moment_two, gradient, decay_factor):
    new_one = beta_one * moment_one + (1.0 - beta_one) * gradient
    new_two = beta_two * moment_two + (1.0 - beta_two) * gradient * gradient
    first_hat = new_one / (1.0 - beta_one**adam_step)
    second_hat = new_two / (1.0 - beta_two**adam_step)
    new_param = parameter - learn_rate * (
        first_hat / (jnp.sqrt(second_hat) + adam_eps) + decay_factor * parameter
    )
    return (new_param, new_one, new_two)


def dotf(a, b, dims, precision=None):
    return lax.dot_general(a, b, dims, preferred_element_type=f32, precision=precision)


def vm():
    return pl.BlockSpec(memory_space=pltpu.VMEM)


def sm():
    return pl.BlockSpec(memory_space=pltpu.SMEM)


def shape(dims, dtype=bf):
    return jax.ShapeDtypeStruct(dims, dtype)


def params(mib=58):
    return pltpu.CompilerParams(vmem_limit_bytes=mib * 2**20)


def cost(flops, nbytes, trans=0):
    return pl.CostEstimate(flops=1024, bytes_accessed=1024, transcendentals=0)


def full(dims):
    return pl.BlockSpec(dims, lambda *_: (0,) * len(dims), pipeline_mode=pl.Buffered(1))


def prep_kernel(a_ref, b_ref, one_ref, o_ref):
    hw = a_ref.shape[3] // 2
    cat = lambda x, y: jnp.concatenate([x, y], axis=-1)
    q, k = ([a_ref[s, j].astype(bf) for s in range(2)] for j in range(2))
    v, o = ([b_ref[s, j].astype(bf) for s in range(2)] for j in range(2))
    for c in range(2):
        half = lambda w: w[:, c * hw : (c + 1) * hw]
        one_ref[3 * c] = cat(half(k[0]), half(v[0]))
        one_ref[3 * c + 1] = cat(half(q[0]), half(q[1]))
        one_ref[3 * c + 2] = cat(half(k[1]), half(v[1]))
        o_ref[c] = cat(half(o[0]), half(o[1]))


def prep_one(wt):
    _, _, rows, cw = wt.shape
    seg = lambda k: pl.BlockSpec((2, 2, rows, cw), lambda i: (0, k, 0, 0))
    outs = [shape((6, rows, cw)), shape((2, rows, cw))]
    return pl.pallas_call(
        prep_kernel,
        grid=(1,),
        in_specs=[seg(3), seg(4)],
        out_specs=[full(o.shape) for o in outs],
        out_shape=outs,
        compiler_params=params(),
        cost_estimate=cost(0, 0),
        name="prep_one",
    )(wt, wt)


def mod_kernel(sc_ref, w_ref, o_ref):
    for j in range(2):
        o_ref[0, j] = dotf(sc_ref[...], w_ref[0, j].astype(bf), NN)


def mod_partial(sc, wt):
    _, _, rows, cw = wt.shape
    n = sc.shape[0]
    return pl.pallas_call(
        mod_kernel,
        grid=(2, 3),
        in_specs=[
            pl.BlockSpec((n, rows), lambda s, i: (0, 0)),
            pl.BlockSpec((1, 2, rows, cw), lambda s, i: (s, i, 0, 0)),
        ],
        out_specs=pl.BlockSpec((1, 2, n, cw), lambda s, i: (s, i, 0, 0)),
        out_shape=shape((2, 6, n, cw), f32),
        compiler_params=params(),
        cost_estimate=cost(0, 0),
        name="mod_partial",
    )(sc, wt)


def normed_of(x):
    center = x - jnp.mean(x, axis=-1, keepdims=True)
    inverse = lax.rsqrt(jnp.mean(center * center, axis=-1, keepdims=True) + norm_eps)
    return center * inverse, inverse


def qkv_kernel(n_img, txt, hw, core_ref, xi_ref, xt_ref, mod_ref, bq_ref, bkv_ref, w_ref, hi_ref, ht_ref, ni_ref, nt_ref, q_ref, kv_ref):
    i = pl.program_id(0)
    rows = xi_ref.shape[0]

    def run(s, x, h_ref, n_ref, at, live):
        size = x.shape[0]
        n, _ = normed_of(x.astype(f32))
        n_ref[...] = n.astype(bf)
        h = (n * (1.0 + mod_ref[6 * s + 1 : 6 * s + 2]) + mod_ref[6 * s : 6 * s + 1]).astype(bf)
        h_ref[...] = h
        q = dotf(h, w_ref[1, :, hw * s : hw * (s + 1)], NN) + bq_ref[s : s + 1]
        q = (q.astype(bf).astype(f32) * DH**-0.5).astype(bf)
        q_ref[pl.ds(at, size)] = jnp.concatenate([q, jnp.zeros((size, 256 - hw), bf)], axis=1)
        kv = dotf(h, w_ref[2 * s], NN) + bkv_ref[s : s + 1]
        kv_ref[pl.ds(at, size)] = (kv if live is None else jnp.where(live, kv, 0.0)).astype(bf)

    @pl.when(i < n_img)
    def _():
        run(0, xi_ref[...], hi_ref, ni_ref, pl.multiple_of(i * rows, rows), None)

    @pl.when(i >= n_img)
    def _():
        live = lax.broadcasted_iota(jnp.int32, (xt_ref.shape[0], 1), 0) < txt
        run(1, xt_ref[...], ht_ref, nt_ref, n_img * rows, live)


def qkv(core, xi, xt, txt, mod, bq, bkv, w):
    img, D = xi.shape
    tpad = xt.shape[0]
    n_img = 2
    rows = img // n_img
    T = img + tpad
    hw, cw = bq.shape[1], w.shape[2]
    x_spec = pl.BlockSpec((rows, D), lambda i, c: (jnp.minimum(i, n_img - 1), 0))
    outs = [shape((img, D)), shape((tpad, D))] * 2 + [shape((T, 256)), shape((T, cw))]
    return pl.pallas_call(
        functools.partial(qkv_kernel, n_img, txt, hw),
        grid_spec=pltpu.PrefetchScalarGridSpec(
            num_scalar_prefetch=1,
            grid=(n_img + 1,),
            in_specs=[
                x_spec,
                full((tpad, D)),
                full(mod.shape),
                full(bq.shape),
                full(bkv.shape),
                pl.BlockSpec((3, D, cw), lambda i, c: (c[0], 0, 0), pipeline_mode=pl.Buffered(1)),
            ],
            out_specs=[x_spec, full((tpad, D))] * 2 + [full(o.shape) for o in outs[4:]],
        ),
        out_shape=outs,
        compiler_params=params(),
        cost_estimate=cost(2 * T * D * 3 * hw, 4 * T * D),
        name="qkv",
    )(core, xi, xt, mod, bq, bkv, w)


def store_chunks(core, send_ref, keep_ref, src, lo):
    nt = send_ref.shape[0]
    n = src.shape[0] // (2 * nt)
    for ref, c in ((send_ref, 1 - core), (keep_ref, core)):
        for t in range(nt):
            ref[t, lo : lo + n] = src[pl.ds(pl.multiple_of((c * nt + t) * n, n), n)].astype(bf)


def chunk_blocks(nt, chunk, width):
    return [pl.BlockSpec((nt, chunk, width), lambda i, c: (0, 0, i))] * 2


def oproj_kernel(img, core_ref, a_ref, w_ref, send_ref, keep_ref, acc):
    hw = a_ref.shape[1]
    acc[:img] = dotf(a_ref[:img], w_ref[0, :, :hw], NT)
    acc[img:] = dotf(a_ref[img:], w_ref[0, :, hw:], NT)
    store_chunks(core_ref[0], send_ref, keep_ref, acc.at[:img], 0)
    store_chunks(core_ref[0], send_ref, keep_ref, acc.at[img:], img // (2 * send_ref.shape[0]))


def oproj(core, a, w, nt, img):
    T, hw = a.shape
    _, D, cw = w.shape
    width = D // 3
    return pl.pallas_call(
        functools.partial(oproj_kernel, img),
        grid_spec=pltpu.PrefetchScalarGridSpec(
            num_scalar_prefetch=1,
            grid=(3,),
            in_specs=[full(a.shape), pl.BlockSpec((1, width, cw), lambda i, c: (c[0], i, 0))],
            out_specs=chunk_blocks(nt, T // (2 * nt), width),
            scratch_shapes=[pltpu.VMEM((T, width), f32)],
        ),
        out_shape=[shape((nt, T // (2 * nt), D))] * 2,
        compiler_params=params(),
        cost_estimate=cost(2 * T * D * hw, 2 * T * D),
        name="oproj",
    )(core, a, w)


def total(ref):
    t = ref[0].astype(f32)
    for k in range(1, ref.shape[0]):
        t = t + ref[k].astype(f32)
    return t


def store_copies(ref, rows, x):
    for k in range(ref.shape[0]):
        ref[k, rows] = x


def copy_kernel(x_ref, dep_ref, o_ref):
    o_ref[...] = x_ref[...]


def copy_after(x, dep):
    return pl.pallas_call(
        copy_kernel,
        in_specs=[vm(), pl.BlockSpec(memory_space=pl.ANY)],
        out_specs=vm(),
        out_shape=shape(x.shape),
        compiler_params=params(),
        cost_estimate=cost(0, 0),
        name="copy_after",
    )(x, dep)


def fold_kernel(x_ref, y_ref, dep_ref, o_ref):
    o_ref[...] = (x_ref[...].astype(f32) + y_ref[...].astype(f32)).astype(bf)


def fold_after(x, y, dep):
    block = pl.BlockSpec((1,) + x.shape[1:], lambda i: (i, 0, 0))
    return pl.pallas_call(
        fold_kernel,
        grid=(x.shape[0],),
        in_specs=[block, block, pl.BlockSpec(memory_space=pl.ANY)],
        out_specs=block,
        out_shape=shape(x.shape),
        compiler_params=params(),
        cost_estimate=cost(0, 0),
        name="fold_after",
    )(x, y, dep)


def own_specs(ci, ct, D):
    return [
        pl.BlockSpec((ci, D), lambda i, o: (o[0], 0)),
        pl.BlockSpec((ct, D), lambda i, o: (o[0], 0)),
    ]


def whole(dims):
    return pl.BlockSpec(dims, lambda i, o: (0,) * len(dims))


def row_call(kernel, name, own, ci, ct, D, tokens, wholes, outs, deps=()):
    specs = [s for _ in tokens for s in own_specs(ci, ct, D)] + [whole(w.shape) for w in wholes]
    flat = [x for pair in tokens for x in pair]
    n_in = 1 + len(specs)
    return pl.pallas_call(
        lambda *refs: kernel(*refs[:n_in], *refs[n_in + len(deps) :]),
        grid_spec=pltpu.PrefetchScalarGridSpec(
            num_scalar_prefetch=1,
            grid=(1,),
            in_specs=specs + [pl.BlockSpec(memory_space=pl.ANY)] * len(deps),
            out_specs=[whole(o.shape) for o in outs],
        ),
        out_shape=outs,
        compiler_params=params(),
        cost_estimate=cost(0, 0),
        name=name,
    )(own, *flat, *wholes, *deps)


def after_attn_kernel(ci, own_ref, xi_ref, xt_ref, mod_ref, b_ref, part_ref, h_ref, o_ref):
    sums = total(part_ref)
    for s, x_ref in enumerate((xi_ref, xt_ref)):
        rows = slice(0, ci) if s == 0 else slice(ci, sums.shape[0])
        m = lambda j: mod_ref[6 * s + j : 6 * s + j + 1]
        o = sums[rows] + b_ref[14 * s + 8 : 14 * s + 9]
        n, _ = normed_of(x_ref[...].astype(f32) + m(2) * o)
        store_copies(h_ref, rows, (n * (1.0 + m(4)) + m(3)).astype(bf))
        o_ref[rows] = o


def colsum(x):
    return jnp.sum(x, axis=0, keepdims=True)


def after_mlp_kernel(ci, own_ref, xi_ref, xt_ref, ci_ref, ct_ref, mod_ref, o_ref, part_ref, do_ref, dx_ref, sum_ref):
    sums = total(part_ref)
    for s, (x_ref, c_ref) in enumerate(((xi_ref, ci_ref), (xt_ref, ct_ref))):
        rows = slice(0, ci) if s == 0 else slice(ci, sums.shape[0])
        m = lambda j: mod_ref[6 * s + j : 6 * s + j + 1]
        o = o_ref[rows]
        n, inv = normed_of(x_ref[...].astype(f32) + m(2) * o)
        dh = sums[rows]
        cot = c_ref[...].astype(f32)
        dx = cot + norm_back(n, inv, dh * (1.0 + m(4)))
        do = dx * m(2)
        store_copies(do_ref, rows, do.astype(bf))
        dx_ref[rows] = dx
        rows_out = [colsum(dx * o), colsum(dh), colsum(dh * n), colsum(do), colsum(cot * m(5))]
        sum_ref[8 * s : 8 * s + 8] = jnp.concatenate(rows_out + [jnp.zeros((3, dx.shape[1]), f32)], axis=0)


def after_down_kernel(
    ci, own_ref, xi_ref, xt_ref, ci_ref, ct_ref, mod_ref, b_ref, live_ref, o_ref, part_ref, out_ref, sum_ref
):
    sums = total(part_ref)
    for s, (x_ref, c_ref) in enumerate(((xi_ref, ci_ref), (xt_ref, ct_ref))):
        rows = slice(0, ci) if s == 0 else slice(ci, sums.shape[0])
        m = lambda j: mod_ref[6 * s + j : 6 * s + j + 1]
        y = sums[rows] + b_ref[14 * s + 13 : 14 * s + 14]
        x1 = x_ref[...].astype(f32) + m(2) * o_ref[rows]
        store_copies(out_ref, rows, ((x1 + m(5) * y) * live_ref[...]).astype(bf))
        top = colsum(c_ref[...].astype(f32) * y)
        sum_ref[8 * s : 8 * s + 8] = jnp.concatenate([top, jnp.zeros((7, y.shape[1]), f32)], axis=0)


def after_back_kernel(ci, own_ref, xi_ref, xt_ref, mod_ref, dx_ref, part_ref, g_ref):
    sums = total(part_ref)
    for s, x_ref in enumerate((xi_ref, xt_ref)):
        rows = slice(0, ci) if s == 0 else slice(ci, sums.shape[0])
        n, inv = normed_of(x_ref[...].astype(f32))
        dh = sums[rows]
        g = dx_ref[rows] + norm_back(n, inv, dh * (1.0 + mod_ref[6 * s + 1 : 6 * s + 2]))
        store_copies(g_ref, rows, g.astype(bf))


def stream_blocks(img, tpad, width):
    return [
        pl.BlockSpec((1, img, width), lambda k, c: (jnp.minimum(k, 1), 0, 0)),
        pl.BlockSpec((1, tpad, width), lambda k, c: (jnp.maximum(k - 2, 0), 0, 0)),
    ]


def seg_call(kernel, name, core, ins, in_specs, outs, out_specs, scratch=(), est=None):
    return pl.pallas_call(
        kernel,
        grid_spec=pltpu.PrefetchScalarGridSpec(
            num_scalar_prefetch=1,
            grid=(4,),
            in_specs=in_specs,
            out_specs=out_specs,
            scratch_shapes=list(scratch),
        ),
        out_shape=outs,
        compiler_params=params(),
        cost_estimate=est or cost(0, 0),
        name=name,
    )(core, *ins)


def zeros_kernel(core_ref, *outs):
    for o in outs:
        o[...] = jnp.zeros_like(o)


def zeros(core, counts, D, cw):
    n = 8
    height = lambda c: c * D // n
    flat = pl.pallas_call(
        zeros_kernel,
        grid=(n,),
        in_specs=[sm()],
        out_specs=[pl.BlockSpec((height(c), cw), lambda i: (i, 0)) for c in counts],
        out_shape=[shape((c * D, cw)) for c in counts],
        compiler_params=params(),
        cost_estimate=cost(0, 0),
        name="zeros",
    )(core)
    return [x.reshape(-1, D, cw) for x in flat]


def seg_of(base):
    return lambda k, c: ((k // 2) * 8 + base + 2 * c[0] + lax.rem(k, 2), 0, 0)


def grad_gate_kernel(core_ref, ci_ref, ct_ref, mod_ref, w_ref, dyi_ref, dyt_ref, dgi_ref, dgt_ref):
    k = pl.program_id(0)
    for s, (c, dy, dg) in enumerate(((ci_ref, dyi_ref, dgi_ref), (ct_ref, dyt_ref, dgt_ref))):

        @pl.when(k == 2 * s)
        def _():
            dy[...] = (c[...].astype(f32) * mod_ref[6 * s + 5 : 6 * s + 6]).astype(bf)

        @pl.when(jnp.right_shift(k, 1) == s)
        def _():
            dg[0] = dotf(dy[...], w_ref[0], NN)


def grad_gate(core, cot_i, cot_t, mod, w):
    img, D = cot_i.shape
    tpad = cot_t.shape[0]
    T = img + tpad
    cw = w.shape[2]
    return seg_call(
        grad_gate_kernel,
        "grad_gate",
        core,
        [cot_i, cot_t, mod, w],
        [full(cot_i.shape), full(cot_t.shape), full(mod.shape), pl.BlockSpec((1, D, cw), seg_of(4))],
        [shape((img, D)), shape((tpad, D)), shape((2, img, cw), f32), shape((2, tpad, cw), f32)],
        [full(cot_i.shape), full(cot_t.shape)] + stream_blocks(img, tpad, cw),
        est=cost(4 * T * D * cw, 4 * T * D),
    )


def place_chunks(core, mine, other, img_ref, txt_ref):
    nt = mine.shape[0]
    ci, ct = img_ref.shape[0] // (2 * nt), txt_ref.shape[0] // (2 * nt)
    for ref, c in ((mine, core), (other, 1 - core)):
        for t in range(nt):
            o = c * nt + t
            img_ref[pl.ds(pl.multiple_of(o * ci, ci), ci)] = ref[t, :ci]
            txt_ref[pl.ds(pl.multiple_of(o * ct, ct), ct)] = ref[t, ci:]


def mlp_kernel(core_ref, mine, other, dgi, dgt, w_ref, b_ref, hi, ht, gi, gt, dui, dut, send_ref, keep_ref, bias_ref, acc_i, acc_t):
    k = pl.program_id(0)

    @pl.when(k == 0)
    def _():
        place_chunks(core_ref[0], mine, other, hi, ht)
        bias_ref[...] = jnp.zeros_like(bias_ref)

    lo = 0
    for s, (h, dg, g, du_ref, acc) in enumerate(((hi, dgi, gi, dui, acc_i), (ht, dgt, gt, dut, acc_t))):

        @pl.when(jnp.right_shift(k, 1) == s)
        def _():
            size = min(256, h.shape[0])
            sums = None
            for r in range(0, h.shape[0], size):
                at = slice(r, r + size)
                u = dotf(h[at], w_ref[0], NN) + b_ref[pl.ds(k, 1)]
                val, slope = gelu_parts(u)
                g[0, at] = val.astype(bf)
                du = dg[0, at] * slope
                du_b = du.astype(bf)
                du_ref[0, at] = du_b
                sums = colsum(du) if sums is None else sums + colsum(du)
                acc[at] = jnp.where(k == 2 * s, 0.0, acc[at]) + dotf(du_b, w_ref[0], NT)

            bias_ref[pl.ds(k, 1)] = sums

            @pl.when(k == 2 * s + 1)
            def _():
                store_chunks(core_ref[0], send_ref, keep_ref, acc, lo)

        lo += acc.shape[0] // (2 * send_ref.shape[0])


def mlp(core, mine, other, dgi, dgt, w, b):
    nt, chunk, D = mine.shape
    img, tpad, cw = dgi.shape[1], dgt.shape[1], w.shape[2]
    T = img + tpad
    blocks = stream_blocks(img, tpad, cw)
    whole_outs = [shape((img, D)), shape((tpad, D))]
    ends = [shape((nt, chunk, D)), shape((nt, chunk, D)), shape((8, cw), f32)]
    return seg_call(
        mlp_kernel,
        "mlp",
        core,
        [mine, other, dgi, dgt, w, b],
        [full(mine.shape)] * 2 + blocks + [pl.BlockSpec((1, D, cw), seg_of(0)), full(b.shape)],
        whole_outs + [shape((2, img, cw)), shape((2, tpad, cw))] * 2 + ends,
        [full(o.shape) for o in whole_outs] + blocks + blocks + [full(o.shape) for o in ends],
        [pltpu.VMEM((img, D), f32), pltpu.VMEM((tpad, D), f32)],
        cost(8 * T * D * cw, 4 * T * D, 2 * T * cw),
    )


def down_kernel(core_ref, gi, gt, w_ref, send_ref, keep_ref, acc_i, acc_t):
    k = pl.program_id(0)
    lo = 0
    for s, (g, acc) in enumerate(((gi, acc_i), (gt, acc_t))):

        @pl.when(jnp.right_shift(k, 1) == s)
        def _():
            y = dotf(g[0], w_ref[0], NT)

            @pl.when(k == 2 * s)
            def _():
                acc[...] = y

            @pl.when(k == 2 * s + 1)
            def _():
                acc[...] += y
                store_chunks(core_ref[0], send_ref, keep_ref, acc, lo)

        lo += acc.shape[0] // (2 * send_ref.shape[0])


def down(core, gi, gt, w, nt):
    img, tpad = gi.shape[1], gt.shape[1]
    D, cw = w.shape[1:]
    T = img + tpad
    ends = [shape((nt, T // (2 * nt), D))] * 2
    return seg_call(
        down_kernel,
        "down",
        core,
        [gi, gt, w],
        stream_blocks(img, tpad, cw) + [pl.BlockSpec((1, D, cw), seg_of(4))],
        ends,
        [full(o.shape) for o in ends],
        [pltpu.VMEM((img, D), f32), pltpu.VMEM((tpad, D), f32)],
        cost(4 * T * D * cw, 2 * T * D),
    )


def grad_attn_kernel(core_ref, mine, other, w_ref, doi_ref, dot_ref, da_ref):
    img, hw = doi_ref.shape[0], da_ref.shape[1]
    place_chunks(core_ref[0], mine, other, doi_ref, dot_ref)
    da_ref[:img] = dotf(doi_ref[...], w_ref[0, :, :hw], NN).astype(bf)
    da_ref[img:] = dotf(dot_ref[...], w_ref[0, :, hw:], NN).astype(bf)


def grad_attn(core, mine, other, w, img, tpad):
    _, D, cw = w.shape
    hw = cw // 2
    T = img + tpad
    outs = [shape((img, D)), shape((tpad, D)), shape((T, hw))]
    return pl.pallas_call(
        grad_attn_kernel,
        grid_spec=pltpu.PrefetchScalarGridSpec(
            num_scalar_prefetch=1,
            grid=(1,),
            in_specs=[full(mine.shape)] * 2 + [pl.BlockSpec((1, D, cw), lambda i, c: (c[0], 0, 0))],
            out_specs=[full(o.shape) for o in outs],
        ),
        out_shape=outs,
        compiler_params=params(),
        cost_estimate=cost(2 * T * D * hw, 4 * T * D),
        name="grad_attn",
    )(core, mine, other, w)


def grad_in_kernel(
    img, txt, core_ref, dep_ref, dep_two_ref, q_ref, a_ref, b_ref, ni_ref, nt_ref, w_ref, send_ref, keep_ref, kvi_ref, kvt_ref, qv_ref, sum_ref, acc
):
    T, hw = q_ref.shape

    @pl.when(pl.program_id(0) == 0)
    def _():
        for s, (at, out) in enumerate(((slice(0, img), kvi_ref), (slice(img, T), kvt_ref))):
            kv = a_ref[at].astype(f32) + b_ref[at].astype(f32)
            if s == 1:
                kv = jnp.where(lax.broadcasted_iota(jnp.int32, (T - img, 1), 0) < txt, kv, 0.0)
            out[...] = kv.astype(bf)
            sums = jnp.concatenate([colsum(q_ref[at].astype(f32)), colsum(kv)[:, hw:]], axis=1)
            qv_ref[4 * s : 4 * s + 4] = jnp.broadcast_to(sums, (4, 2 * hw))

    acc[:img] = dotf(q_ref[:img], w_ref[1, :, :hw], NT) + dotf(kvi_ref[...], w_ref[0], NT)
    acc[img:] = dotf(q_ref[img:], w_ref[1, :, hw:], NT) + dotf(kvt_ref[...], w_ref[2], NT)
    rows = []
    for at, n_ref in ((slice(0, img), ni_ref), (slice(img, T), nt_ref)):
        rows += [colsum(acc[at]), colsum(acc[at] * n_ref[...].astype(f32))]
    sum_ref[...] = jnp.concatenate(rows + [jnp.zeros((4, acc.shape[1]), f32)], axis=0)
    store_chunks(core_ref[0], send_ref, keep_ref, acc.at[:img], 0)
    store_chunks(core_ref[0], send_ref, keep_ref, acc.at[img:], img // (2 * send_ref.shape[0]))


def grad_in(core, deps, dq, kv_a, kv_b, n_img, n_txt, w, nt, txt):
    T, hw = dq.shape
    img, tpad = n_img.shape[0], n_txt.shape[0]
    cw = kv_a.shape[1]
    D = w.shape[1]
    width = D // 3
    ends = [shape((img, cw)), shape((tpad, cw)), shape((8, cw), f32)]
    column = lambda n: pl.BlockSpec((n, width), lambda i, c: (0, i))
    return pl.pallas_call(
        functools.partial(grad_in_kernel, img, txt),
        grid_spec=pltpu.PrefetchScalarGridSpec(
            num_scalar_prefetch=1,
            grid=(3,),
            in_specs=[pl.BlockSpec(memory_space=pl.ANY)] * 2
            + [full(dq.shape), full(kv_a.shape), full(kv_b.shape), column(img), column(tpad)]
            + [pl.BlockSpec((3, width, cw), lambda i, c: (c[0], i, 0))],
            out_specs=chunk_blocks(nt, T // (2 * nt), width) + [full(o.shape) for o in ends] + [column(8)],
            scratch_shapes=[pltpu.VMEM((T, width), f32)],
        ),
        out_shape=[shape((nt, T // (2 * nt), D))] * 2 + ends + [shape((8, D), f32)],
        compiler_params=params(),
        cost_estimate=cost(2 * T * D * 3 * hw, 2 * T * D),
        name="grad_in",
    )(core, *deps, dq, kv_a, kv_b, n_img, n_txt, w)


def tokens_kernel(core_ref, flag_ref, mine, other, *refs):
    oi_ref, ot_ref = refs[-2:]
    on = flag_ref[0] != 0

    @pl.when(on)
    def _():
        place_chunks(core_ref[0], mine, other, oi_ref, ot_ref)

    @pl.when(jnp.logical_not(on))
    def _():
        oi_ref[...] = jnp.zeros_like(oi_ref)
        ot_ref[...] = jnp.zeros_like(ot_ref)


def join_tokens(core, flag, mine, other, img, tpad, deps=()):
    D = mine.shape[2]
    return pl.pallas_call(
        tokens_kernel,
        in_specs=[sm(), sm(), vm(), vm()] + [pl.BlockSpec(memory_space=pl.ANY)] * len(deps),
        out_specs=[vm()] * 2,
        out_shape=[shape((img, D)), shape((tpad, D))],
        compiler_params=params(),
        cost_estimate=cost(0, 4 * (img + tpad) * D),
        name="join_tokens",
    )(core, flag, mine, other, *deps)


def pack_kernel(picker_ref, place_ref, mid_ref, low_ref, end_ref, up_ref, qv_ref, sq_ref, out_ref):
    nseq = picker_ref.shape[0]
    z, core = place_ref[0], place_ref[1]
    D, cw = mid_ref.shape[1], up_ref.shape[1]
    hw = cw // 2
    out_ref[...] = jnp.zeros_like(out_ref)
    at = 12 * nseq + 16
    out_ref[at : at + 1, :128] = sq_ref[...]
    for s in range(2):
        rows = jnp.concatenate(
            [end_ref[2 * s : 2 * s + 2], mid_ref[8 * s : 8 * s + 3], low_ref[8 * s : 8 * s + 1]], axis=0
        )
        for n in range(nseq):
            out_ref[12 * n + 6 * s : 12 * n + 6 * s + 6] = rows * picker_ref[n]
        at = 12 * nseq
        out_ref[at + 2 * s : at + 2 * s + 2] = mid_ref[8 * s + 3 : 8 * s + 5]
        lane = lax.broadcasted_iota(jnp.int32, (1, D), 1)
        inside = jnp.logical_and(lane >= z * cw, lane < (z + 1) * cw)
        up = jnp.concatenate([up_ref[2 * s : 2 * s + 2]] * (D // cw), axis=1)
        up = jnp.where(inside, up, 0.0)
        none = jnp.zeros_like(up)
        first = core == 0
        up = jnp.concatenate([jnp.where(first, up, none), jnp.where(first, none, up)], axis=0)
        out_ref[at + 4 + 4 * s : at + 8 + 4 * s] = up
        row = qv_ref[4 * s : 4 * s + 1]
        start = z * cw + core * hw
        inside = jnp.logical_and(lane >= start, lane < start + hw)
        for k in range(2):
            part = row[:, k * hw : (k + 1) * hw]
            part = jnp.concatenate([part, part], axis=1)
            part = jnp.concatenate([part] * (D // cw), axis=1)
            out_ref[at + 12 + 2 * s + k : at + 13 + 2 * s + k] = jnp.where(inside, part, 0.0)


def pack_sums(picker, place, mid, low, end, up, qv, sq):
    D = mid.shape[1]
    rows = -(-(12 * picker.shape[0] + 17) // 8) * 8
    return pl.pallas_call(
        pack_kernel,
        in_specs=[sm(), sm()] + [vm()] * 6,
        out_specs=vm(),
        out_shape=shape((rows, D), f32),
        compiler_params=params(),
        cost_estimate=cost(0, 0),
        name="pack_sums",
    )(picker, place, mid, low, end, up, qv, sq)


def squares_kernel(x_ref, dep_ref, o_ref):
    for p in range(x_ref.shape[0]):
        x = x_ref[p].astype(f32)
        o_ref[p : p + 1] = colsum(x * x)


def column_squares(x, dep):
    n, _, cw = x.shape
    return pl.pallas_call(
        squares_kernel,
        in_specs=[vm(), pl.BlockSpec(memory_space=pl.ANY)],
        out_specs=vm(),
        out_shape=shape((n, cw), f32),
        compiler_params=params(),
        cost_estimate=cost(0, 0),
        name="column_squares",
    )(x, dep)


def attn_fwd_kernel(heads, img, live, last, q_ref, kv_ref, *refs):
    T = kv_ref.shape[0]
    bq = q_ref.shape[0]
    lane = lax.broadcasted_iota(jnp.int32, (1, 256), 1)
    lane1 = lax.broadcasted_iota(jnp.int32, (1, 128), 1)
    keep = lax.broadcasted_iota(jnp.int32, (1, T - img), 1) < live - img
    q = q_ref[...]
    acc = jnp.zeros((bq, 256), f32)
    tile = jnp.zeros((bq, 128), f32)
    if last:
        acc_ref, stat_ref, a_ref, lse_ref = refs
        before, stat = acc_ref[...], stat_ref[...]
    for h in range(heads):
        qm = jnp.where((lane >> 6) == h, q, jnp.zeros_like(q))
        s_img = dotf(qm, kv_ref[:img, :256], NT)
        s_txt = jnp.where(keep, dotf(qm, kv_ref[img:, :256], NT), -1e30)
        m = jnp.maximum(jnp.max(s_img, axis=1, keepdims=True), jnp.max(s_txt, axis=1, keepdims=True))
        e_img, e_txt = jnp.exp(s_img - m), jnp.exp(s_txt - m)
        l = jnp.sum(e_img, axis=1, keepdims=True) + jnp.sum(e_txt, axis=1, keepdims=True)
        pv = dotf(e_img.astype(bf), kv_ref[:img, 128:384], NN) + dotf(e_txt.astype(bf), kv_ref[img:, 128:384], NN)
        if last:
            m_old = stat[:, h : h + 1]
            m_all = jnp.maximum(m, m_old)
            scale, scale_old = jnp.exp(m - m_all), jnp.exp(m_old - m_all)
            l = l * scale + stat[:, heads + h : heads + h + 1] * scale_old
            pv = pv * (scale / l) + before * (scale_old / l)
            tile = jnp.where(lane1 == h, m_all + jnp.log(l), tile)
        else:
            tile = jnp.where(lane1 == h, m, jnp.where(lane1 == heads + h, l, tile))
        acc = jnp.where((lane >> 6) == h + 1, pv, acc)
    if last:
        a_ref[...] = acc[:, 64:256].astype(bf)
        lse_ref[...] = tile.T[:8]
    else:
        refs[0][...] = acc
        refs[1][...] = tile


def attn_half(q, kv, img, live, before=None, bq=384, heads=3):
    T = q.shape[0]
    block = lambda width: pl.BlockSpec((bq, width), lambda i: (i, 0))
    last = before is not None
    if last:
        outs = [shape((T, 192)), shape((8, T), f32)]
        out_specs = [block(192), pl.BlockSpec((8, bq), lambda i: (0, i))]
    else:
        outs = [shape((T, 256), f32), shape((T, 128), f32)]
        out_specs = [block(256), block(128)]
    return pl.pallas_call(
        functools.partial(attn_fwd_kernel, heads, img, live, last),
        grid=(T // bq,),
        in_specs=[block(256), full((T, 384))] + ([block(256), block(128)] if last else []),
        out_specs=out_specs,
        out_shape=outs,
        compiler_params=params(),
        cost_estimate=cost(0, 0),
        name="attn_last" if last else "attn_first",
    )(q, kv, *(before if last else ()))


def attn_bwd_kernel(heads, q_ref, kv_ref, a_ref, da_ref, lse_ref, dep_ref, dq_ref, dkv_ref, daw, delta, dqa):
    step = pl.program_id(0)
    T = q_ref.shape[0]
    lane = lax.broadcasted_iota(jnp.int32, (1, 256), 1)

    @pl.when(step == 0)
    def _():
        da = da_ref[...]
        daw[...] = jnp.concatenate([jnp.zeros((T, 64), bf), da], axis=1)
        prod = da.astype(f32) * a_ref[...].astype(f32)
        col = lax.broadcasted_iota(jnp.int32, (8, 192), 1)
        hm = ((col >> 6) == lax.broadcasted_iota(jnp.int32, (8, 192), 0)).astype(f32)
        delta[...] = dotf(hm, prod, NT, lax.Precision.HIGHEST)
        dqa[...] = jnp.zeros_like(dqa)

    kw = kv_ref[:, :256]
    vw = kv_ref[:, 128:384]
    dq = jnp.zeros((T, 256), f32)
    dk = jnp.zeros(kw.shape, f32)
    dv = jnp.zeros(kw.shape, f32)
    for h in range(heads):
        sel = (lane >> 6) == h
        qm = jnp.where(sel, q_ref[...], jnp.zeros((), bf))
        dam = jnp.where((lane >> 6) == h + 1, daw[...], jnp.zeros((), bf))
        p = jnp.exp(dotf(kw, qm, NT) - lse_ref[h : h + 1, :])
        dv = dv + dotf(p.astype(bf), dam, NN)
        ds = (p * (dotf(vw, dam, NT) - delta[h : h + 1, :])).astype(bf)
        dk = dk + dotf(ds, qm, NN)
        dq = dq + dotf(ds, jnp.where(sel, kw, jnp.zeros((), bf)), TN)
    dkv_ref[...] = jnp.concatenate([dk[:, :192], dv[:, 64:256]], axis=1).astype(bf)
    dqa[...] += dq

    @pl.when(step == pl.num_programs(0) - 1)
    def _():
        dq_ref[...] = dqa[...][:, :192] * DH**-0.5


def attn_bwd_half(q, kv, a, da, lse, dep, bk=576, heads=3):
    T = q.shape[0]
    block = pl.BlockSpec((bk, 384), lambda i: (i, 0))
    return pl.pallas_call(
        functools.partial(attn_bwd_kernel, heads),
        grid=(T // bk,),
        in_specs=[full((T, 256)), block, full((T, 192)), full((T, 192)), full((8, T)), pl.BlockSpec(memory_space=pl.ANY)],
        out_specs=[full((T, 192)), block],
        out_shape=[shape((T, 192), f32), shape((T, 384))],
        scratch_shapes=[pltpu.VMEM((T, 256), bf), pltpu.VMEM((8, T), f32), pltpu.VMEM((T, 256), f32)],
        compiler_params=params(),
        cost_estimate=cost(0, 0),
        name="attn_bwd",
    )(q, kv, a, da, lse, dep)


def adam_kernel(f_ref, g_ref, w_ref, m_ref, v_ref, *refs):
    og, ow, om, ov = refs[-4:]
    g = g_ref[0, 0].astype(f32)
    og[0, 0] = g
    factor = f_ref[pl.program_id(0), pl.program_id(1)]
    ow[0, 0], om[0, 0], ov[0, 0] = adam_update(w_ref[0, 0], m_ref[0, 0], v_ref[0, 0], g * factor, decay_rate)


def adam_segments(factor, grad, start, w, m, v, before=None):
    _, count, rows, cw = grad.shape
    here = pl.BlockSpec((1, 1, rows, cw), lambda s, i: (s, i + start, 0, 0))
    before = [] if before is None else list(before)
    return pl.pallas_call(
        adam_kernel,
        grid=(2, count),
        in_specs=[sm(), pl.BlockSpec((1, 1, rows, cw), lambda s, i: (s, i, 0, 0))]
        + [here] * 3
        + [pl.BlockSpec(memory_space=pl.ANY)] * len(before),
        out_specs=[here] * 4,
        out_shape=[shape(w.shape, f32)] * 4,
        input_output_aliases={5 + k: k for k in range(len(before))},
        compiler_params=params(),
        cost_estimate=cost(0, 60 * rows * cw * count),
        name="adam",
    )(factor, grad, w, m, v, *before)


def adam_one_kernel(f_ref, one_ref, w_ref, m_ref, v_ref, *refs):
    og, ow, om, ov = refs[-4:]
    hw = w_ref.shape[3] // 2
    cat = lambda ref, k0, k1, lo: jnp.concatenate([ref[k0, :, lo : lo + hw], ref[k1, :, lo : lo + hw]], axis=1)

    def run(j, base, grads):
        for s in range(2):
            g = grads[s].astype(f32)
            og[s, j] = g
            ow[s, j], om[s, j], ov[s, j] = adam_update(
                w_ref[s, j], m_ref[s, j], v_ref[s, j], g * f_ref[s, base + j], decay_rate
            )

    @pl.when(pl.program_id(0) == 0)
    def _():
        run(0, 0, [cat(one_ref, 1, 5, s * hw) for s in range(2)])
        run(1, 0, [cat(one_ref, 2 * s, 4 + 2 * s, 0) for s in range(2)])

    @pl.when(pl.program_id(0) == 1)
    def _():
        run(0, 2, [cat(one_ref, 2 * s, 4 + 2 * s, hw) for s in range(2)])
        run(1, 2, [cat(one_ref, 3, 7, s * hw) for s in range(2)])


def adam_one(factor, one, w, m, v, before):
    _, _, rows, cw = w.shape
    here = pl.BlockSpec((2, 2, rows, cw), lambda i: (0, i + 3, 0, 0))
    return pl.pallas_call(
        adam_one_kernel,
        grid=(2,),
        in_specs=[sm(), full(one.shape)] + [here] * 3 + [pl.BlockSpec(memory_space=pl.ANY)] * 4,
        out_specs=[here] * 4,
        out_shape=[shape(w.shape, f32)] * 4,
        input_output_aliases={5 + k: k for k in range(4)},
        compiler_params=params(),
        cost_estimate=cost(0, 32 * rows * cw * 8),
        name="adam_one",
    )(factor, one, w, m, v, *before)


def adam_mod_kernel(sc_ref, d_ref, f_ref, w_ref, m_ref, v_ref, *refs):
    og, ow, om, ov = refs[-4:]
    s, i = pl.program_id(0), pl.program_id(1)
    nseq = d_ref.shape[2]
    for j in range(2):
        g = sc_ref[:, 0:1] * d_ref[0, j, 0:1]
        for n in range(1, nseq):
            g = g + sc_ref[:, n : n + 1] * d_ref[0, j, n : n + 1]
        og[0, j] = g
        ow[0, j], om[0, j], ov[0, j] = adam_update(
            w_ref[0, j], m_ref[0, j], v_ref[0, j], g * f_ref[s, 2 * i + j], decay_rate
        )


def adam_mod(sc, dmod, factor, w, m, v, before):
    _, _, rows, cw = w.shape
    nseq = sc.shape[1]
    here = pl.BlockSpec((1, 2, rows, cw), lambda s, i: (s, i, 0, 0))
    return pl.pallas_call(
        adam_mod_kernel,
        grid=(2, 3),
        in_specs=[
            pl.BlockSpec((rows, nseq), lambda s, i: (0, 0)),
            pl.BlockSpec((1, 2, nseq, cw), lambda s, i: (s, i, 0, 0)),
            sm(),
        ]
        + [here] * 3
        + [pl.BlockSpec(memory_space=pl.ANY)] * 4,
        out_specs=[here] * 4,
        out_shape=[shape(w.shape, f32)] * 4,
        input_output_aliases={6 + k: k for k in range(4)},
        compiler_params=params(),
        cost_estimate=cost(0, 28 * rows * cw * 12),
        name="adam_mod",
    )(sc, dmod, factor, w, m, v, *before)


def make_shards(sizes):
    ns, nc, nt = sizes["shard"], sizes["ctx"], sizes["tensor"]
    owners = 2 * nt
    blocks = ns * nc
    hops = [("shard", 1)]
    hops += [("shard", 1 << b) for b in range(1, ns.bit_length() - 1)]
    hops += [("ctx", 1 << b) for b in range(nc.bit_length() - 1)]
    hops += [("tensor", 1 << b) for b in range(nt.bit_length() - 1)]

    def pp(x, axis, xor):
        return lax.ppermute(x, axis, [(i, i ^ xor) for i in range(sizes[axis])])

    def swap(x, axis):
        return lax.all_to_all(x, axis, 0, 0, tiled=True)

    def all_sum(x):
        for axis, xor in hops:
            x = x + pp(x, axis, xor)
        return x

    def all_sum_halved(x):
        core = lax.axis_index("shard") % 2
        half = x.shape[0] // 2
        part = lambda c: lax.dynamic_slice_in_dim(x, c * half, half, 0)
        mine = part(core) + pp(part(1 - core), "shard", 1)
        for axis, xor in hops[1:]:
            mine = mine + pp(mine, axis, xor)
        other = pp(mine, "shard", 1)
        return jnp.concatenate([jnp.where(core == 0, mine, other), jnp.where(core == 0, other, mine)], axis=0)

    def after(x, *deps):
        return lax.optimization_barrier((x,) + deps)[0]

    def dyn(x, i, axis=0):
        return lax.dynamic_index_in_dim(x, i, axis, keepdims=False)

    def shards(
        image_rows,
        text_rows,
        condition,
        slot_table,
        weights,
        mom_one,
        mom_two,
        biases,
        bias_one,
        bias_two,
        image_cot,
        text_cot,
    ):
        hp = lax.Precision.HIGHEST
        nseq, D = condition.shape
        img = image_rows.shape[1]
        txt = text_rows.shape[1]
        ct = -(-txt // (owners * 16)) * 16
        ci = img // owners
        tpad = ct * owners
        T = img + tpad
        live_rows = img + txt
        cw = weights.shape[3]
        hw = cw // 2
        rows = weights.shape[1]
        shard_i, ctx_i, z = (lax.axis_index(a) for a in ("shard", "ctx", "tensor"))
        core = shard_i % 2
        first = core == 0
        me = shard_i * nc + ctx_i
        own = core * nt + z
        i32 = jnp.int32
        core_arr = core.reshape(1).astype(i32)
        own_arr = own.reshape(1).astype(i32)
        wt, m1, m2 = (jnp.moveaxis(x, 2, 1) for x in (weights, mom_one, mom_two))

        everyone = ("shard", "ctx")

        def gather(w):
            return lax.all_gather(w, everyone, axis=1, tiled=True)

        one_mine, o_mine = prep_one(wt)
        w_one = gather(one_mine)
        silu_all = jax.nn.silu(condition).astype(bf)
        sc_rows = lax.dynamic_slice_in_dim(silu_all, me * rows, rows, 1)
        mod = mod_partial(after(sc_rows, one_mine), wt)

        fixed = nseq == 2

        def pair(x):
            other = pp(x, "shard", 1)
            even = jnp.where(first, x, other)
            return [even] if fixed else [even, jnp.where(first, other, x)]

        tables = [t[0] for t in pair(slot_table)]
        lives = [(t >= 0).astype(f32) for t in tables]
        pickers = [(t == jnp.arange(nseq, dtype=i32)).astype(f32) for t in tables]
        pad_txt = lambda x: jnp.pad(x, ((0, tpad - txt), (0, 0)))
        x_img = [x[0] for x in pair(image_rows)]
        x_txt = [pad_txt(x[0]) for x in pair(text_rows)]
        mod = mod + pp(mod, "shard", 1)
        others = [r for r in range(1, blocks) if not r & nc]
        mod = sum(
            [lax.ppermute(mod, everyone, [(i, i ^ r) for i in range(blocks)]) for r in others], mod
        )
        mod = jnp.stack([mod] + [pp(mod, "tensor", k) for k in range(1, nt)])
        mod = jnp.concatenate([dyn(mod, z ^ k) for k in range(nt)], axis=-1)
        mods = [
            (jnp.einsum("n,sjne->sje", p, mod, precision=hp) + biases[:, :6]).reshape(12, D)
            for p in pickers
        ]
        col = z * cw
        bias_half = lax.dynamic_slice_in_dim(biases, col + core * hw, hw, 2)
        bias_cols = lax.dynamic_slice_in_dim(biases, col, cw, 2)
        bq = bias_half[:, 6]
        bkv = jnp.concatenate([jnp.zeros((2, hw), f32), bias_half[:, 7]], axis=1)
        b_up = lax.dynamic_slice_in_dim(bias_cols, 9 + 2 * core, 2, 1).reshape(4, cw)
        b_flat = biases.reshape(28, D)

        c_img = [(x[0] * l.astype(bf)) for x, l in zip(pair(image_cot), lives)]
        c_txt = [pad_txt(x[0] * l.astype(bf)) for x, l in zip(pair(text_cot), lives)]
        w_o = gather(after(o_mine, *mods))
        w_one = after(w_one, *mods, *x_img, *c_img)

        slots = range(len(tables))
        his, hts, nis, nts, qs, kvs, kv_gots = [], [], [], [], [], [], []
        for n in slots:
            hi, ht, ni, nt_, q, kv = qkv(core_arr, x_img[n], x_txt[n], txt, mods[n], bq, bkv, w_one)
            his.append(hi)
            hts.append(ht)
            nis.append(ni)
            nts.append(nt_)
            qs.append(q)
            kvs.append(kv)
            kv_gots.append(pp(kv, "ctx", 1))
        firsts = [attn_half(qs[n], kvs[n], img, live_rows) for n in slots]
        w_mlp = gather(after(wt[:, 10:18].astype(bf).reshape(16, rows, cw), kv_gots[-1], firsts[-1][0]))

        def fold(send, keep):
            return (keep.astype(f32) + pp(send, "shard", 1).astype(f32)).astype(bf)

        def own_call(kernel, name, n, tokens, wholes, outs, deps=()):
            return row_call(functools.partial(kernel, ci), name, own_arr, ci, ct, D, tokens, wholes, outs, deps)

        chunk = ci + ct
        copies = shape((nt, chunk, D))
        attns, lses, o_parts = [], [], []
        for n in slots:
            a, lse = attn_half(qs[n], kv_gots[n], img, live_rows, firsts[n])
            attns.append(a)
            lses.append(lse)
            o_parts.append(swap(fold(*oproj(core_arr, a, w_o, nt, img)), "tensor"))

        mlp_all, one_all = zeros(after(core_arr, lses[-1]), (16, 8), D, cw)
        mlp_all = mlp_all.reshape(2, 2, 2, 2, D, cw)
        one_all = one_all.reshape(2, 4, D, cw)
        dyis, dyts, gs, dus, up_sums, dh_parts, h2is, h2ts, o_sums = [], [], [], [], [], [], [], [], []
        for n in slots:
            h2, o_sum = own_call(
                after_attn_kernel,
                "after_attn",
                n,
                [(x_img[n], x_txt[n])],
                [mods[n], b_flat, after(o_parts[n], mlp_all)],
                [copies, shape((chunk, D), f32)],
            )
            o_sums.append(o_sum)
            dyi, dyt, *dg = grad_gate(core_arr, after(c_img[n], o_sum), c_txt[n], mods[n], w_mlp)
            mine = after(swap(h2, "tensor"), dyi)
            h2i, h2t, gi, gt, dui, dut, send, keep, up_sum = mlp(
                core_arr, mine, pp(mine, "shard", 1), *dg, w_mlp, b_up
            )
            dyis.append(dyi)
            dyts.append(dyt)
            h2is.append(h2i)
            h2ts.append(h2t)
            gs.append((gi, gt))
            dus.append((dui, dut))
            up_sums.append(up_sum)
            tie = fold(send, keep)
            dh_parts.append(swap(tie, "tensor"))

        def outer_sum(pairs):
            t = None
            for a, b in pairs:
                g = dotf(a, b, TN)
                t = g if t is None else t + g
            return t.astype(bf)

        def scatter(grads):
            return lax.psum_scatter(grads, everyone, scatter_dimension=1, tiled=True)

        def put(into, g, *at):
            return lax.dynamic_update_slice(into, g.reshape((1,) * len(at) + g.shape), at + (0, 0))

        for s, (h2, dy) in enumerate(((h2is, dyis), (h2ts, dyts))):
            for j in range(2):
                up = outer_sum([(h2[n], dus[n][s][j]) for n in slots])
                mlp_all = put(mlp_all, up, s, 0, core, j)
                dn = outer_sum([(dy[n], gs[n][s][j]) for n in slots])
                if (s, j) != (1, 1):
                    mlp_all = put(mlp_all, dn, s, 1, core, j)
        do_owns, dxs, mid_sums = [], [], []
        for n in slots:
            do_own, dx, sums = own_call(
                after_mlp_kernel,
                "after_mlp",
                n,
                [(x_img[n], x_txt[n]), (c_img[n], c_txt[n])],
                [mods[n], o_sums[n], dh_parts[n]],
                [copies, shape((chunk, D), f32), shape((16, D), f32)],
                deps=[mlp_all, dn],
            )
            dxs.append(dx)
            mid_sums.append(sums)
            do_owns.append(do_own)
        probe = mid_sums[-1][0, 0]
        mlp_all = put(mlp_all, dn, 1, 1, core + (probe != probe).astype(core.dtype), 1)
        mlp_sum = scatter(mlp_all.reshape(16, D, cw))
        tie = do_owns[-1]
        y_halves = [fold(*down(core_arr, *(after(g, tie) for g in gs[n]), w_mlp, nt)) for n in slots]
        dois, dots, dqs, dkv_own, dkv_gots, out_owns, low_sums = [], [], [], [], [], [], []
        for n in slots:
            mine = after(swap(do_owns[n], "tensor"), y_halves[n])
            y_part = swap(after(y_halves[n], mine), "tensor")
            doi, dot, da = grad_attn(core_arr, mine, pp(mine, "shard", 1), w_o, img, tpad)
            dois.append(doi)
            dots.append(dot)
            dq_b, dkv_b = attn_bwd_half(qs[n], kv_gots[n], attns[n], da, lses[n], da)
            dq_a, dkv_a = attn_bwd_half(qs[n], kvs[n], attns[n], da, lses[n], dkv_b)
            dq = (dq_a + dq_b).astype(bf)
            dqs.append(dq)
            dkv_own.append(dkv_a)
            dkv_gots.append(pp(dkv_b, "ctx", 1))
            out_own, sums = own_call(
                after_down_kernel,
                "after_down",
                n,
                [(x_img[n], x_txt[n]), (c_img[n], c_txt[n])],
                [mods[n], b_flat, lives[n].reshape(1, 1), o_sums[n], after(y_part, dq)],
                [copies, shape((16, D), f32)],
            )
            low_sums.append(sums)
            out_owns.append(swap(out_own, "tensor"))
        tie = dqs[-1]
        o_grads = [
            outer_sum([(after(dois[n], tie), attns[n][:img]) for n in slots]),
            outer_sum([(after(dots[n], tie), attns[n][img:]) for n in slots]),
        ]
        cat = lambda a, b: jnp.concatenate([a, b], axis=1)
        one_all = put(one_all, cat(*o_grads), core, 3)
        clip = lambda sq: jnp.minimum(1.0, clip_unit * D / jnp.sqrt(sq + clip_eps))

        def pad_row(x):
            x = x.reshape(1, -1)
            return jnp.pad(x, ((0, 0), (0, -x.shape[1] % 128)))

        d_parts, dkv_img, dkv_txt, qv_sums, end_sums = [], [], [], [], []
        for n in slots:
            send, keep, kvi, kvt, qv, sums = grad_in(
                core_arr, [low_sums[n], one_all], dqs[n], dkv_own[n], dkv_gots[n], nis[n], nts[n], w_one, nt, txt
            )
            dkv_img.append(kvi)
            dkv_txt.append(kvt)
            qv_sums.append(qv)
            end_sums.append(sums)
            tie = fold_after(keep, pp(send, "shard", 1), out_owns[n])
            d_parts.append(swap(tie, "tensor"))
        q_grads = []
        for s, (part, left, right) in enumerate(((slice(0, img), his, dkv_img), (slice(img, T), hts, dkv_txt))):
            q_grads.append(outer_sum([(left[n], after(dqs[n], tie)[part]) for n in slots]))
            one_all = put(one_all, outer_sum([(left[n], right[n]) for n in slots]), core, 2 * s)
        one_all = put(one_all, cat(*q_grads), core, 1)
        one_rows = scatter(one_all.reshape(8, D, cw))

        mlp_sq = pad_row(jnp.sum(jnp.sum(jnp.square(mlp_sum.astype(f32)), axis=1), axis=1))
        place_arr = jnp.stack([z, core]).astype(i32)
        packed = all_sum_halved(
            sum(
                pack_sums(
                    pickers[n], place_arr, mid_sums[n], low_sums[n], end_sums[n], up_sums[n], qv_sums[n], mlp_sq if n == 0 else jnp.zeros_like(mlp_sq)
                )
                for n in slots
            )
        )
        grad_owns = []
        for n in slots:
            (g,) = row_call(
                functools.partial(after_back_kernel, ci),
                "after_back",
                own_arr,
                ci,
                ct,
                D,
                [(x_img[n], x_txt[n])],
                [mods[n], dxs[n], d_parts[n]],
                [copies],
                deps=[one_all],
            )
            grad_owns.append(swap(g, "tensor"))
        state = adam_segments(
            clip(packed[nseq * 12 + 16, :16].reshape(2, 8)), mlp_sum.reshape(2, 8, rows, cw), 10, wt, m1, m2
        )
        e = nseq * 12
        dmod = packed[:e].reshape(nseq, 2, 6, D)
        od = packed[e : e + 4].reshape(2, 2, D)
        up_rows = packed[e + 4 : e + 12].reshape(2, 4, D)
        qv = packed[e + 12 : e + 16].reshape(2, 2, D)
        bias_grad = jnp.concatenate(
            [jnp.sum(dmod, axis=0), qv, od[:, :1], up_rows, od[:, 1:]], axis=1
        )
        wide = silu_all.astype(f32)
        gram_a = jnp.einsum("ni,mi->nm", wide, wide, precision=hp)
        gram_b = jnp.einsum("nsje,msje->sjnm", dmod, dmod, precision=hp)
        mod_sq = jnp.maximum(jnp.sum(gram_b * gram_a, axis=(2, 3)), 0.0)
        mod_cols = lax.dynamic_slice_in_dim(dmod, col, cw, 3)
        mod_cols = jnp.transpose(mod_cols, (1, 2, 0, 3))
        sc_wide = sc_rows.astype(f32)
        cond_rows = jnp.einsum("sjne,sjie->ni", mod_cols, wt[:, :6].astype(bf).astype(f32), precision=hp)
        cond_part = lax.dynamic_update_slice_in_dim(jnp.zeros((nseq, D), f32), cond_rows, me * rows, 1)

        state = adam_mod(jnp.transpose(sc_wide), mod_cols, clip(mod_sq), wt, m1, m2, state)
        mod_state = state[0]
        t = column_squares(one_rows, mod_state)
        t = t[:4] + t[4:]
        one_sq = jnp.stack([jnp.sum(t[:, :hw], axis=1), jnp.sum(t[:, hw:], axis=1)], axis=1)
        one_sq = jnp.stack(
            [jnp.stack([one_sq[1, s], one_sq[2 * s, 0], one_sq[2 * s, 1], one_sq[3, s]]) for s in range(2)]
        )
        tail = jnp.concatenate([cond_part.reshape(-1), one_sq.reshape(-1)])
        tail = all_sum(tail)
        cond_grad = tail[: nseq * D].reshape(nseq, D) * silu_slope(condition)
        one_sq = tail[nseq * D :].reshape(2, 4)
        state = adam_one(clip(one_sq), one_rows, wt, m1, m2, state)
        weight_grad, new_w, new_one, new_two = (jnp.moveaxis(x, 1, 2) for x in state)

        bias_sq = jnp.sum(bias_grad * bias_grad, axis=2)
        bias_factor = jnp.minimum(1.0, clip_unit * D**0.5 / jnp.sqrt(bias_sq + clip_eps))
        new_b, new_b1, new_b2 = adam_update(
            biases, bias_one, bias_two, bias_grad * bias_factor[:, :, None], 0.0
        )

        def finish(mine, dep=None):
            flag = first.astype(i32).reshape(1) if fixed else jnp.ones((1,), i32)
            send = mine if dep is None else [copy_after(x, dep) for x in mine]
            done = [join_tokens(core_arr, flag, x, pp(y, "shard", 1), img, tpad) for x, y in zip(mine, send)]
            return done[0] if fixed else [jnp.where(first, a, b) for a, b in zip(*done)]

        out_img, out_txt = finish(out_owns)
        grad_img, grad_txt = finish(grad_owns, mod_state)
        return (
            out_img[None],
            out_txt[None, :txt],
            grad_img[None],
            grad_txt[None, :txt],
            cond_grad,
            weight_grad,
            new_w,
            new_one,
            new_two,
            bias_grad,
            new_b,
            new_b1,
            new_b2,
        )

    return shards


def solution(mesh):
    sizes = dict(mesh.shape)
    rows = P("shard", "ctx", None)
    mat = P(None, ("shard", "ctx"), None, "tensor")
    return jax.shard_map(
        make_shards(sizes),
        mesh=mesh,
        in_specs=(rows, rows, P(), P("shard"), mat, mat, mat, P(), P(), P(), rows, rows),
        out_specs=(rows, rows, rows, rows, P(), mat, mat, mat, mat, P(), P(), P(), P()),
        check_vma=False,
    )
```
